32 devices in a mesh: dp: 16 (over z, y, core), tensor: 2 (over x).
Axes of the slice: x: 2, y: 2, z: 4, core: 2. Of those that a mesh axis runs over, the one named last changes fastest.
Arguments:
- block_in: bfloat16 [65536, 512], P(('dp', 'tensor')), may hold values from -6 to 6
- out_cotangent: bfloat16 [65536, 512], P(('dp', 'tensor')), may hold values from -6 to 6
- seq_lengths: int32 [16, 8], P('dp'), may hold values from 0 to 2048, as said below
- premix_gain: bfloat16 [512], replicated, may hold values from 0.5 to 1.5
- forget_weight: bfloat16 [512, 1024], P(None, 'tensor'), may hold values from -0.25 to 0.25
- admit_weight: bfloat16 [512, 1024], P(None, 'tensor'), may hold values from -0.25 to 0.25
- value_weight: bfloat16 [512, 1024], P(None, 'tensor'), may hold values from -0.25 to 0.25
- admit_bias: bfloat16 [1024], P('tensor'), may hold values from -6 to 1
- output_weight: bfloat16 [1024, 512], P('tensor'), may hold values from -0.5 to 0.5
- dense_gain: bfloat16 [512], replicated, may hold values from 0.5 to 1.5
- upper_weight: bfloat16 [512, 2048], P(None, ('dp', 'tensor')), may hold values from -0.25 to 0.25
- lower_weight: bfloat16 [2048, 512], P(('dp', 'tensor')), may hold values from -0.125 to 0.125
Outputs:
- block_out: bfloat16 [65536, 512], P(('dp', 'tensor'))
- input_slope: float32 [65536, 512], P(('dp', 'tensor'))
- premix_slope: float32 [512], P(('dp', 'tensor'))
- forget_slope: float32 [512, 1024], P(None, 'tensor')
- admit_slope: float32 [512, 1024], P(None, 'tensor')
- value_slope: float32 [512, 1024], P(None, 'tensor')
- bias_slope: float32 [1024], P('tensor')
- output_slope: float32 [1024, 512], P('tensor')
- dense_slope: float32 [512], P(('dp', 'tensor'))
- upper_slope: float32 [512, 2048], P(None, ('dp', 'tensor'))
- lower_slope: float32 [2048, 512], P(('dp', 'tensor'))
The draws below stay inside these ranges and needn't reach their ends.
Inputs may be any that keep to these rules, and one draw needn't show every extreme that they name: `seq_lengths`: row g lists the sequences of group g in order: either 4096 // 2048 entries 2048 followed by zeros, or 8 entries 512; exactly 8 rows are of the first kind, which ones drawn from the seed.
All inputs are finite; a program needn't handle non-finite values.
Results may differ from the reference program's by a relative error of at most 0.02.
Values may be sent and summed in bfloat16 or wider, within the bound.
No kernel may reach another device: no remote copies, remote signals or barrier semaphores. Data moves between devices by JAX's collectives and lax.ppermute only.
A program may use at most 320 MiB of HBM per device.

```python
import jax
import jax.numpy as jnp
from jax import lax

D = 512
H = 1024
F = 2048
LONG_LEN = 2048
SHORT_LEN = 512
BLOCK = 32
GROUP_TOKENS = 4096
SLOTS = 8
TOKENS = 65536
N_DP = 16


def draw_seq_lengths(key, part):
    key = jax.random.fold_in(key, 7)
    order = jax.random.permutation(key, N_DP)
    positions = jnp.arange(SLOTS, dtype=jnp.int32)
    long_row = jnp.where(positions < GROUP_TOKENS // LONG_LEN, LONG_LEN, 0)
    short_row = jnp.full((SLOTS,), SHORT_LEN, jnp.int32)
    chosen = jnp.where((order < N_DP // 2)[:, None], long_row[None, :], short_row[None, :])
    return chosen.astype(jnp.int32)


def block_scale(own_key, shape, cuts, low, top_value):
    def one(position, shards_of):
        steps = jax.random.uniform(jax.random.fold_in(jax.random.fold_in(own_key, 6), position), (shards_of,), jnp.float32, low / len(cuts), top_value / len(cuts))
        return jnp.repeat(jnp.exp(steps), shape[position] // shards_of).reshape((-1,) + (1,) * (len(shape) - position - 1))

    gain = one(*cuts[0])
    for cut in cuts[1:]:
        gain = gain * one(*cut)
    return gain


def bell_draw(rng, shape, scale, bound, shards=(), kind=jnp.bfloat16):
    entries = jax.random.normal(rng, shape, jnp.float32) * scale
    if len(shards) > 0:
        entries = block_scale(rng, shape, shards, -0.22, 0.18) * entries
    return jnp.clip(entries, min=-bound, max=bound).astype(kind)


def setup_inputs(seed: int = 0) -> dict:
    seeds = jax.random.split(jax.random.key(seed), 13)
    return {
        "block_in": bell_draw(seeds[0], (TOKENS, D), 1.0, 6.0, ((0, 32),)),
        "out_cotangent": bell_draw(seeds[1], (TOKENS, D), 1.0, 6.0, ((0, 32),)),
        "seq_lengths": draw_seq_lengths(jax.random.fold_in(seeds[12], 71), 0),
        "premix_gain": jnp.clip(1.0 + 0.1 * jax.random.normal(seeds[3], (D,), jnp.float32), 0.5, 1.5).astype(jnp.bfloat16),
        "forget_weight": bell_draw(seeds[4], (D, H), D ** -0.5, 0.25, ((1, 2),)),
        "admit_weight": bell_draw(seeds[5], (D, H), D ** -0.5, 0.25, ((1, 2),)),
        "value_weight": bell_draw(seeds[6], (D, H), D ** -0.5, 0.25, ((1, 2),)),
        "admit_bias": jnp.clip(-6.0 + 7.0 * jax.random.uniform(seeds[7], (H,), jnp.float32) ** block_scale(seeds[7], (H,), ((0, 2),), -0.2, 0.2), -6.0, 1.0).astype(jnp.bfloat16),
        "output_weight": bell_draw(seeds[8], (H, D), (H // 8) ** -0.5, 0.5, ((0, 2),)),
        "dense_gain": jnp.clip(1.0 + 0.1 * jax.random.normal(seeds[9], (D,), jnp.float32), 0.5, 1.5).astype(jnp.bfloat16),
        "upper_weight": bell_draw(seeds[10], (D, F), D ** -0.5, 0.25, ((1, 32),)),
        "lower_weight": bell_draw(seeds[11], (F, D), F ** -0.5, 0.125, ((0, 32),)),
    }


@jax.custom_vjp
def low(v):
    return lax.optimization_barrier(v.astype(jnp.bfloat16)).astype(jnp.float32)

@jax.custom_vjp
def low_back(v):
    return v

def low_keep(v):
    return (low(v), None)

def low_pass(kept, grad):
    return (grad,)

def back_keep(v):
    return (v, None)

def back_low(kept, grad):
    return (low(grad),)
low.defvjp(low_keep, low_pass)
low_back.defvjp(back_keep, back_low)
EPSILON = 1e-06

def gate_terms(forget_logit, admit_logit, value_logit):
    log_forget = -jax.nn.softplus(-forget_logit)
    log_admit = -jax.nn.softplus(-admit_logit)
    margin = log_forget - log_admit
    return (-jax.nn.softplus(-margin), jnp.exp(-jax.nn.softplus(margin)) * value_logit)

def block_local(pair):
    keep_log, inflow = pair
    summed = jnp.cumsum(keep_log, axis=2)
    width = keep_log.shape[2]
    lower = jnp.arange(width)[:, None] >= jnp.arange(width)[None, :]
    spread = summed[:, :, :, None, :] - summed[:, :, None, :, :]
    weights = jnp.exp(jnp.where(lower[None, None, :, :, None], spread, -jnp.inf))
    return (summed, lax.optimization_barrier(jnp.sum(weights * inflow[:, :, None, :, :], axis=3)))

def pair_combine(earlier, later):
    return (earlier[0] * later[0], later[0] * earlier[1] + later[1])

def local_pass(keep_log, inflow, resets, width):
    total, channels = keep_log.shape
    blocks = total // width
    per_turn = min(16, blocks)

    def shaped(values):
        return values.reshape(blocks // per_turn, 1, per_turn, width, channels)
    summed, local = lax.map(jax.checkpoint(block_local), (shaped(keep_log), shaped(inflow)))
    summed = summed.reshape(blocks, width, channels)
    local = local.reshape(blocks, width, channels)
    keep_mask = (1.0 - resets)[:, None]
    gains, ends = lax.associative_scan(pair_combine, (jnp.exp(summed[:, -1]) * keep_mask, local[:, -1]))
    return (summed, local, gains, ends)

def finish_states(summed, local, gains, ends, resets, incoming):
    blocks, width, channels = local.shape
    keep_mask = (1.0 - resets)[:, None]
    reached = ends[:-1] + gains[:-1] * incoming[None, :]
    previous = jnp.concatenate([incoming[None, :], reached], 0) * keep_mask
    states = local + jnp.exp(summed) * previous[:, None, :]
    return states.reshape(blocks * width, channels)

def block_resets(seq_lengths, offset, total, width):
    ends = jnp.cumsum(seq_lengths, axis=-1, dtype=jnp.int32)
    begins = ends - seq_lengths
    positions = offset + jnp.arange(total // width, dtype=jnp.int32) * width
    hits = (positions[:, None] == begins[..., None, :]) & (seq_lengths[..., None, :] > 0)
    return jnp.any(hits, -1).astype(jnp.float32)

def group_forward(params, rows, resets):
    premix_gain, forget_weight, admit_weight, value_weight, admit_bias, output_weight, dense_gain, upper_weight, lower_weight = params
    highest = lax.Precision.HIGHEST
    premix_scale = lax.rsqrt(lax.optimization_barrier(jnp.mean(rows * rows, -1, keepdims=True)) + EPSILON)
    normed = low(rows * premix_scale * premix_gain)
    forget_logit = low_back(jnp.dot(normed, forget_weight, precision=highest))
    admit_logit = low_back(jnp.dot(normed, admit_weight, precision=highest) + admit_bias)
    value_logit = low_back(jnp.dot(normed, value_weight, precision=highest))
    keep_log, inflow = gate_terms(forget_logit, admit_logit, value_logit)
    pieces = local_pass(keep_log, inflow, resets, BLOCK)
    zeros_row = jnp.zeros((keep_log.shape[1],), jnp.float32)
    states = low(finish_states(pieces[0], pieces[1], pieces[2], pieces[3], resets, zeros_row))
    mixed = low_back(jnp.dot(states, output_weight, precision=highest))
    middle = rows + mixed
    dense_scale = lax.rsqrt(lax.optimization_barrier(jnp.mean(middle * middle, -1, keepdims=True)) + EPSILON)
    dense_in = low(middle * dense_scale * dense_gain)
    upper = low_back(jnp.dot(dense_in, upper_weight, precision=highest))
    active = low(jax.nn.gelu(upper, approximate=True))
    return middle + jnp.dot(active, lower_weight, precision=highest)

def reference(block_in, out_cotangent, seq_lengths, premix_gain, forget_weight, admit_weight, value_weight, admit_bias, output_weight, dense_gain, upper_weight, lower_weight):
    params = (premix_gain.astype(jnp.float32), forget_weight.astype(jnp.float32), admit_weight.astype(jnp.float32), value_weight.astype(jnp.float32), admit_bias.astype(jnp.float32), output_weight.astype(jnp.float32), dense_gain.astype(jnp.float32), upper_weight.astype(jnp.float32), lower_weight.astype(jnp.float32))
    groups = seq_lengths.shape[0]
    rows_all = block_in.astype(jnp.float32).reshape(groups, GROUP_TOKENS, D)
    cotangents = out_cotangent.astype(jnp.float32).reshape(groups, GROUP_TOKENS, D)
    resets = block_resets(seq_lengths, 0, GROUP_TOKENS, BLOCK)

    def one_group(carried, item):
        rows, cotangent, reset = item

        def forward(weights, inputs):
            return group_forward(weights, inputs, reset)
        result, pull = jax.vjp(forward, params, rows)
        weight_slopes, row_slope = pull(cotangent)
        carried = jax.tree.map(jnp.add, carried, weight_slopes)
        return (carried, (result.astype(jnp.bfloat16), row_slope))
    start_sums = jax.tree.map(jnp.zeros_like, params)
    totals, (outputs, slopes) = lax.scan(one_group, start_sums, (rows_all, cotangents, resets))
    premix_slope, forget_slope, admit_slope, value_slope, bias_slope, output_slope, dense_slope, upper_slope, lower_slope = totals
    return (outputs.reshape(TOKENS, D), slopes.reshape(TOKENS, D), premix_slope, forget_slope, admit_slope, value_slope, bias_slope, output_slope, dense_slope, upper_slope, lower_slope)
```

```python
import functools

import jax
import jax.numpy as jnp
from jax import lax
from jax.experimental import pallas as pl
from jax.experimental.pallas import tpu as pltpu
from jax.sharding import PartitionSpec as P

EPSILON = 1e-06
LONGEST = 2048
SEGMENTS = 8
PLACES = 16
STEPS = 32
BLOCK = SEGMENTS * STEPS
GELU_SLOPE = 0.7978845608028654
GELU_CUBE = 0.044715
VMEM_BYTES = 56 * 1024 * 1024
F32 = jnp.float32
BF16 = jnp.bfloat16


def dot_nn(left, right):
    return lax.dot_general(left, right, (((1,), (0,)), ((), ())), preferred_element_type=F32)


def dot_nt(left, right):
    return lax.dot_general(left, right, (((1,), (1,)), ((), ())), preferred_element_type=F32)


def row_scale(rows):
    return lax.rsqrt(jnp.mean(rows * rows, -1, keepdims=True) + EPSILON)


def fold_rows(values):
    return jnp.sum(values.reshape(-1, 8, values.shape[-1]), 0)


def put_blocks(values, out, me, first):
    tall = values.shape[0] // PLACES
    for block in range(PLACES):
        there = pl.multiple_of((block ^ me) * tall, tall)
        out[pl.ds(there, tall), first : first + values.shape[1]] = values[block * tall : (block + 1) * tall].astype(out.dtype)


def interleave(block, scratch):
    lanes = scratch.shape[0]
    for lane in range(lanes):
        for run in range(SEGMENTS):
            part = block[run, :, lane * 128 : (lane + 1) * 128]
            scratch[lane, pl.ds(run, block.shape[1], stride=SEGMENTS), :] = part.astype(F32)
    return jnp.concatenate([scratch[lane] for lane in range(lanes)], -1)


def separate(values, scratch, out):
    lanes = scratch.shape[0]
    for lane in range(lanes):
        scratch[lane] = values[:, lane * 128 : (lane + 1) * 128]
    for run in range(SEGMENTS):
        parts = [scratch[lane, pl.ds(run, out.shape[1], stride=SEGMENTS), :] for lane in range(lanes)]
        out[run] = jnp.concatenate(parts, -1).astype(out.dtype)


def gates(forget_logit, admit_logit):
    top = jnp.maximum(jnp.maximum(-admit_logit, -forget_logit), 0.0)
    one = jnp.exp(-top)
    admit_exp = jnp.exp(-admit_logit - top)
    forget_exp = jnp.exp(-forget_logit - top)
    keep_part = one + admit_exp
    admit_part = one + forget_exp
    total = keep_part + admit_part
    inverse = pl.reciprocal(total, approx=True)
    inverse = inverse * (2.0 - total * inverse)
    keep = keep_part * inverse
    admit = admit_part * inverse
    return keep, admit, keep * (forget_exp * inverse), -admit * (admit_exp * inverse)


def product_of_runs(values):
    result = values[0:1]
    for run in range(1, SEGMENTS):
        result = result * values[run : run + 1]
    return result


def chain_runs(ends, gains, mask, carry, out):
    entering = mask[0:1] * carry
    out[0:1] = entering
    for run in range(1, SEGMENTS):
        entering = mask[run : run + 1] * (ends[run - 1 : run] + gains[run - 1 : run] * entering)
        out[run : run + 1] = entering


def mixer_kernel(first, *refs):
    if first:
        x_ref, gain_ref, *refs = refs
    else:
        normed_in, *refs = refs
    wf, wa, wv, bias, mask, carry, *refs = refs
    if first:
        x_out, normed_out, *refs = refs
    keep_out, admit_out, state_out, forget_fac, admit_fac, ends_out, *refs = refs
    logits, hs, ps, vs, fs, as_, enter, *refs = refs
    phase, block = pl.program_id(0), pl.program_id(1)
    channels = wf.shape[1]
    start = pl.multiple_of(block * BLOCK, BLOCK)

    @pl.when((phase == 0) & (block == 0))
    def _():
        hs[0:8, :] = jnp.zeros((8, channels), F32)
        ps[0:8, :] = jnp.ones((8, channels), F32)

    @pl.when(phase == 0)
    def _():
        if first:
            rows = interleave(x_ref[...], refs[0])
            x_out[...] = rows.astype(BF16)
            normed = (rows * row_scale(rows) * gain_ref[...]).astype(BF16)
            normed_out[...] = normed
        else:
            normed = normed_in[...]
        logits[:, :channels] = dot_nn(normed, wf[...])
        logits[:, channels : 2 * channels] = dot_nn(normed, wa[...])
        logits[:, 2 * channels :] = dot_nn(normed, wv[...])

        def some_rows(group, _):
            here = pl.multiple_of(group * 64, 64)
            there = pl.multiple_of(start + here, 64)
            for lane in range(0, channels, 128):
                cols = pl.ds(lane, 128)
                forget_logit = logits[pl.ds(here, 64), pl.ds(lane, 128)]
                admit_logit = logits[pl.ds(here, 64), pl.ds(channels + lane, 128)] + bias[:, lane : lane + 128]
                value = logits[pl.ds(here, 64), pl.ds(2 * channels + lane, 128)]
                keep, admit, forget_side, admit_side = gates(forget_logit, admit_logit)
                keep_out[pl.ds(here, 64), cols] = keep
                admit_out[pl.ds(here, 64), cols] = admit.astype(BF16)
                vs[pl.ds(there, 64), cols] = value
                fs[pl.ds(there, 64), cols] = forget_side
                as_[pl.ds(there, 64), cols] = admit_side
                inflow = admit * value
                state = hs[pl.ds(there, 8), cols]
                gain = ps[pl.ds(there, 8), cols]
                for step in range(8):
                    rows8 = slice(step * 8, step * 8 + 8)
                    state = keep[rows8] * state + inflow[rows8]
                    gain = gain * keep[rows8]
                    hs[pl.ds(there + 8 + step * 8, 8), cols] = state
                    ps[pl.ds(there + 8 + step * 8, 8), cols] = gain
            return 0

        lax.fori_loop(0, BLOCK // 64, some_rows, 0)

    @pl.when((phase == 1) & (block == 0))
    def _():
        total = hs.shape[0]
        ends, gains = hs[total - 8 : total, :], ps[total - 8 : total, :]
        chain_runs(ends, gains, mask, carry[...], enter)
        ends_out[0:1, :] = ends[7:8] + gains[7:8] * enter[7:8, :]
        ends_out[1:2, :] = product_of_runs(gains * mask[...])
        ends_out[2:8, :] = jnp.zeros((6, channels), F32)

    @pl.when(phase == 1)
    def _():
        def some_rows(group, _):
            here = pl.multiple_of(group * 64, 64)
            there = pl.multiple_of(start + here, 64)
            for lane in range(0, channels, 128):
                cols = pl.ds(lane, 128)
                entering = enter[:, lane : lane + 128]
                states = hs[pl.ds(there, 72), cols].reshape(9, 8, 128) + ps[pl.ds(there, 72), cols].reshape(9, 8, 128) * entering
                states = states.reshape(72, 128)
                state_out[pl.ds(here, 64), cols] = states[8:].astype(BF16)
                change = states[:64] - vs[pl.ds(there, 64), cols]
                forget_fac[pl.ds(here, 64), cols] = (change * fs[pl.ds(there, 64), cols]).astype(BF16)
                admit_fac[pl.ds(here, 64), cols] = (change * as_[pl.ds(there, 64), cols]).astype(BF16)
            return 0

        lax.fori_loop(0, BLOCK // 64, some_rows, 0)


def mixer_forward(first, rows_in, gain, weights, bias, mask, carry):
    width = rows_in.shape[-1]
    rows = rows_in.size // width
    channels = weights[0].shape[1]
    blocks = rows // BLOCK
    early = lambda phase, block: (jnp.where(phase == 0, block, blocks - 1), 0)
    late = lambda phase, block: (jnp.where(phase == 0, 0, block), 0)
    whole = lambda phase, block: (0, 0)
    if first:
        in_specs = [
            pl.BlockSpec((SEGMENTS, STEPS, width), lambda phase, block: (0, jnp.where(phase == 0, block, blocks - 1), 0)),
            pl.BlockSpec((1, width), whole),
        ]
        operands = [rows_in.reshape(SEGMENTS, rows // SEGMENTS, width), gain]
        out_specs = [pl.BlockSpec((BLOCK, width), early)] * 2
        out_shape = [jax.ShapeDtypeStruct((rows, width), BF16)] * 2
    else:
        in_specs, operands = [pl.BlockSpec((BLOCK, width), early)], [rows_in]
        out_specs, out_shape = [], []
    in_specs += [pl.BlockSpec((width, channels), whole)] * 3
    in_specs += [pl.BlockSpec((1, channels), whole), pl.BlockSpec((8, channels), whole), pl.BlockSpec((1, channels), whole)]
    out_specs += [pl.BlockSpec((BLOCK, channels), early)] * 2 + [pl.BlockSpec((BLOCK, channels), late)] * 3
    out_specs += [pl.BlockSpec((8, channels), whole)]
    out_shape += [jax.ShapeDtypeStruct((rows, channels), d) for d in (F32, BF16, BF16, BF16, BF16)]
    out_shape += [jax.ShapeDtypeStruct((8, channels), F32)]
    scratch = [pltpu.VMEM((BLOCK, 3 * channels), F32)]
    scratch += [pltpu.VMEM((rows + 8, channels), F32)] * 2
    scratch += [pltpu.VMEM((rows, channels), F32)] * 3
    scratch += [pltpu.VMEM((8, channels), F32)]
    if first:
        scratch += [pltpu.VMEM((width // 128, BLOCK, 128), F32)]
    return pl.pallas_call(
        functools.partial(mixer_kernel, first),
        grid=(2, blocks),
        in_specs=in_specs,
        out_specs=out_specs,
        out_shape=out_shape,
        scratch_shapes=scratch,
        compiler_params=pltpu.CompilerParams(vmem_limit_bytes=VMEM_BYTES, dimension_semantics=("arbitrary", "arbitrary")),
        cost_estimate=pl.CostEstimate(flops=2 * rows * width * 3 * channels, bytes_accessed=rows * channels * 16, transcendentals=4 * rows * channels),
        name="mixer_forward",
    )(*operands, *weights, bias, mask, carry)


def dense_kernel(sets, hidden_chunk, *refs):
    x_ref, c_ref, *refs = refs
    states, refs = refs[:sets], refs[sets:]
    outs_w, refs = refs[:sets], refs[sets:]
    gain_ref, w_ref, me_ref, *refs = refs
    out_ref, mixed_ref, grads_ref, slope_ref, *refs = refs
    outputs_ref, refs = refs[:sets], refs[sets:]
    upper_acc, lower_acc, output_acc, cotangent_s, out_s = refs
    step = pl.program_id(0)
    rows, width = x_ref.shape
    shards, both, _ = w_ref.shape
    half = both // 2
    per = hidden_chunk // half

    @pl.when(step == 0)
    def _():
        upper_acc[...] = jnp.zeros_like(upper_acc)
        lower_acc[...] = jnp.zeros_like(lower_acc)
        output_acc[...] = jnp.zeros_like(output_acc)
        slope_ref[...] = jnp.zeros_like(slope_ref)

    middle = x_ref[...].astype(F32)
    for state, weight in zip(states, outs_w):
        middle = middle + dot_nn(state[...], weight[...])
    scale = row_scale(middle)
    gain = gain_ref[...]
    dense_in = (middle * scale * gain).astype(BF16)
    dense_t = dense_in.T
    cotangent = interleave(c_ref[...], cotangent_s).astype(BF16)
    cotangent_t = cotangent.T
    fed, delta = None, None
    for chunk in range(shards // per):
        here = slice(chunk * per, chunk * per + per)
        cols = slice(chunk * hidden_chunk, (chunk + 1) * hidden_chunk)
        upper_w = w_ref[here, :half, :].reshape(hidden_chunk, width)
        lower_w = w_ref[here, half:, :].reshape(hidden_chunk, width)
        upper = dot_nt(dense_in, upper_w)
        square = upper * upper
        bell = 0.5 + 0.5 * jnp.tanh(upper * (GELU_SLOPE + GELU_SLOPE * GELU_CUBE * square))
        active = upper * bell
        slope = bell + active * (1.0 - bell) * (2.0 * GELU_SLOPE + 6.0 * GELU_SLOPE * GELU_CUBE * square)
        active = active.astype(BF16)
        part = dot_nn(active, lower_w)
        fed = part if fed is None else fed + part
        upper_delta = (slope * dot_nt(cotangent, lower_w)).astype(BF16)
        part = dot_nn(upper_delta, upper_w)
        delta = part if delta is None else delta + part
        lower_acc[:, cols] += dot_nn(cotangent_t, active)
        upper_acc[:, cols] += dot_nn(dense_t, upper_delta)
    separate(middle + fed, out_s, out_ref)
    slope_ref[...] += fold_rows(delta * middle * scale)
    scaled = delta * gain
    inner = jnp.mean(scaled * middle, -1, keepdims=True)
    mixed = (cotangent.astype(F32) + scale * (scaled - middle * (scale * scale * inner))).astype(BF16)
    mixed_ref[...] = mixed
    mixed_t = mixed.T
    channels = states[0].shape[1]
    for index, state in enumerate(states):
        output_acc[:, index * channels : (index + 1) * channels] += dot_nn(mixed_t, state[...])

    @pl.when(step == pl.num_programs(0) - 1)
    def _():
        for shard in range(0, shards, 2):
            cols = slice(shard * half, (shard + 2) * half)
            grads_ref[shard : shard + 2, :half, :] = upper_acc[:, cols].T.astype(BF16).reshape(2, half, width)
            grads_ref[shard : shard + 2, half:, :] = lower_acc[:, cols].T.astype(BF16).reshape(2, half, width)
        for index, output in enumerate(outputs_ref):
            put_blocks(output_acc[:, index * channels : (index + 1) * channels], output, me_ref[0], 0)


def dense_both(x_rows, cotangent, states, output_weights, gain, gathered, me):
    rows, width = x_rows.shape
    shards, both, _ = gathered.shape
    hidden = shards * both // 2
    channels = states[0].shape[1]
    sets = len(states)
    tall = min(rows, 512)
    by_rows = lambda block: (block, 0)
    by_runs = lambda block: (0, block, 0)
    whole = lambda block: (0, 0)
    runs_spec = pl.BlockSpec((SEGMENTS, tall // SEGMENTS, width), by_runs)
    in_specs = [pl.BlockSpec((tall, width), by_rows), runs_spec]
    in_specs += [pl.BlockSpec((tall, channels), by_rows)] * sets
    in_specs += [pl.BlockSpec((channels, width), whole)] * sets
    in_specs += [pl.BlockSpec((1, width), whole), pl.BlockSpec((shards, both, width), lambda block: (0, 0, 0))]
    in_specs += [pl.BlockSpec(memory_space=pltpu.SMEM)]
    return pl.pallas_call(
        functools.partial(dense_kernel, sets, 512),
        grid=(rows // tall,),
        in_specs=in_specs,
        out_specs=[
            runs_spec,
            pl.BlockSpec((tall, width), by_rows),
            pl.BlockSpec((shards, both, width), lambda block: (0, 0, 0)),
            pl.BlockSpec((8, width), whole),
        ]
        + [pl.BlockSpec((width, channels), whole)] * sets,
        out_shape=[
            jax.ShapeDtypeStruct((SEGMENTS, rows // SEGMENTS, width), BF16),
            jax.ShapeDtypeStruct((rows, width), BF16),
            jax.ShapeDtypeStruct((shards, both, width), BF16),
            jax.ShapeDtypeStruct((8, width), F32),
        ]
        + [jax.ShapeDtypeStruct((width, channels), BF16)] * sets,
        scratch_shapes=[
            pltpu.VMEM((width, hidden), F32),
            pltpu.VMEM((width, hidden), F32),
            pltpu.VMEM((width, sets * channels), F32),
            pltpu.VMEM((width // 128, tall, 128), F32),
            pltpu.VMEM((width // 128, tall, 128), F32),
        ],
        compiler_params=pltpu.CompilerParams(vmem_limit_bytes=VMEM_BYTES, dimension_semantics=("arbitrary",)),
        cost_estimate=pl.CostEstimate(flops=12 * rows * width * hidden, bytes_accessed=rows * width * 12, transcendentals=rows * hidden),
        name="dense_both",
    )(x_rows, cotangent.reshape(SEGMENTS, rows // SEGMENTS, width), *states, *output_weights, gain, gathered, me)


def mixer_back_kernel(mixed_ref, normed_ref, weight, keep_ref, admit_ref, forget_fac, admit_fac, mask, carry, output_grads, me_ref, *refs):
    delta_out, slopes_out, bias_out, ends_out, *refs = refs
    cs, ps, state_delta, slopes_acc, last, enter = refs
    phase, block = pl.program_id(0), pl.program_id(1)
    blocks = pl.num_programs(1)
    channels = keep_ref.shape[1]
    place = jnp.where(phase == 0, blocks - 1 - block, block)
    start = pl.multiple_of(place * BLOCK, BLOCK)

    @pl.when((phase == 0) & (block == 0))
    def _():
        last[0:8, :] = jnp.zeros((8, channels), F32)
        last[8:16, :] = jnp.ones((8, channels), F32)

    @pl.when(phase == 0)
    def _():
        state_delta[...] = dot_nt(mixed_ref[...], weight[...])

        def some_rows(turn, _):
            here = pl.multiple_of((BLOCK // 64 - 1 - turn) * 64, 64)
            there = pl.multiple_of(start + here, 64)
            for lane in range(0, channels, 128):
                cols = pl.ds(lane, 128)
                keep = keep_ref[pl.ds(here, 64), cols]
                fresh = state_delta[pl.ds(here, 64), cols]
                kept = last[0:8, cols]
                gain = last[8:16, cols]
                for step in range(7, -1, -1):
                    rows8 = slice(step * 8, step * 8 + 8)
                    carried = fresh[rows8] + kept
                    cs[pl.ds(there + step * 8, 8), cols] = carried
                    ps[pl.ds(there + step * 8, 8), cols] = gain
                    kept = keep[rows8] * carried
                    gain = gain * keep[rows8]
                last[0:8, cols] = kept
                last[8:16, cols] = gain
            return 0

        lax.fori_loop(0, BLOCK // 64, some_rows, 0)

    @pl.when((phase == 1) & (block == 0))
    def _():
        kept, gain = last[0:8, :], last[8:16, :]
        entering = carry[...]
        enter[7:8, :] = entering
        for run in range(SEGMENTS - 1, 0, -1):
            entering = mask[run : run + 1, :] * (kept[run : run + 1] + gain[run : run + 1] * entering)
            enter[run - 1 : run, :] = entering
        ends_out[0:1, :] = mask[0:1, :] * (kept[0:1] + gain[0:1] * entering)
        ends_out[1:2, :] = product_of_runs(gain * mask[...])
        ends_out[2:8, :] = jnp.zeros((6, channels), F32)
        slopes_acc[...] = jnp.zeros_like(slopes_acc)
        bias_out[...] = jnp.zeros_like(bias_out)

    @pl.when(phase == 1)
    def _():
        def some_rows(group, _):
            here = pl.multiple_of(group * 64, 64)
            there = pl.multiple_of(start + here, 64)
            for lane in range(0, channels, 128):
                cols = pl.ds(lane, 128)
                entering = enter[:, lane : lane + 128]
                carried = cs[pl.ds(there, 64), cols].reshape(8, 8, 128) + ps[pl.ds(there, 64), cols].reshape(8, 8, 128) * entering
                carried = carried.reshape(64, 128)
                admit_delta = (carried * admit_fac[pl.ds(here, 64), cols].astype(F32)).astype(BF16)
                delta_out[pl.ds(here, 64), pl.ds(lane, 128)] = (carried * forget_fac[pl.ds(here, 64), cols].astype(F32)).astype(BF16)
                delta_out[pl.ds(here, 64), pl.ds(channels + lane, 128)] = admit_delta
                delta_out[pl.ds(here, 64), pl.ds(2 * channels + lane, 128)] = (carried * admit_ref[pl.ds(here, 64), cols].astype(F32)).astype(BF16)
                bias_out[:, cols] += fold_rows(admit_delta.astype(F32))
            return 0

        lax.fori_loop(0, BLOCK // 64, some_rows, 0)
        normed_t = normed_ref[...].T
        for part in range(3):
            cols = slice(part * channels, (part + 1) * channels)
            slopes_acc[:, cols] += dot_nn(normed_t, delta_out[:, cols])

    @pl.when((phase == 1) & (block == blocks - 1))
    def _():
        for part in range(3):
            cols = slice(part * channels, (part + 1) * channels)
            put_blocks(slopes_acc[:, cols], slopes_out, me_ref[0], part * channels)
        slopes_out[:, 3 * channels :] = output_grads[...]


def mixer_backward(mixed, normed, weight, keep, admit, forget_fac, admit_fac, mask, carry, output_grads, me):
    rows, width = mixed.shape
    channels = keep.shape[1]
    blocks = rows // BLOCK
    back = lambda phase, block: (jnp.where(phase == 0, blocks - 1 - block, 0), 0)
    late = lambda phase, block: (jnp.where(phase == 0, 0, block), 0)
    whole = lambda phase, block: (0, 0)
    return pl.pallas_call(
        mixer_back_kernel,
        grid=(2, blocks),
        in_specs=[
            pl.BlockSpec((BLOCK, width), back),
            pl.BlockSpec((BLOCK, width), late),
            pl.BlockSpec((channels, width), whole),
            pl.BlockSpec((BLOCK, channels), back),
            pl.BlockSpec((BLOCK, channels), late),
            pl.BlockSpec((BLOCK, channels), late),
            pl.BlockSpec((BLOCK, channels), late),
            pl.BlockSpec((8, channels), whole),
            pl.BlockSpec((1, channels), whole),
            pl.BlockSpec((width, channels), whole),
            pl.BlockSpec(memory_space=pltpu.SMEM),
        ],
        out_specs=[
            pl.BlockSpec((BLOCK, 3 * channels), late),
            pl.BlockSpec((width, 4 * channels), whole),
            pl.BlockSpec((8, channels), whole),
            pl.BlockSpec((8, channels), whole),
        ],
        out_shape=[
            jax.ShapeDtypeStruct((rows, 3 * channels), BF16),
            jax.ShapeDtypeStruct((width, 4 * channels), BF16),
            jax.ShapeDtypeStruct((8, channels), F32),
            jax.ShapeDtypeStruct((8, channels), F32),
        ],
        scratch_shapes=[
            pltpu.VMEM((rows, channels), F32),
            pltpu.VMEM((rows, channels), F32),
            pltpu.VMEM((BLOCK, channels), F32),
            pltpu.VMEM((width, 3 * channels), F32),
            pltpu.VMEM((16, channels), F32),
            pltpu.VMEM((8, channels), F32),
        ],
        compiler_params=pltpu.CompilerParams(vmem_limit_bytes=VMEM_BYTES, dimension_semantics=("arbitrary", "arbitrary")),
        cost_estimate=pl.CostEstimate(flops=2 * rows * width * 4 * channels, bytes_accessed=rows * channels * 16, transcendentals=0),
        name="mixer_backward",
    )(mixed, normed, weight, keep, admit, forget_fac, admit_fac, mask, carry, output_grads, me)


def input_kernel(sets, *refs):
    x_ref, mixed_ref, gain_ref, *refs = refs
    deltas, refs = refs[:sets], refs[sets:]
    weights, refs = refs[: 3 * sets], refs[3 * sets :]
    out_ref, slope_ref, out_s = refs
    channels = weights[0].shape[1]

    @pl.when(pl.program_id(0) == 0)
    def _():
        slope_ref[...] = jnp.zeros_like(slope_ref)

    normed_delta = None
    for index in range(sets):
        for part in range(3):
            cols = slice(part * channels, (part + 1) * channels)
            term = dot_nt(deltas[index][:, cols], weights[3 * index + part][...])
            normed_delta = term if normed_delta is None else normed_delta + term
    rows = x_ref[...].astype(F32)
    scale = row_scale(rows)
    slope_ref[...] += fold_rows(normed_delta * rows * scale)
    scaled = normed_delta * gain_ref[...]
    inner = jnp.mean(scaled * rows, -1, keepdims=True)
    result = mixed_ref[...].astype(F32) + scale * (scaled - rows * (scale * scale * inner))
    separate(result, out_s, out_ref)


def input_backward(x_rows, mixed, gain, deltas, weights):
    rows, width = x_rows.shape
    sets = len(deltas)
    channels = weights[0].shape[1]
    by_rows = lambda block: (block, 0)
    whole = lambda block: (0, 0)
    return pl.pallas_call(
        functools.partial(input_kernel, sets),
        grid=(rows // BLOCK,),
        in_specs=[pl.BlockSpec((BLOCK, width), by_rows)] * 2
        + [pl.BlockSpec((1, width), whole)]
        + [pl.BlockSpec((BLOCK, 3 * channels), by_rows)] * sets
        + [pl.BlockSpec((width, channels), whole)] * (3 * sets),
        out_specs=[pl.BlockSpec((SEGMENTS, STEPS, width), lambda block: (0, block, 0)), pl.BlockSpec((8, width), whole)],
        out_shape=[jax.ShapeDtypeStruct((SEGMENTS, rows // SEGMENTS, width), F32), jax.ShapeDtypeStruct((8, width), F32)],
        scratch_shapes=[pltpu.VMEM((width // 128, BLOCK, 128), F32)],
        compiler_params=pltpu.CompilerParams(vmem_limit_bytes=VMEM_BYTES, dimension_semantics=("arbitrary",)),
        cost_estimate=pl.CostEstimate(flops=2 * rows * width * 3 * channels * sets, bytes_accessed=rows * channels * 6 * sets, transcendentals=0),
        name="input_backward",
    )(x_rows, mixed, gain, *deltas, *weights)


def finish_kernel(channels, sums_ref, me_ref, forget_out, admit_out, value_out, output_out, scratch):
    tall = sums_ref.shape[0] // PLACES
    for place in range(PLACES):
        there = pl.multiple_of((place ^ me_ref[0]) * tall, tall)
        here = slice(place * tall, (place + 1) * tall)
        for part, out in enumerate((forget_out, admit_out, value_out, scratch)):
            out[pl.ds(there, tall), :] = sums_ref[here, part * channels : (part + 1) * channels].astype(F32)
    output_out[...] = scratch[...].T


def finish_slopes(sums, me):
    width, channels = sums.shape[0], sums.shape[1] // 4
    return pl.pallas_call(
        functools.partial(finish_kernel, channels),
        in_specs=[pl.BlockSpec(memory_space=pltpu.VMEM), pl.BlockSpec(memory_space=pltpu.SMEM)],
        out_shape=[jax.ShapeDtypeStruct((width, channels), F32)] * 3 + [jax.ShapeDtypeStruct((channels, width), F32)],
        scratch_shapes=[pltpu.VMEM((width, channels), F32)],
        compiler_params=pltpu.CompilerParams(vmem_limit_bytes=VMEM_BYTES),
        name="finish_slopes",
    )(sums, me)


def run_masks(seq_lengths, rows, shift, channels):
    ends = jnp.cumsum(seq_lengths[0])
    begins = ends - seq_lengths[0]
    places = shift + jnp.arange(SEGMENTS, dtype=jnp.int32) * (rows // SEGMENTS)
    fresh = jnp.any((places[:, None] == begins[None, :]) & (seq_lengths[0] > 0)[None, :], -1)
    return jnp.broadcast_to(jnp.where(fresh, 0.0, 1.0).astype(F32)[:, None], (SEGMENTS, channels))


def regroup(stacked, half):
    count, both, width = stacked.shape
    if both == 2 * half:
        return stacked
    arrays = jnp.moveaxis(stacked.reshape(count, 2, both // 2, width), 1, 0).reshape(2, -1, half, width)
    return jnp.moveaxis(arrays, 0, 1).reshape(-1, 2 * half, width)


def added(mine, theirs):
    return (mine.astype(F32) + theirs.astype(F32)).astype(mine.dtype)


class Exchange:
    def __init__(self, count):
        self.count = count

    def swap(self, values, bit):
        pairs = [(device, device ^ bit) for device in range(self.count)]
        return lax.ppermute(values, ("dp", "tensor"), pairs)

    def grow(self, values, bit):
        return jnp.concatenate([values, self.swap(values, bit)], 0)

    def halve(self, values, bit):
        half = values.shape[0] // 2
        return added(values[:half], self.swap(values[half:], bit))


class Links:
    TENSOR, CORE, NEAR, Z_NEAR, Z_FAR = 1, 2, 4, 8, 16

    def __init__(self):
        self.exchange = Exchange(32)
        core = lax.axis_index("dp") % 2
        dp = lax.axis_index("dp")
        self.core = core
        self.me = (core * 8 + (dp // 2 % 2) * 4 + (dp // 4 % 2) * 2 + dp // 8).astype(jnp.int32)

    def weights(self, own_weights):
        parts = []
        for group in (own_weights[:3], own_weights[3:]):
            half = group[0].shape[0] // 2
            mine = jnp.stack([lax.dynamic_slice_in_dim(w, self.core * half, half) for w in group])
            got = self.exchange.swap(mine, self.TENSOR)
            rest = self.exchange.swap(got, self.CORE)
            first = self.core == 0
            whole = jnp.concatenate([jnp.where(first, got, rest), jnp.where(first, rest, got)], 1)
            parts += [whole[index] for index in range(len(group))]
        return own_weights, parts

    def bias(self, own_bias):
        return own_bias, self.exchange.swap(own_bias, self.TENSOR)

    def dense(self, shard):
        held = shard[None]
        for bit in (self.Z_NEAR, self.Z_FAR, self.NEAR, self.TENSOR, self.CORE):
            held = self.exchange.grow(held, bit)
        return held

    def dense_sums(self, grads):
        for bit in (self.CORE, self.TENSOR, self.NEAR, self.Z_FAR, self.Z_NEAR):
            grads = self.exchange.halve(grads, bit)
        return grads[0]

    def mixer_sums(self, own_grads, other_grads):
        sums = self.exchange.halve(own_grads, self.CORE)
        other = self.exchange.halve(other_grads, self.CORE)
        sums = added(sums, self.exchange.swap(other, self.TENSOR))
        for bit in (self.NEAR, self.Z_NEAR, self.Z_FAR):
            sums = self.exchange.halve(sums, bit)
        for bit in (self.Z_FAR, self.Z_NEAR, self.NEAR, self.CORE):
            sums = self.exchange.grow(sums, bit)
        return sums

    def small_sums(self, values):
        for bit in (self.CORE, self.TENSOR, self.NEAR, self.Z_NEAR, self.Z_FAR):
            values = values + self.exchange.swap(values, bit)
        return values


class Plain:
    def __init__(self, n_tensor, own):
        self.n_tensor, self.own = n_tensor, own
        self.me = jnp.int32(0)

    def halves(self, whole):
        middle = whole.shape[1] // 2
        return whole[:, :middle], whole[:, middle:]

    def weights(self, own_weights):
        pairs = [self.halves(lax.all_gather(w, "tensor", axis=1, tiled=True)) for w in own_weights[:3]]
        last = lax.all_gather(own_weights[3], "tensor", axis=0, tiled=True)
        pairs.append(tuple(jnp.split(last, 2, 0)))
        return [p[0] for p in pairs], [p[1] for p in pairs]

    def bias(self, own_bias):
        return tuple(jnp.split(lax.all_gather(own_bias, "tensor", axis=0, tiled=True), 2))

    def dense(self, shard):
        return regroup(lax.all_gather(shard, ("dp", "tensor"), axis=0), 64)

    def dense_sums(self, grads):
        count = lax.axis_size("dp") * self.n_tensor
        half = grads.shape[0] * grads.shape[1] // (2 * count)
        return lax.psum_scatter(regroup(grads, half), ("dp", "tensor"), scatter_dimension=0, tiled=True)[0]

    def mixer_sums(self, low_grads, high_grads):
        width = low_grads.shape[0]
        whole = jnp.concatenate([low_grads.reshape(width, 4, -1), high_grads.reshape(width, 4, -1)], 2)
        part = lax.psum_scatter(whole, "tensor", scatter_dimension=2, tiled=True)
        return lax.psum(part, "dp").reshape(width, 4 * self.own)

    def small_sums(self, values):
        return lax.psum(values, ("dp", "tensor"))


def on_device(
    block_in,
    out_cotangent,
    seq_lengths,
    premix_gain,
    forget_weight,
    admit_weight,
    value_weight,
    admit_bias,
    output_weight,
    dense_gain,
    upper_weight,
    lower_weight,
):
    n_dp, n_tensor = lax.axis_size("dp"), lax.axis_size("tensor")
    rows, width = block_in.shape
    place = lax.axis_index("tensor")
    own = forget_weight.shape[1]
    premix = premix_gain.astype(F32)[None]
    dense = dense_gain.astype(F32)[None]
    paired = (n_dp, n_tensor) == (16, 2)
    links = Links() if paired else Plain(n_tensor, own)
    me = links.me.reshape(1)

    weights = links.weights([forget_weight, admit_weight, value_weight, output_weight])
    biases = [b.astype(F32)[None] for b in links.bias(admit_bias)]
    gathered = links.dense(jnp.concatenate([upper_weight.T, lower_weight], 0))
    channels = weights[0][0].shape[1]

    mask = run_masks(seq_lengths, rows, place * rows, channels)
    crossing = rows % LONGEST != 0

    def chained(ends, backwards):
        every = lax.all_gather(ends, "tensor", axis=0)
        entering = jnp.zeros_like(ends[0:1])
        mine = entering
        order = range(n_tensor - 1, -1, -1) if backwards else range(n_tensor)
        for index in order:
            mine = jnp.where(place == index, entering, mine)
            entering = every[index, 0:1] + every[index, 1:2] * entering
        return mine

    nothing = jnp.zeros((1, channels), F32)

    def forward(first, rows_in, index):
        carry = nothing
        if crossing:
            ends = mixer_forward(first, rows_in, premix, weights[index][:3], biases[index], mask, carry)[-1]
            carry = chained(ends, False)
        return mixer_forward(first, rows_in, premix, weights[index][:3], biases[index], mask, carry)

    x_rows, normed, *kept_0 = forward(True, block_in, 0)
    kept_1 = forward(False, normed, 1)
    kept = [kept_0, kept_1]
    outputs = [w[3] for w in weights]
    block_out, mixed, dense_grads, dense_part, *output_grads = dense_both(
        x_rows, out_cotangent, [k[2] for k in kept], outputs, dense, gathered, me
    )

    def backward(index):
        keep, admit, _, forget_fac, admit_fac, _ = kept[index]
        args = (mixed, normed, outputs[index], keep, admit, forget_fac, admit_fac, mask)
        carry = nothing
        if crossing:
            carry = chained(mixer_backward(*args, carry, output_grads[index], me)[-1], True)
        return mixer_backward(*args, carry, output_grads[index], me)

    back_1 = backward(1)
    back_0 = backward(0)
    input_slope, premix_part = input_backward(x_rows, mixed, premix, [back_0[0], back_1[0]], weights[0][:3] + weights[1][:3])

    dense_sum = links.dense_sums(dense_grads).astype(F32)
    hidden = upper_weight.shape[1]
    upper_slope, lower_slope = dense_sum[:hidden].T, dense_sum[hidden:]
    sums = links.mixer_sums(back_0[1], back_1[1])
    forget_slope, admit_slope, value_slope, output_slope = finish_slopes(sums, me)
    bias_parts = [jnp.sum(b[2], 0) for b in (back_0, back_1)]
    if paired:
        bias_parts = [jnp.where(place == 0, bias_parts[0], bias_parts[1]), jnp.where(place == 0, bias_parts[1], bias_parts[0])]
    small = links.small_sums(jnp.concatenate([jnp.sum(premix_part, 0), jnp.sum(dense_part, 0)] + bias_parts, 0))
    shard = width // (n_dp * n_tensor)
    at = (lax.axis_index("dp") * n_tensor + place) * shard
    premix_slope = lax.dynamic_slice(small, (at,), (shard,))
    dense_slope = lax.dynamic_slice(small, (width + at,), (shard,))
    bias_slope = lax.dynamic_slice(small, (2 * width + place * own,), (own,))
    return (
        block_out.reshape(rows, width),
        input_slope.reshape(rows, width),
        premix_slope,
        forget_slope,
        admit_slope,
        value_slope,
        bias_slope,
        output_slope,
        dense_slope,
        upper_slope,
        lower_slope,
    )


def solution(mesh):
    placed = (
        P(("dp", "tensor"), None),
        P(("dp", "tensor"), None),
        P("dp", None),
        P(),
        P(None, "tensor"),
        P(None, "tensor"),
        P(None, "tensor"),
        P("tensor"),
        P("tensor", None),
        P(),
        P(None, ("dp", "tensor")),
        P(("dp", "tensor"), None),
    )
    return jax.shard_map(
        on_device,
        mesh=mesh,
        in_specs=placed,
        out_specs=(
            P(("dp", "tensor"), None),
            P(("dp", "tensor"), None),
            P(("dp", "tensor")),
            P(None, "tensor"),
            P(None, "tensor"),
            P(None, "tensor"),
            P("tensor"),
            P("tensor", None),
            P(("dp", "tensor")),
            P(None, ("dp", "tensor")),
            P(("dp", "tensor"), None),
        ),
        check_vma=False,
    )
```

```python
import functools

import jax
import jax.numpy as jnp
from jax import lax
from jax.experimental import pallas as pl
from jax.experimental.pallas import tpu as pltpu
from jax.sharding import PartitionSpec as P

EPSILON = 1e-06
LONGEST = 2048
SEGMENTS = 8
PLACES = 16
STEPS = 64
BLOCK = SEGMENTS * STEPS
GROUP = 32
GELU_SLOPE = 0.7978845608028654
GELU_CUBE = 0.044715
VMEM_BYTES = 56 * 1024 * 1024
F32 = jnp.float32
BF16 = jnp.bfloat16


def dot_nn(left, right):
    return lax.dot_general(left, right, (((1,), (0,)), ((), ())), preferred_element_type=F32)


def dot_nt(left, right):
    return lax.dot_general(left, right, (((1,), (1,)), ((), ())), preferred_element_type=F32)


def row_scale(rows):
    return lax.rsqrt(jnp.mean(rows * rows, -1, keepdims=True) + EPSILON)


def fold_rows(values):
    return jnp.sum(values.reshape(-1, 8, values.shape[-1]), 0)


def put_blocks(values, halves, me, first):
    tall = values.shape[0] // PLACES
    for place in range(PLACES):
        block = pl.multiple_of((place ^ me) * tall, tall)
        there = (place % (PLACES // 2)) * tall
        out = halves[place // (PLACES // 2)]
        out[there : there + tall, first : first + values.shape[1]] = values[pl.ds(block, tall), :].astype(out.dtype)


def interleave(block, scratch):
    lanes = scratch.shape[0]
    for lane in range(lanes):
        for run in range(SEGMENTS):
            part = block[run, :, lane * 128 : (lane + 1) * 128]
            scratch[lane, pl.ds(run, block.shape[1], stride=SEGMENTS), :] = part.astype(F32)
    return jnp.concatenate([scratch[lane] for lane in range(lanes)], -1)


def separate(values, scratch, out):
    lanes = scratch.shape[0]
    for lane in range(lanes):
        scratch[lane] = values[:, lane * 128 : (lane + 1) * 128]
    for run in range(SEGMENTS):
        parts = [scratch[lane, pl.ds(run, out.shape[1], stride=SEGMENTS), :] for lane in range(lanes)]
        out[run] = jnp.concatenate(parts, -1).astype(out.dtype)


def gates(forget_logit, admit_logit):
    top = jnp.maximum(jnp.maximum(-admit_logit, -forget_logit), 0.0)
    one = jnp.exp(-top)
    admit_exp = jnp.exp(-admit_logit - top)
    forget_exp = jnp.exp(-forget_logit - top)
    keep_part = one + admit_exp
    admit_part = one + forget_exp
    total = keep_part + admit_part
    inverse = pl.reciprocal(total, approx=True)
    inverse = inverse * (2.0 - total * inverse)
    keep = keep_part * inverse
    admit = admit_part * inverse
    return keep, admit, keep * (forget_exp * inverse), -admit * (admit_exp * inverse)


def product_of_runs(values):
    result = values[0:1]
    for run in range(1, SEGMENTS):
        result = result * values[run : run + 1]
    return result


def chain_runs(ends, gains, mask, carry, out):
    entering = mask[0:1] * carry
    out[0:1] = entering
    for run in range(1, SEGMENTS):
        entering = mask[run : run + 1] * (ends[run - 1 : run] + gains[run - 1 : run] * entering)
        out[run : run + 1] = entering


def mixer_kernel(first, *refs):
    if first:
        x_ref, gain_ref, *refs = refs
    else:
        normed_in, *refs = refs
    wf, wa, wv, bias, mask, carry, *refs = refs
    if first:
        x_out, normed_out, *refs = refs
    admit_out, state_out, forget_fac, admit_fac, ends_out, *refs = refs
    logits, hs, ps, vs, fs, as_, enter, *refs = refs
    phase, block = pl.program_id(0), pl.program_id(1)
    channels = wf.shape[1]
    start = pl.multiple_of(block * BLOCK, BLOCK)

    @pl.when((phase == 0) & (block == 0))
    def _():
        hs[0:8, :] = jnp.zeros((8, channels), F32)
        ps[0:8, :] = jnp.ones((8, channels), F32)

    @pl.when(phase == 0)
    def _():
        if first:
            rows = interleave(x_ref[...], refs[0])
            x_out[...] = rows.astype(BF16)
            normed = (rows * row_scale(rows) * gain_ref[...]).astype(BF16)
            normed_out[...] = normed
        else:
            normed = normed_in[...]
        wide = min(channels, 256)
        for chunk in range(channels // wide):
            cols = slice(chunk * wide, (chunk + 1) * wide)
            for part, weight in enumerate((wf, wa, wv)):
                logits[chunk, part] = dot_nn(normed, weight[:, cols])
        for chunk in range(channels // wide):
            for lane in range(0, wide, 128):
                inner, cols = slice(lane, lane + 128), slice(chunk * wide + lane, chunk * wide + lane + 128)
                state, gain = hs[pl.ds(start, 8), cols], ps[pl.ds(start, 8), cols]
                for here in range(0, BLOCK, GROUP):
                    rows = slice(here, here + GROUP)
                    there = pl.ds(start + here, GROUP)
                    value = logits[chunk, 2, rows, inner]
                    keep, admit, forget_side, admit_side = gates(
                        logits[chunk, 0, rows, inner], logits[chunk, 1, rows, inner] + bias[:, cols]
                    )
                    admit_out[rows, cols] = admit.astype(BF16)
                    vs[there, cols] = value
                    fs[there, cols] = forget_side
                    as_[there, cols] = admit_side
                    inflow = admit * value
                    for step in range(0, GROUP, 8):
                        state = keep[step : step + 8] * state + inflow[step : step + 8]
                        gain = gain * keep[step : step + 8]
                        hs[pl.ds(start + here + step + 8, 8), cols] = state
                        ps[pl.ds(start + here + step + 8, 8), cols] = gain

    @pl.when((phase == 1) & (block == 0))
    def _():
        total = hs.shape[0]
        ends, gains = hs[total - 8 : total, :], ps[total - 8 : total, :]
        chain_runs(ends, gains, mask, carry[...], enter)
        ends_out[0:1, :] = ends[7:8] + gains[7:8] * enter[7:8, :]
        ends_out[1:2, :] = product_of_runs(gains * mask[...])
        ends_out[2:8, :] = jnp.zeros((6, channels), F32)

    @pl.when(phase == 1)
    def _():
        def some_rows(group, _):
            here = pl.multiple_of(group * 64, 64)
            there = pl.multiple_of(start + here, 64)
            for lane in range(0, channels, 128):
                cols = pl.ds(lane, 128)
                entering = enter[:, lane : lane + 128]
                states = hs[pl.ds(there, 72), cols].reshape(9, 8, 128) + ps[pl.ds(there, 72), cols].reshape(9, 8, 128) * entering
                states = states.reshape(72, 128)
                state_out[pl.ds(here, 64), cols] = states[8:].astype(BF16)
                change = states[:64] - vs[pl.ds(there, 64), cols]
                forget_fac[pl.ds(here, 64), cols] = (change * fs[pl.ds(there, 64), cols]).astype(BF16)
                admit_fac[pl.ds(here, 64), cols] = (change * as_[pl.ds(there, 64), cols]).astype(BF16)
            return 0

        lax.fori_loop(0, BLOCK // 64, some_rows, 0)


def mixer_forward(first, rows_in, gain, weights, bias, mask, carry):
    width = rows_in.shape[-1]
    rows = rows_in.size // width
    channels = weights[0].shape[1]
    blocks = rows // BLOCK
    early = lambda phase, block: (jnp.where(phase == 0, block, blocks - 1), 0)
    late = lambda phase, block: (jnp.where(phase == 0, 0, block), 0)
    whole = lambda phase, block: (0, 0)
    if first:
        in_specs = [
            pl.BlockSpec((SEGMENTS, STEPS, width), lambda phase, block: (0, jnp.where(phase == 0, block, blocks - 1), 0)),
            pl.BlockSpec((1, width), whole),
        ]
        operands = [rows_in.reshape(SEGMENTS, rows // SEGMENTS, width), gain]
        out_specs = [pl.BlockSpec((BLOCK, width), early)] * 2
        out_shape = [jax.ShapeDtypeStruct((rows, width), BF16)] * 2
    else:
        in_specs, operands = [pl.BlockSpec((BLOCK, width), early)], [rows_in]
        out_specs, out_shape = [], []
    in_specs += [pl.BlockSpec((width, channels), whole)] * 3
    in_specs += [pl.BlockSpec((1, channels), whole), pl.BlockSpec((8, channels), whole), pl.BlockSpec((1, channels), whole)]
    out_specs += [pl.BlockSpec((BLOCK, channels), early)] + [pl.BlockSpec((BLOCK, channels), late)] * 3
    out_specs += [pl.BlockSpec((8, channels), whole)]
    out_shape += [jax.ShapeDtypeStruct((rows, channels), BF16)] * 4
    out_shape += [jax.ShapeDtypeStruct((8, channels), F32)]
    wide = min(channels, 256)
    scratch = [pltpu.VMEM((channels // wide, 3, BLOCK, wide), F32)]
    scratch += [pltpu.VMEM((rows + 8, channels), F32)] * 2
    scratch += [pltpu.VMEM((rows, channels), F32)] * 3
    scratch += [pltpu.VMEM((8, channels), F32)]
    if first:
        scratch += [pltpu.VMEM((width // 128, BLOCK, 128), F32)]
    return pl.pallas_call(
        functools.partial(mixer_kernel, first),
        grid=(2, blocks),
        in_specs=in_specs,
        out_specs=out_specs,
        out_shape=out_shape,
        scratch_shapes=scratch,
        compiler_params=pltpu.CompilerParams(vmem_limit_bytes=VMEM_BYTES, dimension_semantics=("arbitrary", "arbitrary")),
        cost_estimate=pl.CostEstimate(flops=2 * rows * width * 3 * channels, bytes_accessed=rows * channels * 16, transcendentals=4 * rows * channels),
        name="mixer_forward",
    )(*operands, *weights, bias, mask, carry)


def dense_kernel(sets, hidden_chunk, *refs):
    x_ref, c_ref, *refs = refs
    states, refs = refs[:sets], refs[sets:]
    outs_w, refs = refs[:sets], refs[sets:]
    gain_ref, w_ref, me_ref, *refs = refs
    out_ref, mixed_ref, upper_keep, upper_send, lower_keep, lower_send, slope_ref, *refs = refs
    outputs_ref, refs = refs[:sets], refs[sets:]
    upper_acc, lower_acc, output_acc, cotangent_s, out_s = refs
    step = pl.program_id(0)
    rows, width = x_ref.shape
    shards, both, _ = w_ref.shape
    half = both // 2
    per = hidden_chunk // half

    @pl.when(step == 0)
    def _():
        upper_acc[...] = jnp.zeros_like(upper_acc)
        lower_acc[...] = jnp.zeros_like(lower_acc)
        output_acc[...] = jnp.zeros_like(output_acc)
        slope_ref[...] = jnp.zeros_like(slope_ref)

    middle = x_ref[...].astype(F32)
    for state, weight in zip(states, outs_w):
        middle = middle + dot_nn(state[...], weight[...])
    scale = row_scale(middle)
    gain = gain_ref[...]
    dense_in = (middle * scale * gain).astype(BF16)
    dense_t = dense_in.T
    cotangent = interleave(c_ref[...], cotangent_s).astype(BF16)
    cotangent_t = cotangent.T
    fed, delta = None, None
    for chunk in range(shards // per):
        here = slice(chunk * per, chunk * per + per)
        cols = slice(chunk * hidden_chunk, (chunk + 1) * hidden_chunk)
        upper_w = w_ref[here, :half, :].reshape(hidden_chunk, width)
        lower_w = w_ref[here, half:, :].reshape(hidden_chunk, width)
        upper = dot_nt(dense_in, upper_w)
        square = upper * upper
        bell = 0.5 + 0.5 * jnp.tanh(upper * (GELU_SLOPE + GELU_SLOPE * GELU_CUBE * square))
        active = upper * bell
        slope = bell + active * (1.0 - bell) * (2.0 * GELU_SLOPE + 6.0 * GELU_SLOPE * GELU_CUBE * square)
        active = active.astype(BF16)
        part = dot_nn(active, lower_w)
        fed = part if fed is None else fed + part
        upper_delta = (slope * dot_nt(cotangent, lower_w)).astype(BF16)
        part = dot_nn(upper_delta, upper_w)
        delta = part if delta is None else delta + part
        lower_acc[:, cols] += dot_nn(cotangent_t, active)
        upper_acc[:, cols] += dot_nn(dense_t, upper_delta)
    separate(middle + fed, out_s, out_ref)
    slope_ref[...] += fold_rows(delta * middle * scale)
    scaled = delta * gain
    inner = jnp.mean(scaled * middle, -1, keepdims=True)
    mixed = (cotangent.astype(F32) + scale * (scaled - middle * (scale * scale * inner))).astype(BF16)
    mixed_ref[...] = mixed
    mixed_t = mixed.T
    channels = states[0].shape[1]
    for index, state in enumerate(states):
        output_acc[:, index * channels : (index + 1) * channels] += dot_nn(mixed_t, state[...])

    @pl.when(step == pl.num_programs(0) - 1)
    def _():
        for shard in range(0, shards, 2):
            cols = slice(shard * half, (shard + 2) * half)
            upper_ref, lower_ref = (upper_keep, lower_keep) if shard < shards // 2 else (upper_send, lower_send)
            there = shard % (shards // 2)
            upper_ref[there : there + 2] = upper_acc[:, cols].T.astype(BF16).reshape(2, half, width)
            lower_ref[there : there + 2] = lower_acc[:, cols].T.astype(BF16).reshape(2, half, width)
        for index, output in enumerate(outputs_ref):
            tall = output_acc.shape[0] // PLACES
            for place in range(PLACES):
                there = pl.multiple_of((place ^ me_ref[1]) * tall, tall)
                output[place * tall : (place + 1) * tall, :] = output_acc[pl.ds(there, tall), index * channels : (index + 1) * channels].astype(BF16)


def dense_both(x_rows, cotangent, states, output_weights, gain, gathered, me):
    rows, width = x_rows.shape
    shards, both, _ = gathered.shape
    hidden = shards * both // 2
    channels = states[0].shape[1]
    sets = len(states)
    tall = min(rows, 512)
    by_rows = lambda block: (block, 0)
    by_runs = lambda block: (0, block, 0)
    whole = lambda block: (0, 0)
    runs_spec = pl.BlockSpec((SEGMENTS, tall // SEGMENTS, width), by_runs)
    in_specs = [pl.BlockSpec((tall, width), by_rows), runs_spec]
    in_specs += [pl.BlockSpec((tall, channels), by_rows)] * sets
    in_specs += [pl.BlockSpec((channels, width), whole)] * sets
    in_specs += [pl.BlockSpec((1, width), whole), pl.BlockSpec((shards, both, width), lambda block: (0, 0, 0))]
    in_specs += [pl.BlockSpec(memory_space=pltpu.SMEM)]
    return pl.pallas_call(
        functools.partial(dense_kernel, sets, 512),
        grid=(rows // tall,),
        in_specs=in_specs,
        out_specs=[
            runs_spec,
            pl.BlockSpec((tall, width), by_rows),
        ]
        + [pl.BlockSpec((shards // 2, both // 2, width), lambda block: (0, 0, 0))] * 4
        + [pl.BlockSpec((8, width), whole)]
        + [pl.BlockSpec((width, channels), whole)] * sets,
        out_shape=[
            jax.ShapeDtypeStruct((SEGMENTS, rows // SEGMENTS, width), BF16),
            jax.ShapeDtypeStruct((rows, width), BF16),
        ]
        + [jax.ShapeDtypeStruct((shards // 2, both // 2, width), BF16)] * 4
        + [jax.ShapeDtypeStruct((8, width), F32)]
        + [jax.ShapeDtypeStruct((width, channels), BF16)] * sets,
        scratch_shapes=[
            pltpu.VMEM((width, hidden), F32),
            pltpu.VMEM((width, hidden), F32),
            pltpu.VMEM((width, sets * channels), F32),
            pltpu.VMEM((width // 128, tall, 128), F32),
            pltpu.VMEM((width // 128, tall, 128), F32),
        ],
        compiler_params=pltpu.CompilerParams(vmem_limit_bytes=VMEM_BYTES, dimension_semantics=("arbitrary",)),
        cost_estimate=pl.CostEstimate(flops=12 * rows * width * hidden, bytes_accessed=rows * width * 12, transcendentals=rows * hidden),
        name="dense_both",
    )(x_rows, cotangent.reshape(SEGMENTS, rows // SEGMENTS, width), *states, *output_weights, gain, gathered, me)


def mixer_back_kernel(sets, mixed_ref, normed_ref, mask, me_ref, *refs):
    per_set = [refs[index * 6 : index * 6 + 6] for index in range(sets)]
    refs = refs[6 * sets :]
    carried_out, refs = refs[:sets], refs[sets:]
    first_out, second_out, refs = refs[:2], refs[2:4], refs[4:]
    bias_out, ends_out, *refs = refs
    cs, ps, state_delta, admits, deltas, slopes_acc, last, enter = refs
    phase, block = pl.program_id(0), pl.program_id(1)
    blocks = pl.num_programs(1)
    channels = mask.shape[1]
    place = jnp.where(phase == 0, blocks - 1 - block, block)
    start = pl.multiple_of(place * BLOCK, BLOCK)

    @pl.when((phase == 0) & (block == 0))
    def _():
        last[:, 0:8, :] = jnp.zeros((sets, 8, channels), F32)
        last[:, 8:16, :] = jnp.ones((sets, 8, channels), F32)

    @pl.when(phase == 0)
    def _():
        for index in range(sets):
            state_delta[index] = dot_nt(mixed_ref[...], per_set[index][0][...])
        for index in range(sets):
            admit_ref = per_set[index][1]
            admits[index, pl.ds(start, BLOCK), :] = admit_ref[...]
            for lane in range(0, channels, 128):
                cols = slice(lane, lane + 128)
                kept, gain = last[index, 0:8, cols], last[index, 8:16, cols]
                for here in range(BLOCK - 16, -1, -16):
                    keep = 1.0 - admit_ref[here : here + 16, cols].astype(F32)
                    for step in (8, 0):
                        carried = state_delta[index, here + step : here + step + 8, cols] + kept
                        cs[index, pl.ds(start + here + step, 8), cols] = carried
                        ps[index, pl.ds(start + here + step, 8), cols] = gain
                        kept = keep[step : step + 8] * carried
                        gain = keep[step : step + 8] * gain
                last[index, 0:8, cols] = kept
                last[index, 8:16, cols] = gain

    @pl.when((phase == 1) & (block == 0))
    def _():
        for index in range(sets):
            kept, gain = last[index, 0:8, :], last[index, 8:16, :]
            entering = per_set[index][4][...]
            enter[index, 7:8, :] = entering
            for run in range(SEGMENTS - 1, 0, -1):
                entering = mask[run : run + 1, :] * (kept[run : run + 1] + gain[run : run + 1] * entering)
                enter[index, run - 1 : run, :] = entering
            ends_out[index, 0:1, :] = mask[0:1, :] * (kept[0:1] + gain[0:1] * entering)
            ends_out[index, 1:2, :] = product_of_runs(gain * mask[...])
            ends_out[index, 2:8, :] = jnp.zeros((6, channels), F32)
        bias_out[...] = jnp.zeros_like(bias_out)
        slopes_acc[...] = jnp.zeros_like(slopes_acc)

    @pl.when(phase == 1)
    def _():
        normed_t = normed_ref[...].T
        wide = min(channels, 256)
        for index in range(sets):
            _, _, forget_fac, admit_fac, _, output_grads = per_set[index]
            for first in range(0, channels, wide):
                for lane in range(first, first + wide, 128):
                    cols = slice(lane, lane + 128)
                    entering = enter[index, :, cols]
                    bias = jnp.zeros((8, 128), F32)
                    for here in range(0, BLOCK, GROUP):
                        rows, there = slice(here, here + GROUP), pl.ds(start + here, GROUP)
                        gains = ps[index, there, cols].reshape(GROUP // 8, 8, 128)
                        carried = (cs[index, there, cols].reshape(GROUP // 8, 8, 128) + gains * entering).reshape(GROUP, 128)
                        carried_out[index][rows, cols] = carried.astype(BF16)
                        admit_delta = (carried * admit_fac[rows, cols].astype(F32)).astype(BF16)
                        deltas[index, 0, rows, cols] = (carried * forget_fac[rows, cols].astype(F32)).astype(BF16)
                        deltas[index, 1, rows, cols] = admit_delta
                        deltas[index, 2, rows, cols] = (carried * admits[index, there, cols].astype(F32)).astype(BF16)
                        bias = bias + fold_rows(admit_delta.astype(F32))
                    bias_out[index, :, cols] += bias
                for part in range(3):
                    cols = slice(first, first + wide)
                    slopes_acc[index, part, :, cols] += dot_nn(normed_t, deltas[index, part, :, cols])
            tall = output_grads.shape[0]
            for half in range(2):
                @pl.when(block // (blocks // 2) == half)
                def _():
                    there = pl.multiple_of(block % (blocks // 2) * tall, tall)
                    second_out[half][index, pl.ds(there, tall), channels:] = output_grads[...]

    @pl.when((phase == 1) & (block == blocks - 1))
    def _():
        for index in range(sets):
            put_blocks(slopes_acc.at[index, 0], [out.at[index] for out in first_out], me_ref[0], 0)
            put_blocks(slopes_acc.at[index, 1], [out.at[index] for out in first_out], me_ref[0], channels)
            put_blocks(slopes_acc.at[index, 2], [out.at[index] for out in second_out], me_ref[1], 0)


def mixer_backward(mixed, normed, mask, me, per_set):
    rows, width = mixed.shape
    sets = len(per_set)
    channels = mask.shape[1]
    blocks = rows // BLOCK
    back = lambda phase, block: (jnp.where(phase == 0, blocks - 1 - block, 0), 0)
    late = lambda phase, block: (jnp.where(phase == 0, 0, block), 0)
    whole = lambda phase, block: (0, 0)
    all3 = lambda phase, block: (0, 0, 0)
    set_specs = [
        pl.BlockSpec((channels, width), whole),
        pl.BlockSpec((BLOCK, channels), back),
        pl.BlockSpec((BLOCK, channels), late),
        pl.BlockSpec((BLOCK, channels), late),
        pl.BlockSpec((1, channels), whole),
        pl.BlockSpec((width // blocks, channels), late),
    ]
    results = pl.pallas_call(
        functools.partial(mixer_back_kernel, sets),
        grid=(2, blocks),
        in_specs=[
            pl.BlockSpec((BLOCK, width), back),
            pl.BlockSpec((BLOCK, width), late),
            pl.BlockSpec((8, channels), whole),
            pl.BlockSpec(memory_space=pltpu.SMEM),
        ]
        + set_specs * sets,
        out_specs=[pl.BlockSpec((BLOCK, channels), late)] * sets
        + [pl.BlockSpec((sets, width // 2, 2 * channels), all3)] * 4
        + [pl.BlockSpec((sets, 8, channels), all3)] * 2,
        out_shape=[jax.ShapeDtypeStruct((rows, channels), BF16)] * sets
        + [jax.ShapeDtypeStruct((sets, width // 2, 2 * channels), BF16)] * 4
        + [jax.ShapeDtypeStruct((sets, 8, channels), F32)] * 2,
        scratch_shapes=[
            pltpu.VMEM((sets, rows, channels), F32),
            pltpu.VMEM((sets, rows, channels), F32),
            pltpu.VMEM((sets, BLOCK, channels), F32),
            pltpu.VMEM((sets, rows, channels), BF16),
            pltpu.VMEM((sets, 3, BLOCK, channels), BF16),
            pltpu.VMEM((sets, 3, width, channels), F32),
            pltpu.VMEM((sets, 16, channels), F32),
            pltpu.VMEM((sets, 8, channels), F32),
        ],
        compiler_params=pltpu.CompilerParams(vmem_limit_bytes=VMEM_BYTES, dimension_semantics=("arbitrary", "arbitrary")),
        cost_estimate=pl.CostEstimate(flops=2 * rows * width * 4 * channels * sets, bytes_accessed=rows * channels * 12 * sets, transcendentals=0),
        name="mixer_backward",
    )(mixed, normed, mask, me, *[item for one in per_set for item in one])
    return results[:sets], results[sets : sets + 2], results[sets + 2 : sets + 4], *results[sets + 4 :]


def input_kernel(sets, *refs):
    x_ref, mixed_ref, gain_ref, *refs = refs
    factors, refs = refs[: 4 * sets], refs[4 * sets :]
    weights, refs = refs[: 3 * sets], refs[3 * sets :]
    out_ref, slope_ref, out_s = refs

    @pl.when(pl.program_id(0) == 0)
    def _():
        slope_ref[...] = jnp.zeros_like(slope_ref)

    normed_delta = None
    for index in range(sets):
        carried = factors[4 * index][...].astype(F32)
        for part in range(3):
            delta = (carried * factors[4 * index + 1 + part][...].astype(F32)).astype(BF16)
            term = dot_nt(delta, weights[3 * index + part][...])
            normed_delta = term if normed_delta is None else normed_delta + term
    rows = x_ref[...].astype(F32)
    scale = row_scale(rows)
    slope_ref[...] += fold_rows(normed_delta * rows * scale)
    scaled = normed_delta * gain_ref[...]
    inner = jnp.mean(scaled * rows, -1, keepdims=True)
    result = mixed_ref[...].astype(F32) + scale * (scaled - rows * (scale * scale * inner))
    separate(result, out_s, out_ref)


def input_backward(x_rows, mixed, gain, factors, weights):
    rows, width = x_rows.shape
    sets = len(factors) // 4
    channels = weights[0].shape[1]
    by_rows = lambda block: (block, 0)
    whole = lambda block: (0, 0)
    return pl.pallas_call(
        functools.partial(input_kernel, sets),
        grid=(rows // BLOCK,),
        in_specs=[pl.BlockSpec((BLOCK, width), by_rows)] * 2
        + [pl.BlockSpec((1, width), whole)]
        + [pl.BlockSpec((BLOCK, channels), by_rows)] * (4 * sets)
        + [pl.BlockSpec((width, channels), whole)] * (3 * sets),
        out_specs=[pl.BlockSpec((SEGMENTS, STEPS, width), lambda block: (0, block, 0)), pl.BlockSpec((8, width), whole)],
        out_shape=[jax.ShapeDtypeStruct((SEGMENTS, rows // SEGMENTS, width), F32), jax.ShapeDtypeStruct((8, width), F32)],
        scratch_shapes=[pltpu.VMEM((width // 128, BLOCK, 128), F32)],
        compiler_params=pltpu.CompilerParams(vmem_limit_bytes=VMEM_BYTES, dimension_semantics=("arbitrary",)),
        cost_estimate=pl.CostEstimate(flops=2 * rows * width * 3 * channels * sets, bytes_accessed=rows * channels * 8 * sets, transcendentals=0),
        name="input_backward",
    )(x_rows, mixed, gain, *factors, *weights)


def finish_kernel(channels, first_low, first_high, second_low, second_high, me_ref, forget_out, admit_out, value_out, output_out, scratch):
    tall = 2 * first_low.shape[0] // PLACES
    for place in range(PLACES):
        here = slice(place % (PLACES // 2) * tall, (place % (PLACES // 2) + 1) * tall)
        first_ref, second_ref = ((first_low, second_low), (first_high, second_high))[place // (PLACES // 2)]
        for index, (sums, outs) in enumerate(((first_ref, (forget_out, admit_out)), (second_ref, (value_out, scratch)))):
            there = pl.multiple_of((place ^ me_ref[index]) * tall, tall)
            outs[0][pl.ds(there, tall), :] = sums[here, :channels].astype(F32)
            outs[1][pl.ds(there, tall), :] = sums[here, channels:].astype(F32)
    output_out[...] = scratch[...].T


def finish_slopes(first, second, me):
    width, channels = 2 * first[0].shape[0], first[0].shape[1] // 2
    return pl.pallas_call(
        functools.partial(finish_kernel, channels),
        in_specs=[pl.BlockSpec(memory_space=pltpu.VMEM)] * 4 + [pl.BlockSpec(memory_space=pltpu.SMEM)],
        out_shape=[jax.ShapeDtypeStruct((width, channels), F32)] * 3 + [jax.ShapeDtypeStruct((channels, width), F32)],
        scratch_shapes=[pltpu.VMEM((width, channels), F32)],
        compiler_params=pltpu.CompilerParams(vmem_limit_bytes=VMEM_BYTES),
        name="finish_slopes",
    )(*first, *second, me)


def run_masks(seq_lengths, rows, shift, channels):
    ends = jnp.cumsum(seq_lengths[0])
    begins = ends - seq_lengths[0]
    places = shift + jnp.arange(SEGMENTS, dtype=jnp.int32) * (rows // SEGMENTS)
    fresh = jnp.any((places[:, None] == begins[None, :]) & (seq_lengths[0] > 0)[None, :], -1)
    return jnp.broadcast_to(jnp.where(fresh, 0.0, 1.0).astype(F32)[:, None], (SEGMENTS, channels))


def regroup(stacked, half):
    count, both, width = stacked.shape
    if both == 2 * half:
        return stacked
    arrays = jnp.moveaxis(stacked.reshape(count, 2, both // 2, width), 1, 0).reshape(2, -1, half, width)
    return jnp.moveaxis(arrays, 0, 1).reshape(-1, 2 * half, width)


def added(mine, theirs):
    return (mine.astype(F32) + theirs.astype(F32)).astype(mine.dtype)


def after(values, *earlier):
    return lax.optimization_barrier((values, earlier))[0]


class Links:
    TENSOR, CORE, NEAR, Z_NEAR, Z_FAR = 1, 2, 4, 8, 16
    FIRST = (CORE, TENSOR, NEAR, Z_NEAR, Z_FAR)
    SECOND = (CORE, Z_NEAR, TENSOR, NEAR, Z_FAR)

    def __init__(self):
        dp = lax.axis_index("dp")
        core, near, z_near, z_far = dp % 2, dp // 2 % 2, dp // 4 % 2, dp // 8
        self.core = core
        first = core * 8 + near * 4 + z_near * 2 + z_far
        second = core * 8 + z_near * 4 + near * 2 + z_far
        self.me = jnp.stack([first, second]).astype(jnp.int32)

    def swap(self, values, bit):
        pairs = [(device, device ^ bit) for device in range(32)]
        return lax.ppermute(values, ("dp", "tensor"), pairs)

    def begin_weights(self, own_weights):
        half = own_weights[0].shape[0] // 2
        cut = [lax.dynamic_slice_in_dim(w, self.core * half, half) for w in own_weights]
        mine = jnp.stack(cut[:3])
        first = self.swap(mine, self.TENSOR)
        return mine, first, lambda: self.swap(after(cut[3], first), self.TENSOR)

    def end_weights(self, got):
        rest = self.swap(got, self.CORE)
        lower = self.core == 0
        return jnp.concatenate([jnp.where(lower, got, rest), jnp.where(lower, rest, got)], -2)

    def bias(self, own_bias):
        return own_bias, self.swap(own_bias, self.TENSOR)

    def begin_dense(self, shard):
        return [shard] + [self.swap(shard, bits) for bits in (self.Z_NEAR, self.Z_FAR, self.Z_NEAR | self.Z_FAR)]

    def middle_dense(self, pieces):
        own = jnp.stack(pieces)
        return own, self.swap(own, self.NEAR), self.swap(own, self.TENSOR)

    def end_dense(self, own, near, other):
        own = jnp.concatenate([own, near], 0)
        other = jnp.concatenate([other, self.swap(other, self.NEAR)], 0)
        own_rest, other_rest = self.swap(own, self.CORE), self.swap(other, self.CORE)
        return jnp.concatenate([own, other, own_rest, other_rest], 0)

    def dense_begin(self, upper, lower):
        cut = lambda values: values.reshape(2, 2, 2, 2, *values.shape[1:])
        orders = ([0, 1, 3, 2], [1, 0, 3, 2])
        return [(cut(keep), cut(self.swap(send, self.CORE)), order) for (keep, send), order in zip((upper, lower), orders)]

    def dense_step(self, stream):
        bits = (self.TENSOR, self.NEAR, self.Z_FAR, self.Z_NEAR)
        kept, received, order = stream
        if not order:
            return added(kept, received)
        axis = order[0]
        part = lambda values, index: lax.index_in_dim(values, index, axis, keepdims=True)
        send = added(part(kept, 1), part(received, 1))
        return added(part(kept, 0), part(received, 0)), self.swap(send, bits[axis]), order[1:]

    def mixer_step(self, kept, received, bit, extra=None):
        if bit == self.TENSOR:
            part = lambda values, index: values[index : index + 1]
        else:
            part = lambda values, index: values[:, index * (values.shape[1] // 2) : (index + 1) * (values.shape[1] // 2)]
        send = added(part(kept, 1), part(received, 1))
        keep = added(part(kept, 0), part(received, 0))
        if extra is None:
            return keep, self.swap(send, bit)
        got = self.swap(jnp.concatenate([send, extra], 1), bit)
        return keep, got[:, : send.shape[1]], added(extra, got[:, send.shape[1] :])

    def mixer_grow(self, values, bit):
        return jnp.concatenate([values, self.swap(values, bit)], 1)

    def grow_with(self, values, extra, bit):
        got = self.swap(jnp.concatenate([values, extra], 1), bit)
        return values, got[:, : values.shape[1]], added(extra, got[:, values.shape[1] :])


class Plain:
    def __init__(self, n_tensor, own):
        self.n_tensor, self.own = n_tensor, own
        self.me = jnp.zeros((2,), jnp.int32)

    def weights(self, own_weights):
        whole = [lax.all_gather(w, "tensor", axis=1, tiled=True) for w in own_weights[:3]]
        pairs = [jnp.split(w, 2, 1) for w in whole]
        pairs.append(jnp.split(lax.all_gather(own_weights[3], "tensor", axis=0, tiled=True), 2, 0))
        return [p[0] for p in pairs], [p[1] for p in pairs]

    def bias(self, own_bias):
        return tuple(jnp.split(lax.all_gather(own_bias, "tensor", axis=0, tiled=True), 2))

    def dense(self, shard):
        return regroup(lax.all_gather(shard, ("dp", "tensor"), axis=0), 64)

    def dense_sums(self, upper, lower):
        pairs = [jnp.concatenate(halves, 0) for halves in (upper, lower)]
        return [lax.psum_scatter(g.reshape(-1, g.shape[-1]), ("dp", "tensor"), scatter_dimension=0, tiled=True) for g in pairs]

    def mixer_sums(self, grads):
        grads = jnp.concatenate(grads, 1)
        _, width, columns = grads.shape
        whole = jnp.moveaxis(grads.reshape(2, width, 2, columns // 2), 0, 2).reshape(width, 2, columns)
        part = lax.psum_scatter(whole, "tensor", scatter_dimension=2, tiled=True)
        return jnp.split(lax.psum(part, "dp").reshape(width, 2 * self.own), 2, 0)

def on_device(
    block_in,
    out_cotangent,
    seq_lengths,
    premix_gain,
    forget_weight,
    admit_weight,
    value_weight,
    admit_bias,
    output_weight,
    dense_gain,
    upper_weight,
    lower_weight,
):
    n_dp, n_tensor = lax.axis_size("dp"), lax.axis_size("tensor")
    rows, width = block_in.shape
    place = lax.axis_index("tensor")
    own = forget_weight.shape[1]
    premix = premix_gain.astype(F32)[None]
    dense = dense_gain.astype(F32)[None]
    paired = (n_dp, n_tensor) == (16, 2)
    links = Links() if paired else Plain(n_tensor, own)
    me = links.me
    own_weights = [forget_weight, admit_weight, value_weight, output_weight]
    dense_shard = jnp.concatenate([upper_weight.T, lower_weight], 0)
    if paired:
        weights = [own_weights, None]
        channels = own
        mine, got, begin_output = links.begin_weights(own_weights)
        pieces = links.begin_dense(after(dense_shard, mine))
    else:
        weights = links.weights(own_weights)
        channels = weights[0][0].shape[1]
    biases = [b.astype(F32)[None] for b in links.bias(admit_bias)]
    mask = run_masks(seq_lengths, rows, place * rows, channels)
    crossing = rows % LONGEST != 0
    nothing = jnp.zeros((1, channels), F32)

    def chained(ends, backwards):
        every = lax.all_gather(ends, "tensor", axis=0)
        entering = jnp.zeros_like(ends[0:1])
        mine = entering
        order = range(n_tensor - 1, -1, -1) if backwards else range(n_tensor)
        for index in order:
            mine = jnp.where(place == index, entering, mine)
            entering = every[index, 0:1] + every[index, 1:2] * entering
        return mine

    def forward(first, rows_in, index):
        carry = nothing
        if crossing:
            ends = mixer_forward(first, rows_in, premix, weights[index][:3], biases[index], mask, carry)[-1]
            carry = chained(ends, False)
        return mixer_forward(first, rows_in, premix, weights[index][:3], biases[index], mask, carry)

    x_rows, normed, *kept_0 = forward(True, block_in, 0)
    if paired:
        got, pieces = after((got, pieces), normed)
        got_output = begin_output()
        middle = links.middle_dense(pieces)
        other = links.end_weights(got)
        weights[1] = [other[0], other[1], other[2]]
    kept_1 = forward(False, normed, 1)
    if paired:
        got_output, middle = after((got_output, middle), kept_1[1])
        weights[1].append(links.end_weights(got_output))
        gathered = links.end_dense(*middle)
    else:
        gathered = links.dense(dense_shard)
    kept = [kept_0, kept_1]
    outputs = [w[3] for w in weights]
    block_out, mixed, *dense_grads, dense_part, grads_0, grads_1 = dense_both(
        x_rows, out_cotangent, [k[1] for k in kept], outputs, dense, gathered, me
    )
    output_grads = [grads_0, grads_1]
    if paired:
        dense_streams = links.dense_begin(dense_grads[:2], dense_grads[2:])

    carries = [nothing, nothing]
    for _ in range(2 if crossing else 1):
        per_set = [
            (outputs[index], kept[index][0], kept[index][2], kept[index][3], carries[index], output_grads[index])
            for index in range(2)
        ]
        carried, first, second, bias_parts, ends = mixer_backward(mixed, normed, mask, me, per_set)
        if crossing:
            carries = [chained(ends[index], True) for index in range(2)]
    factors = [f for index in range(2) for f in (carried[index], kept[index][2], kept[index][3], kept[index][0])]
    if paired:
        first = first[0], links.swap(first[1], Links.CORE)
        second = second[0], links.swap(second[1], Links.CORE)
        factors[0] = after(factors[0], first, second)
        first = links.mixer_step(*first, Links.FIRST[1])
        second = links.mixer_step(*second, Links.SECOND[1])
    input_slope, premix_part = input_backward(x_rows, mixed, premix, factors, weights[0][:3] + weights[1][:3])

    bias_parts = jnp.sum(bias_parts, 1)
    if paired:
        bias_parts = jnp.where(place == 0, bias_parts, bias_parts[::-1])
    small = jnp.concatenate([jnp.sum(premix_part, 0), jnp.sum(dense_part, 0), bias_parts[0], bias_parts[1]], 0)
    if paired:
        small = small.reshape(1, -1, 2 * channels).astype(BF16)
        filled = small.shape[1]
        small = jnp.pad(small, ((0, 0), (0, 16 - filled), (0, 0)))
        first, second = after((first, second), small)
        for step in (2, 3, 4):
            first = links.mixer_step(*first, Links.FIRST[step])
            *second, small = links.mixer_step(*second, Links.SECOND[step], small)
        first, second = added(*first), added(*second)
        first, second = links.mixer_grow(first, Links.Z_FAR), links.mixer_grow(second, Links.Z_FAR)
        low, high, small = links.grow_with(first, small, Links.Z_NEAR)
        first, second = jnp.concatenate([low, high], 1), links.mixer_grow(second, Links.NEAR)
        first, second = links.mixer_grow(first, Links.NEAR), links.mixer_grow(second, Links.Z_NEAR)
        first = first[0], links.swap(first, Links.CORE)[0]
        low, high, small = links.grow_with(second, small, Links.CORE)
        second = low[0], high[0]
        small = small[0, :filled].reshape(-1).astype(F32)
        for _ in range(4):
            dense_streams = [links.dense_step(d) for d in dense_streams]
        upper_sum, lower_sum = (links.dense_step(d).reshape(-1, width) for d in dense_streams)
    else:
        small = lax.psum(small, ("dp", "tensor"))
        upper_sum, lower_sum = links.dense_sums(dense_grads[:2], dense_grads[2:])
        first, second = links.mixer_sums(first), links.mixer_sums(second)
    upper_slope, lower_slope = upper_sum.astype(F32).T, lower_sum.astype(F32)
    forget_slope, admit_slope, value_slope, output_slope = finish_slopes(first, second, me)
    shard = width // (n_dp * n_tensor)
    at = (lax.axis_index("dp") * n_tensor + place) * shard
    premix_slope = lax.dynamic_slice(small, (at,), (shard,))
    dense_slope = lax.dynamic_slice(small, (width + at,), (shard,))
    bias_slope = lax.dynamic_slice(small, (2 * width + place * own,), (own,))
    return (
        block_out.reshape(rows, width),
        input_slope.reshape(rows, width),
        premix_slope,
        forget_slope,
        admit_slope,
        value_slope,
        bias_slope,
        output_slope,
        dense_slope,
        upper_slope,
        lower_slope,
    )


def solution(mesh):
    placed = (
        P(("dp", "tensor"), None),
        P(("dp", "tensor"), None),
        P("dp", None),
        P(),
        P(None, "tensor"),
        P(None, "tensor"),
        P(None, "tensor"),
        P("tensor"),
        P("tensor", None),
        P(),
        P(None, ("dp", "tensor")),
        P(("dp", "tensor"), None),
    )
    return jax.shard_map(
        on_device,
        mesh=mesh,
        in_specs=placed,
        out_specs=(
            P(("dp", "tensor"), None),
            P(("dp", "tensor"), None),
            P(("dp", "tensor")),
            P(None, "tensor"),
            P(None, "tensor"),
            P(None, "tensor"),
            P("tensor"),
            P("tensor", None),
            P(("dp", "tensor")),
            P(None, ("dp", "tensor")),
            P(("dp", "tensor"), None),
        ),
        check_vma=False,
    )
```

```python
import functools

import jax
import jax.numpy as jnp
from jax import lax
from jax.experimental import pallas as pl
from jax.experimental.pallas import tpu as pltpu
from jax.sharding import PartitionSpec as P

EPSILON = 1e-06
LONGEST = 2048
SEGMENTS = 8
PLACES = 16
STEPS = 64
BLOCK = SEGMENTS * STEPS
GROUP = 32
GELU_SLOPE = 0.7978845608028654
GELU_CUBE = 0.044715
VMEM_BYTES = 56 * 1024 * 1024
F32 = jnp.float32
BF16 = jnp.bfloat16


def dot_nn(left, right):
    return lax.dot_general(left, right, (((1,), (0,)), ((), ())), preferred_element_type=F32)


def dot_nt(left, right):
    return lax.dot_general(left, right, (((1,), (1,)), ((), ())), preferred_element_type=F32)


def row_scale(rows):
    return lax.rsqrt(jnp.mean(rows * rows, -1, keepdims=True) + EPSILON)


def fold_rows(values):
    return jnp.sum(values.reshape(-1, 8, values.shape[-1]), 0)


def put_blocks(values, halves, me, first):
    tall = values.shape[0] // PLACES
    for place in range(PLACES):
        block = pl.multiple_of((place ^ me) * tall, tall)
        there = (place % (PLACES // 2)) * tall
        out = halves[place // (PLACES // 2)]
        out[there : there + tall, first : first + values.shape[1]] = values[pl.ds(block, tall), :].astype(out.dtype)


def interleave(block, scratch):
    lanes = scratch.shape[0]
    for lane in range(lanes):
        for run in range(SEGMENTS):
            part = block[run, :, lane * 128 : (lane + 1) * 128]
            scratch[lane, pl.ds(run, block.shape[1], stride=SEGMENTS), :] = part.astype(F32)
    return jnp.concatenate([scratch[lane] for lane in range(lanes)], -1)


def separate(values, scratch, out):
    lanes = scratch.shape[0]
    for lane in range(lanes):
        scratch[lane] = values[:, lane * 128 : (lane + 1) * 128]
    for run in range(SEGMENTS):
        parts = [scratch[lane, pl.ds(run, out.shape[1], stride=SEGMENTS), :] for lane in range(lanes)]
        out[run] = jnp.concatenate(parts, -1).astype(out.dtype)


def gates(forget_logit, admit_logit):
    top = jnp.maximum(jnp.maximum(-admit_logit, -forget_logit), 0.0)
    one = jnp.exp(-top)
    admit_exp = jnp.exp(-admit_logit - top)
    forget_exp = jnp.exp(-forget_logit - top)
    keep_part = one + admit_exp
    admit_part = one + forget_exp
    total = keep_part + admit_part
    inverse = pl.reciprocal(total, approx=True)
    inverse = inverse * (2.0 - total * inverse)
    keep = keep_part * inverse
    admit = admit_part * inverse
    return keep, admit, keep * (forget_exp * inverse), -admit * (admit_exp * inverse)


def goes_on(lengths_ref, scalars_ref, run, tall):
    place = scalars_ref[0] + run * tall
    begin = jnp.int32(0)
    fresh = False
    for entry in range(lengths_ref.shape[1]):
        length = lengths_ref[0, entry]
        fresh = fresh | ((begin == place) & (length > 0))
        begin = begin + length
    return jnp.where(fresh, 0.0, 1.0).astype(F32)


def product_of_runs(values, masks):
    result = masks[0] * values[0:1]
    for run in range(1, SEGMENTS):
        result = result * (masks[run] * values[run : run + 1])
    return result


def mixer_kernel(first, *refs):
    if first:
        x_ref, gain_ref, *refs = refs
    else:
        normed_in, *refs = refs
    wf, wa, wv, bias, lengths, scalars, carry, *refs = refs
    if first:
        x_out, normed_out, *refs = refs
    admit_out, state_out, forget_fac, admit_fac, ends_out, *refs = refs
    logits, hs, ps, vs, fs, as_, enter, *refs = refs
    phase, block = pl.program_id(0), pl.program_id(1)
    channels = wf.shape[1]
    start = pl.multiple_of(block * BLOCK, BLOCK)

    @pl.when((phase == 0) & (block == 0))
    def _():
        hs[0:8, :] = jnp.zeros((8, channels), F32)
        ps[0:8, :] = jnp.ones((8, channels), F32)

    @pl.when(phase == 0)
    def _():
        if first:
            rows = interleave(x_ref[...], refs[0])
            x_out[...] = rows.astype(BF16)
            normed = (rows * row_scale(rows) * gain_ref[...]).astype(BF16)
            normed_out[...] = normed
        else:
            normed = normed_in[...]
        wide = min(channels, 256)
        chunks = channels // wide
        weights = (wf, wa, wv)

        def project(chunk, kind):
            logits[chunk, kind] = dot_nn(normed, weights[kind][:, chunk * wide : (chunk + 1) * wide])

        def gate(chunk, lane, here, chain):
            inner, cols = slice(lane, lane + 128), slice(chunk * wide + lane, chunk * wide + lane + 128)
            rows = slice(here, here + GROUP)
            there = pl.ds(start + here, GROUP)
            value = logits[chunk, 2, rows, inner]
            keep, admit, forget_side, admit_side = gates(
                logits[chunk, 0, rows, inner], logits[chunk, 1, rows, inner] + bias[:, cols]
            )
            admit_out[rows, cols] = admit.astype(BF16)
            vs[there, cols] = value
            fs[there, cols] = forget_side
            as_[there, cols] = admit_side
            inflow = admit * value
            state, gain = chain
            for step in range(0, GROUP, 8):
                state = keep[step : step + 8] * state + inflow[step : step + 8]
                gain = gain * keep[step : step + 8]
                hs[pl.ds(start + here + step + 8, 8), cols] = state
                ps[pl.ds(start + here + step + 8, 8), cols] = gain
            return state, gain

        for kind in range(3):
            project(0, kind)
        for chunk in range(chunks):
            firsts = range(chunk * wide, (chunk + 1) * wide, 128)
            chains = [(hs[pl.ds(start, 8), c : c + 128], ps[pl.ds(start, 8), c : c + 128]) for c in firsts]
            units = [(here, lane) for here in range(0, BLOCK, GROUP) for lane in range(len(chains))]
            ahead = [(chunk + 1, kind) for kind in range(3)] if chunk + 1 < chunks else []
            for index, (here, lane) in enumerate(units):
                if ahead and index % max(1, len(units) // 3) == 0:
                    project(*ahead.pop(0))
                chains[lane] = gate(chunk, lane * 128, here, chains[lane])
            for item in ahead:
                project(*item)

    @pl.when((phase == 1) & (block == 0))
    def _():
        total = hs.shape[0]
        ends, gains = hs[total - 8 : total, :], ps[total - 8 : total, :]
        masks = [goes_on(lengths, scalars, run, (total - 8) // SEGMENTS) for run in range(SEGMENTS)]
        entering = masks[0] * carry[...]
        enter[0:1] = entering
        for run in range(1, SEGMENTS):
            entering = masks[run] * (ends[run - 1 : run] + gains[run - 1 : run] * entering)
            enter[run : run + 1] = entering
        ends_out[0:1, :] = ends[7:8] + gains[7:8] * enter[7:8, :]
        ends_out[1:2, :] = product_of_runs(gains, masks)
        ends_out[2:8, :] = jnp.zeros((6, channels), F32)

    @pl.when(phase == 1)
    def _():
        def some_rows(group, _):
            here = pl.multiple_of(group * 64, 64)
            there = pl.multiple_of(start + here, 64)
            for lane in range(0, channels, 128):
                cols = pl.ds(lane, 128)
                entering = enter[:, lane : lane + 128]
                states = hs[pl.ds(there, 72), cols].reshape(9, 8, 128) + ps[pl.ds(there, 72), cols].reshape(9, 8, 128) * entering
                states = states.reshape(72, 128)
                state_out[pl.ds(here, 64), cols] = states[8:].astype(BF16)
                change = states[:64] - vs[pl.ds(there, 64), cols]
                forget_fac[pl.ds(here, 64), cols] = (change * fs[pl.ds(there, 64), cols]).astype(BF16)
                admit_fac[pl.ds(here, 64), cols] = (change * as_[pl.ds(there, 64), cols]).astype(BF16)
            return 0

        lax.fori_loop(0, BLOCK // 64, some_rows, 0)


def mixer_forward(first, rows_in, gain, weights, bias, lengths, scalars, carry):
    width = rows_in.shape[-1]
    rows = rows_in.size // width
    channels = weights[0].shape[1]
    blocks = rows // BLOCK
    early = lambda phase, block: (jnp.where(phase == 0, block, blocks - 1), 0)
    late = lambda phase, block: (jnp.where(phase == 0, 0, block), 0)
    whole = lambda phase, block: (0, 0)
    if first:
        in_specs = [
            pl.BlockSpec((SEGMENTS, STEPS, width), lambda phase, block: (0, jnp.where(phase == 0, block, blocks - 1), 0)),
            pl.BlockSpec((1, width), whole),
        ]
        operands = [rows_in.reshape(SEGMENTS, rows // SEGMENTS, width), gain]
        out_specs = [pl.BlockSpec((BLOCK, width), early)] * 2
        out_shape = [jax.ShapeDtypeStruct((rows, width), BF16)] * 2
    else:
        in_specs, operands = [pl.BlockSpec((BLOCK, width), early)], [rows_in]
        out_specs, out_shape = [], []
    in_specs += [pl.BlockSpec((width, channels), whole)] * 3
    in_specs += [pl.BlockSpec((1, channels), whole)] + [pl.BlockSpec(memory_space=pltpu.SMEM)] * 2 + [pl.BlockSpec((1, channels), whole)]
    out_specs += [pl.BlockSpec((BLOCK, channels), early)] + [pl.BlockSpec((BLOCK, channels), late)] * 3
    out_specs += [pl.BlockSpec((8, channels), whole)]
    out_shape += [jax.ShapeDtypeStruct((rows, channels), BF16)] * 4
    out_shape += [jax.ShapeDtypeStruct((8, channels), F32)]
    wide = min(channels, 256)
    scratch = [pltpu.VMEM((channels // wide, 3, BLOCK, wide), F32)]
    scratch += [pltpu.VMEM((rows + 8, channels), F32)] * 2
    scratch += [pltpu.VMEM((rows, channels), F32)] * 3
    scratch += [pltpu.VMEM((8, channels), F32)]
    if first:
        scratch += [pltpu.VMEM((width // 128, BLOCK, 128), F32)]
    return pl.pallas_call(
        functools.partial(mixer_kernel, first),
        grid=(2, blocks),
        in_specs=in_specs,
        out_specs=out_specs,
        out_shape=out_shape,
        scratch_shapes=scratch,
        compiler_params=pltpu.CompilerParams(vmem_limit_bytes=VMEM_BYTES, dimension_semantics=("arbitrary", "arbitrary")),
        cost_estimate=pl.CostEstimate(flops=2 * rows * width * 3 * channels, bytes_accessed=rows * channels * 16, transcendentals=4 * rows * channels),
        name="mixer_forward",
    )(*operands, *weights, bias, lengths, scalars, carry)


def dense_kernel(stage, sets, pieces, *refs):
    states, refs = refs[:sets], refs[sets:]
    if stage == 0:
        x_ref, c_ref, *refs = refs
        outs_w, refs = refs[:sets], refs[sets:]
    else:
        middle_ref, sum_ref, delta_ref, dense_ref, cotangent_ref, *refs = refs
    gain_ref, scalars, *refs = refs
    pieces_w, refs = refs[:pieces], refs[pieces:]
    keep_out, send_out, *refs = refs
    if stage == 0:
        middle_out, sum_out, delta_out, dense_out, cotangent_out, upper_acc, lower_acc, cotangent_s = refs
    else:
        out_ref, mixed_ref, slope_ref, *refs = refs
        outputs_ref, refs = refs[:sets], refs[sets:]
        upper_acc, lower_acc, output_acc, out_s = refs
    step = pl.program_id(0)
    gain = gain_ref[...]
    shards, both, width = pieces_w[0].shape
    half = both // 2

    @pl.when(step == 0)
    def _():
        upper_acc[...] = jnp.zeros_like(upper_acc)
        lower_acc[...] = jnp.zeros_like(lower_acc)
        if stage == 1:
            output_acc[...] = jnp.zeros_like(output_acc)
            slope_ref[...] = jnp.zeros_like(slope_ref)

    if stage == 0:
        middle = x_ref[...].astype(F32)
        for state, weight in zip(states, outs_w):
            middle = middle + dot_nn(state[...], weight[...])
        middle_out[...] = middle
        dense_in = (middle * row_scale(middle) * gain).astype(BF16)
        dense_out[...] = dense_in
        cotangent = interleave(c_ref[...], cotangent_s).astype(BF16)
        cotangent_out[...] = cotangent
    else:
        dense_in, cotangent = dense_ref[...], cotangent_ref[...]
    dense_t, cotangent_t = dense_in.T, cotangent.T
    fed, delta = None, None
    joined = max(1, 512 // (shards * half))
    for chunk in range(0, pieces, joined):
        some = pieces_w[chunk : chunk + joined]
        upper_w = jnp.concatenate([w[:, :half, :].reshape(shards * half, width) for w in some], 0)
        lower_w = jnp.concatenate([w[:, half:, :].reshape(shards * half, width) for w in some], 0)
        cols = slice(chunk * shards * half, (chunk + joined) * shards * half)
        upper = dot_nt(dense_in, upper_w)
        square = upper * upper
        bell = 0.5 + 0.5 * jnp.tanh(upper * (GELU_SLOPE + GELU_SLOPE * GELU_CUBE * square))
        active = upper * bell
        slope = bell + active * (1.0 - bell) * (2.0 * GELU_SLOPE + 6.0 * GELU_SLOPE * GELU_CUBE * square)
        active = active.astype(BF16)
        part = dot_nn(active, lower_w)
        fed = part if fed is None else fed + part
        upper_delta = (slope * dot_nt(cotangent, lower_w)).astype(BF16)
        part = dot_nn(upper_delta, upper_w)
        delta = part if delta is None else delta + part
        lower_acc[:, cols] += dot_nn(cotangent_t, active)
        upper_acc[:, cols] += dot_nn(dense_t, upper_delta)
    if stage == 0:
        sum_out[...] = middle + fed
        delta_out[...] = delta
    else:
        separate(sum_ref[...] + fed, out_s, out_ref)
        middle = middle_ref[...]
        scale = row_scale(middle)
        delta = delta_ref[...] + delta
        slope_ref[...] += fold_rows(delta * middle * scale)
        scaled = delta * gain
        inner = jnp.mean(scaled * middle, -1, keepdims=True)
        mixed = (cotangent.astype(F32) + scale * (scaled - middle * (scale * scale * inner))).astype(BF16)
        mixed_ref[...] = mixed
        mixed_t = mixed.T
        channels = states[0].shape[1]
        for index, state in enumerate(states):
            output_acc[:, index * channels : (index + 1) * channels] += dot_nn(mixed_t, state[...])

    @pl.when(step == pl.num_programs(0) - 1)
    def _():
        for shard in range(0, pieces * shards, 2):
            cols = slice(shard * half, (shard + 2) * half)
            out = keep_out if shard < pieces * shards // 2 else send_out
            there = shard % (pieces * shards // 2)
            out[0, there : there + 2] = upper_acc[:, cols].T.astype(BF16).reshape(2, half, width)
            out[1, there : there + 2] = lower_acc[:, cols].T.astype(BF16).reshape(2, half, width)
        if stage == 1:
            tall = output_acc.shape[0] // PLACES
            for index, output in enumerate(outputs_ref):
                for place in range(PLACES):
                    there = pl.multiple_of((place ^ scalars[2]) * tall, tall)
                    output[place * tall : (place + 1) * tall, :] = output_acc[
                        pl.ds(there, tall), index * channels : (index + 1) * channels
                    ].astype(BF16)


def dense_both(stage, states, entering, output_weights, gain, scalars, pieces):
    rows, channels = states[0].shape
    width = gain.shape[1]
    shards, both, _ = pieces[0].shape
    hidden = len(pieces) * shards * both // 2
    sets = len(states)
    tall = min(rows, 512)
    by_rows = lambda block: (block, 0)
    whole = lambda block: (0, 0)
    runs_spec = pl.BlockSpec((SEGMENTS, tall // SEGMENTS, width), lambda block: (0, block, 0))
    runs_shape = (SEGMENTS, rows // SEGMENTS, width)
    row_spec = pl.BlockSpec((tall, width), by_rows)
    grads = (2, len(pieces) * shards // 2, both // 2, width)
    in_specs = [pl.BlockSpec((tall, channels), by_rows)] * sets
    out_specs = [pl.BlockSpec(grads, lambda block: (0, 0, 0, 0))] * 2
    out_shape = [jax.ShapeDtypeStruct(grads, BF16)] * 2
    scratch = [pltpu.VMEM((width, hidden), F32)] * 2
    if stage == 0:
        in_specs += [row_spec, runs_spec] + [pl.BlockSpec((channels, width), whole)] * sets
        entering = [entering[0], entering[1].reshape(runs_shape), *output_weights]
        out_specs += [row_spec] * 5
        out_shape += [jax.ShapeDtypeStruct((rows, width), d) for d in (F32, F32, F32, BF16, BF16)]
    else:
        in_specs += [row_spec] * 5
        out_specs += [runs_spec, row_spec, pl.BlockSpec((8, width), whole)] + [pl.BlockSpec((width, channels), whole)] * sets
        out_shape += [jax.ShapeDtypeStruct(runs_shape, BF16), jax.ShapeDtypeStruct((rows, width), BF16)]
        out_shape += [jax.ShapeDtypeStruct((8, width), F32)] + [jax.ShapeDtypeStruct((width, channels), BF16)] * sets
        scratch += [pltpu.VMEM((width, sets * channels), F32)]
    scratch += [pltpu.VMEM((width // 128, tall, 128), F32)]
    in_specs += [pl.BlockSpec((1, width), whole), pl.BlockSpec(memory_space=pltpu.SMEM)]
    in_specs += [pl.BlockSpec((shards, both, width), lambda block: (0, 0, 0))] * len(pieces)
    return pl.pallas_call(
        functools.partial(dense_kernel, stage, sets, len(pieces)),
        grid=(rows // tall,),
        in_specs=in_specs,
        out_specs=out_specs,
        out_shape=out_shape,
        scratch_shapes=scratch,
        compiler_params=pltpu.CompilerParams(vmem_limit_bytes=VMEM_BYTES, dimension_semantics=("arbitrary",)),
        cost_estimate=pl.CostEstimate(flops=12 * rows * width * hidden, bytes_accessed=rows * width * 24, transcendentals=rows * hidden),
        name="dense_first" if stage == 0 else "dense_second",
    )(*states, *entering, gain, scalars, *pieces)


def mixer_back_kernel(sets, mixed_ref, normed_ref, lengths, scalars, *refs):
    per_set = [refs[index * 6 : index * 6 + 6] for index in range(sets)]
    refs = refs[6 * sets :]
    carried_out, refs = refs[:sets], refs[sets:]
    first_out, second_out, refs = refs[:2], refs[2:4], refs[4:]
    bias_out, ends_out, *refs = refs
    cs, ps, state_delta, admits, deltas, slopes_acc, last, enter = refs
    phase, block = pl.program_id(0), pl.program_id(1)
    blocks = pl.num_programs(1)
    channels = per_set[0][1].shape[1]
    place = jnp.where(phase == 0, blocks - 1 - block, block)
    start = pl.multiple_of(place * BLOCK, BLOCK)

    @pl.when((phase == 0) & (block == 0))
    def _():
        last[:, 0:8, :] = jnp.zeros((sets, 8, channels), F32)
        last[:, 8:16, :] = jnp.ones((sets, 8, channels), F32)

    @pl.when(phase == 0)
    def _():
        def arrive(index):
            state_delta[index] = dot_nt(mixed_ref[...], per_set[index][0][...])

        arrive(0)
        for index in range(sets):
            admit_ref = per_set[index][1]
            for lane in range(0, channels, 128):
                if lane == 0 and index + 1 < sets:
                    arrive(index + 1)
                cols = slice(lane, lane + 128)
                kept, gain = last[index, 0:8, cols], last[index, 8:16, cols]
                for here in range(BLOCK - 16, -1, -16):
                    admit = admit_ref[here : here + 16, cols]
                    admits[index, pl.ds(start + here, 16), cols] = admit
                    keep = 1.0 - admit.astype(F32)
                    for step in (8, 0):
                        carried = state_delta[index, here + step : here + step + 8, cols] + kept
                        cs[index, pl.ds(start + here + step, 8), cols] = carried
                        ps[index, pl.ds(start + here + step, 8), cols] = gain
                        kept = keep[step : step + 8] * carried
                        gain = keep[step : step + 8] * gain
                last[index, 0:8, cols] = kept
                last[index, 8:16, cols] = gain

    @pl.when((phase == 1) & (block == 0))
    def _():
        masks = [goes_on(lengths, scalars, run, cs.shape[1] // SEGMENTS) for run in range(SEGMENTS)]
        for index in range(sets):
            kept, gain = last[index, 0:8, :], last[index, 8:16, :]
            entering = per_set[index][4][...]
            enter[index, 7:8, :] = entering
            for run in range(SEGMENTS - 1, 0, -1):
                entering = masks[run] * (kept[run : run + 1] + gain[run : run + 1] * entering)
                enter[index, run - 1 : run, :] = entering
            ends_out[index, 0:1, :] = masks[0] * (kept[0:1] + gain[0:1] * entering)
            ends_out[index, 1:2, :] = product_of_runs(gain, masks)
            ends_out[index, 2:8, :] = jnp.zeros((6, channels), F32)
        bias_out[...] = jnp.zeros_like(bias_out)
        slopes_acc[...] = jnp.zeros_like(slopes_acc)

    @pl.when(phase == 1)
    def _():
        normed_t = normed_ref[...].T
        wide = min(channels, 256)
        chunks = [(index, first) for index in range(sets) for first in range(0, channels, wide)]

        def move(index, lane, here):
            _, _, forget_fac, admit_fac, _, _ = per_set[index]
            cols = slice(lane, lane + 128)
            rows, there = slice(here, here + GROUP), pl.ds(start + here, GROUP)
            gains = ps[index, there, cols].reshape(GROUP // 8, 8, 128)
            carried = (cs[index, there, cols].reshape(GROUP // 8, 8, 128) + gains * enter[index, :, cols]).reshape(GROUP, 128)
            carried_out[index][rows, cols] = carried.astype(BF16)
            admit_delta = (carried * admit_fac[rows, cols].astype(F32)).astype(BF16)
            deltas[index, 0, rows, cols] = (carried * forget_fac[rows, cols].astype(F32)).astype(BF16)
            deltas[index, 1, rows, cols] = admit_delta
            deltas[index, 2, rows, cols] = (carried * admits[index, there, cols].astype(F32)).astype(BF16)
            return fold_rows(admit_delta.astype(F32))

        def reduce(index, first, kind):
            cols = slice(first, first + wide)
            slopes_acc[index, kind, :, cols] += dot_nn(normed_t, deltas[index, kind, :, cols])

        behind = []
        for index, first in chunks:
            lanes = range(first, first + wide, 128)
            biases = [jnp.zeros((8, 128), F32) for _ in lanes]
            units = [(here, which) for here in range(0, BLOCK, GROUP) for which in range(len(lanes))]
            for position, (here, which) in enumerate(units):
                if behind and position % max(1, len(units) // 3) == 0:
                    reduce(*behind.pop(0))
                biases[which] = biases[which] + move(index, lanes[which], here)
            for lane, bias in zip(lanes, biases):
                bias_out[index, :, lane : lane + 128] += bias
            for item in behind:
                reduce(*item)
            behind = [(index, first, kind) for kind in range(3)]
        for item in behind:
            reduce(*item)
        for index in range(sets):
            output_grads = per_set[index][5]
            tall = output_grads.shape[0]
            for half in range(2):

                @pl.when(block // (blocks // 2) == half)
                def _():
                    there = pl.multiple_of(block % (blocks // 2) * tall, tall)
                    second_out[half][index, pl.ds(there, tall), channels:] = output_grads[...]

    @pl.when((phase == 1) & (block == blocks - 1))
    def _():
        for index in range(sets):
            put_blocks(slopes_acc.at[index, 0], [out.at[index] for out in first_out], scalars[1], 0)
            put_blocks(slopes_acc.at[index, 1], [out.at[index] for out in first_out], scalars[1], channels)
            put_blocks(slopes_acc.at[index, 2], [out.at[index] for out in second_out], scalars[2], 0)


def mixer_backward(mixed, normed, lengths, scalars, per_set):
    rows, width = mixed.shape
    sets = len(per_set)
    channels = per_set[0][1].shape[1]
    blocks = rows // BLOCK
    back = lambda phase, block: (jnp.where(phase == 0, blocks - 1 - block, 0), 0)
    late = lambda phase, block: (jnp.where(phase == 0, 0, block), 0)
    whole = lambda phase, block: (0, 0)
    all3 = lambda phase, block: (0, 0, 0)
    set_specs = [
        pl.BlockSpec((channels, width), whole),
        pl.BlockSpec((BLOCK, channels), back),
        pl.BlockSpec((BLOCK, channels), late),
        pl.BlockSpec((BLOCK, channels), late),
        pl.BlockSpec((1, channels), whole),
        pl.BlockSpec((width // blocks, channels), late),
    ]
    results = pl.pallas_call(
        functools.partial(mixer_back_kernel, sets),
        grid=(2, blocks),
        in_specs=[
            pl.BlockSpec((BLOCK, width), back),
            pl.BlockSpec((BLOCK, width), late),
            pl.BlockSpec(memory_space=pltpu.SMEM),
            pl.BlockSpec(memory_space=pltpu.SMEM),
        ]
        + set_specs * sets,
        out_specs=[pl.BlockSpec((BLOCK, channels), late)] * sets
        + [pl.BlockSpec((sets, width // 2, 2 * channels), all3)] * 4
        + [pl.BlockSpec((sets, 8, channels), all3)] * 2,
        out_shape=[jax.ShapeDtypeStruct((rows, channels), BF16)] * sets
        + [jax.ShapeDtypeStruct((sets, width // 2, 2 * channels), BF16)] * 4
        + [jax.ShapeDtypeStruct((sets, 8, channels), F32)] * 2,
        scratch_shapes=[
            pltpu.VMEM((sets, rows, channels), F32),
            pltpu.VMEM((sets, rows, channels), F32),
            pltpu.VMEM((sets, BLOCK, channels), F32),
            pltpu.VMEM((sets, rows, channels), BF16),
            pltpu.VMEM((sets, 3, BLOCK, channels), BF16),
            pltpu.VMEM((sets, 3, width, channels), F32),
            pltpu.VMEM((sets, 16, channels), F32),
            pltpu.VMEM((sets, 8, channels), F32),
        ],
        compiler_params=pltpu.CompilerParams(vmem_limit_bytes=VMEM_BYTES, dimension_semantics=("arbitrary", "arbitrary")),
        cost_estimate=pl.CostEstimate(flops=2 * rows * width * 4 * channels * sets, bytes_accessed=rows * channels * 12 * sets, transcendentals=0),
        name="mixer_backward",
    )(mixed, normed, lengths, scalars, *[item for one in per_set for item in one])
    return results[:sets], results[sets : sets + 2], results[sets + 2 : sets + 4], *results[sets + 4 :]


def input_kernel(sets, *refs):
    x_ref, mixed_ref, gain_ref, *refs = refs
    factors, refs = refs[: 4 * sets], refs[4 * sets :]
    weights, refs = refs[: 3 * sets], refs[3 * sets :]
    out_ref, slope_ref, out_s = refs

    @pl.when(pl.program_id(0) == 0)
    def _():
        slope_ref[...] = jnp.zeros_like(slope_ref)

    normed_delta = None
    for index in range(sets):
        carried = factors[4 * index][...].astype(F32)
        for part in range(3):
            delta = (carried * factors[4 * index + 1 + part][...].astype(F32)).astype(BF16)
            term = dot_nt(delta, weights[3 * index + part][...])
            normed_delta = term if normed_delta is None else normed_delta + term
    rows = x_ref[...].astype(F32)
    scale = row_scale(rows)
    slope_ref[...] += fold_rows(normed_delta * rows * scale)
    scaled = normed_delta * gain_ref[...]
    inner = jnp.mean(scaled * rows, -1, keepdims=True)
    result = mixed_ref[...].astype(F32) + scale * (scaled - rows * (scale * scale * inner))
    separate(result, out_s, out_ref)


def input_backward(x_rows, mixed, gain, factors, weights):
    rows, width = x_rows.shape
    sets = len(factors) // 4
    channels = weights[0].shape[1]
    by_rows = lambda block: (block, 0)
    whole = lambda block: (0, 0)
    return pl.pallas_call(
        functools.partial(input_kernel, sets),
        grid=(rows // BLOCK,),
        in_specs=[pl.BlockSpec((BLOCK, width), by_rows)] * 2
        + [pl.BlockSpec((1, width), whole)]
        + [pl.BlockSpec((BLOCK, channels), by_rows)] * (4 * sets)
        + [pl.BlockSpec((width, channels), whole)] * (3 * sets),
        out_specs=[pl.BlockSpec((SEGMENTS, STEPS, width), lambda block: (0, block, 0)), pl.BlockSpec((8, width), whole)],
        out_shape=[jax.ShapeDtypeStruct((SEGMENTS, rows // SEGMENTS, width), F32), jax.ShapeDtypeStruct((8, width), F32)],
        scratch_shapes=[pltpu.VMEM((width // 128, BLOCK, 128), F32)],
        compiler_params=pltpu.CompilerParams(vmem_limit_bytes=VMEM_BYTES, dimension_semantics=("arbitrary",)),
        cost_estimate=pl.CostEstimate(flops=2 * rows * width * 3 * channels * sets, bytes_accessed=rows * channels * 8 * sets, transcendentals=0),
        name="input_backward",
    )(x_rows, mixed, gain, *factors, *weights)


def finish_kernel(channels, count, *refs):
    first_refs, second_refs = refs[:count], refs[count : 2 * count]
    scalars, forget_out, admit_out, value_out, output_out, scratch = refs[2 * count :]
    tall = scratch.shape[0] // PLACES
    each = PLACES // count
    for place in range(PLACES):
        here = slice(place % each * tall, (place % each + 1) * tall)
        for index, (sums, outs) in enumerate(((first_refs, (forget_out, admit_out)), (second_refs, (value_out, scratch)))):
            there = pl.multiple_of((place ^ scalars[1 + index]) * tall, tall)
            piece = sums[place // each]
            outs[0][pl.ds(there, tall), :] = piece[here, :channels].astype(F32)
            outs[1][pl.ds(there, tall), :] = piece[here, channels:].astype(F32)
    output_out[...] = scratch[...].T


def finish_slopes(first, second, scalars):
    count = len(first)
    width, channels = count * first[0].shape[0], first[0].shape[1] // 2
    return pl.pallas_call(
        functools.partial(finish_kernel, channels, count),
        in_specs=[pl.BlockSpec(memory_space=pltpu.VMEM)] * (2 * count) + [pl.BlockSpec(memory_space=pltpu.SMEM)],
        out_shape=[jax.ShapeDtypeStruct((width, channels), F32)] * 3 + [jax.ShapeDtypeStruct((channels, width), F32)],
        scratch_shapes=[pltpu.VMEM((width, channels), F32)],
        compiler_params=pltpu.CompilerParams(vmem_limit_bytes=VMEM_BYTES),
        name="finish_slopes",
    )(*first, *second, scalars)


def regroup(stacked, half):
    count, both, width = stacked.shape
    if both == 2 * half:
        return stacked
    arrays = jnp.moveaxis(stacked.reshape(count, 2, both // 2, width), 1, 0).reshape(2, -1, half, width)
    return jnp.moveaxis(arrays, 0, 1).reshape(-1, 2 * half, width)


def after(values, *earlier):
    return lax.optimization_barrier((values, earlier))[0]


def total(terms):
    result = terms[0].astype(F32)
    for term in terms[1:]:
        result = result + term.astype(F32)
    return result.astype(terms[0].dtype)


def hold(terms, *earlier):
    return terms[:-1] + [after(terms[-1], *earlier)]


def part(terms, index, axis):
    half = terms[0].shape[axis] // 2
    return [lax.slice_in_dim(t, index * half, (index + 1) * half, axis=axis) for t in terms]


class Links:
    TENSOR, CORE, NEAR, Z_NEAR, Z_FAR = 1, 2, 4, 8, 16

    def __init__(self):
        dp = lax.axis_index("dp")
        core, near, z_near, z_far = dp % 2, dp // 2 % 2, dp // 4 % 2, dp // 8
        self.core = core
        self.me = [core * 8 + z_near * 4 + near * 2 + z_far, core * 8 + near * 4 + z_near * 2 + z_far]

    def swap(self, values, bits):
        pairs = [(device, device ^ bits) for device in range(32)]
        return lax.ppermute(values, ("dp", "tensor"), pairs)

    def begin_weights(self, own_weights):
        half = own_weights[0].shape[0] // 2
        mine = jnp.stack([lax.dynamic_slice_in_dim(w, self.core * half, half) for w in own_weights])
        return mine, self.swap(mine, self.TENSOR)

    def end_weights(self, got):
        rest = self.swap(got, self.CORE)
        lower = self.core == 0
        whole = jnp.concatenate([jnp.where(lower, got, rest), jnp.where(lower, rest, got)], 1)
        return [whole[index] for index in range(4)]

    def begin_dense(self, shard):
        return [shard] + [self.swap(shard, bits) for bits in (self.Z_NEAR, self.Z_FAR, self.Z_NEAR | self.Z_FAR)]

    def dense_pieces(self, pieces):
        own = jnp.stack(pieces)
        near = self.swap(own, self.NEAR)
        other = self.swap(own, self.TENSOR)
        return own, near, other, self.swap(own, self.CORE)

    def dense_grads_cut(self, values):
        return values.reshape(2, 2, 4, *values.shape[2:])

    def dense_across(self, own_terms, other_terms):
        own = [self.dense_grads_cut(t) for t in own_terms]
        other = [self.dense_grads_cut(t) for t in other_terms]
        pick = lambda terms, index: total([t[:, index] for t in terms])
        sends = [(pick(other, 0), self.TENSOR), (pick(own, 1), self.NEAR), (pick(other, 1), self.TENSOR | self.NEAR)]
        return sends, [t[:, 0] for t in own]

    def dense_along(self, terms):
        sends = []
        for index, bits in ((1, self.Z_NEAR), (2, self.Z_FAR), (3, self.Z_NEAR | self.Z_FAR)):
            sends.append((total([t[:, index] for t in terms]), bits))
        return sends, [t[:, 0] for t in terms]

    def exchange(self, sends, kept):
        return kept + [self.swap(values, bits) for values, bits in sends]

    def halve(self, terms, bits, extra=None):
        axis = 0 if bits == self.TENSOR else 1
        send = total(part(terms, 1, axis))
        if extra is not None:
            send = jnp.concatenate([send, extra], 1)
        return [(send, bits)], part(terms, 0, axis)

    def grow(self, values, bits):
        return jnp.concatenate([values, self.swap(values, bits)], 1)


class Plain:
    def __init__(self, n_tensor, own):
        self.n_tensor, self.own = n_tensor, own
        self.me = [0, 0]

    def weights(self, own_weights):
        whole = [lax.all_gather(w, "tensor", axis=1, tiled=True) for w in own_weights[:3]]
        pairs = [jnp.split(w, 2, 1) for w in whole]
        pairs.append(jnp.split(lax.all_gather(own_weights[3], "tensor", axis=0, tiled=True), 2, 0))
        return [p[0] for p in pairs], [p[1] for p in pairs]

    def bias(self, own_bias):
        return tuple(jnp.split(lax.all_gather(own_bias, "tensor", axis=0, tiled=True), 2))

    def dense(self, shard):
        whole = regroup(lax.all_gather(shard, ("dp", "tensor"), axis=0), 64)
        pieces = [whole[first : first + 4] for first in range(0, whole.shape[0], 4)]
        return pieces[: len(pieces) // 2], pieces[len(pieces) // 2 :]

    def dense_sums(self, grads):
        whole = jnp.concatenate(grads, 1)
        whole = whole.reshape(2, -1, whole.shape[-1])
        return [lax.psum_scatter(w, ("dp", "tensor"), scatter_dimension=0, tiled=True) for w in whole]

    def mixer_sums(self, grads):
        grads = jnp.concatenate(grads, 1)
        _, width, columns = grads.shape
        whole = jnp.moveaxis(grads.reshape(2, width, 2, columns // 2), 0, 2).reshape(width, 2, columns)
        part = lax.psum_scatter(whole, "tensor", scatter_dimension=2, tiled=True)
        return jnp.split(lax.psum(part, "dp").reshape(width, 2 * self.own), 2, 0)

def on_device(
    block_in,
    out_cotangent,
    seq_lengths,
    premix_gain,
    forget_weight,
    admit_weight,
    value_weight,
    admit_bias,
    output_weight,
    dense_gain,
    upper_weight,
    lower_weight,
):
    n_dp, n_tensor = lax.axis_size("dp"), lax.axis_size("tensor")
    rows, width = block_in.shape
    place = lax.axis_index("tensor")
    own = forget_weight.shape[1]
    premix = premix_gain.astype(F32)[None]
    dense = dense_gain.astype(F32)[None]
    paired = (n_dp, n_tensor) == (16, 2)
    links = Links() if paired else Plain(n_tensor, own)
    scalars = jnp.stack([place * rows] + links.me).astype(jnp.int32)
    own_weights = [forget_weight, admit_weight, value_weight, output_weight]
    dense_shard = jnp.concatenate([upper_weight.T, lower_weight], 0)
    if paired:
        weights, biases = [own_weights], [admit_bias]
        channels = own
        mine, got = links.begin_weights(own_weights)
        pieces = links.begin_dense(after(dense_shard, mine))
        biases.append(links.swap(after(admit_bias, pieces[0]), Links.TENSOR))
    else:
        weights, biases = links.weights(own_weights), links.bias(admit_bias)
        channels = weights[0][0].shape[1]
    crossing = rows % LONGEST != 0
    nothing = jnp.zeros((1, channels), F32)

    def chained(ends, backwards):
        every = lax.all_gather(ends, "tensor", axis=0)
        entering = jnp.zeros_like(ends[0:1])
        mine = entering
        order = range(n_tensor - 1, -1, -1) if backwards else range(n_tensor)
        for index in order:
            mine = jnp.where(place == index, entering, mine)
            entering = every[index, 0:1] + every[index, 1:2] * entering
        return mine

    def forward(first, rows_in, index):
        carry = nothing
        args = (first, rows_in, premix, weights[index][:3], biases[index].astype(F32)[None], seq_lengths, scalars)
        if crossing:
            carry = chained(mixer_forward(*args, carry)[-1], False)
        return mixer_forward(*args, carry)

    x_rows, normed, *kept_0 = forward(True, block_in, 0)
    if paired:
        got, pieces, biases[1] = after((got, pieces, biases[1]), normed)
        own_four, near_four, other_four, own_rest = links.dense_pieces(pieces)
        weights.append(links.end_weights(got))
    kept_1 = forward(False, normed, 1)
    kept = [kept_0, kept_1]
    if paired:
        near_four, other_four = after((near_four, other_four), kept_1[1])
        far_four = links.swap(other_four, Links.NEAR)
        other_rest = links.swap(other_four, Links.CORE)
        pieces_0 = [own_four, near_four, own_rest, links.swap(near_four, Links.CORE)]
    else:
        pieces_0, pieces_1 = links.dense(dense_shard)
    outputs = [w[3] for w in weights]
    states = [k[1] for k in kept]
    own_keep, own_send, *rows_0 = dense_both(0, states, (x_rows, out_cotangent), outputs, dense, scalars, pieces_0)
    if paired:
        far_four, other_rest = after((far_four, other_rest), rows_0[0])
        pieces_1 = [other_four, far_four, other_rest, links.swap(far_four, Links.CORE)]
        own_terms = [own_keep, links.swap(own_send, Links.CORE)]
    other_keep, other_send, block_out, mixed, dense_part, *output_grads = dense_both(1, states, rows_0, None, dense, scalars, pieces_1)
    back_mixed = mixed
    if paired:
        other_terms = [other_keep, links.swap(other_send, Links.CORE)]
        dense_sends, dense_kept = links.dense_across(own_terms, other_terms)
        back_mixed = after(mixed, [values for values, _ in dense_sends])
        dense_terms = links.exchange(dense_sends, dense_kept)

    carries = [nothing, nothing]
    for _ in range(2 if crossing else 1):
        per_set = [
            (outputs[index], kept[index][0], kept[index][2], kept[index][3], carries[index], output_grads[index])
            for index in range(2)
        ]
        carried, first, second, bias_parts, ends = mixer_backward(back_mixed, normed, seq_lengths, scalars, per_set)
        if crossing:
            carries = [chained(ends[index], True) for index in range(2)]
    factors = [f for index in range(2) for f in (carried[index], kept[index][2], kept[index][3], kept[index][0])]
    if paired:
        dense_terms = hold(dense_terms, carried[0])
        along, along_kept = links.dense_along(dense_terms)
        core_sends = after([first[1], second[1]], dense_terms[-3:])
        first = [first[0], links.swap(core_sends[0], Links.CORE)]
        second = [second[0], links.swap(core_sends[1], Links.CORE)]
        first, second = links.halve(first, Links.TENSOR), links.halve(second, Links.NEAR)
        factors[0] = after(factors[0], first[0][0][0], second[0][0][0], [values for values, _ in along])
        first, second = links.exchange(*first), links.exchange(*second)
        dense_terms = links.exchange(along, along_kept)
    input_slope, premix_part = input_backward(x_rows, mixed, premix, factors, weights[0][:3] + weights[1][:3])

    bias_parts = jnp.sum(bias_parts, 1)
    if paired:
        bias_parts = jnp.where(place == 0, bias_parts, bias_parts[::-1])
    small = jnp.concatenate([jnp.sum(premix_part, 0), jnp.sum(dense_part, 0), bias_parts[0], bias_parts[1]], 0)
    if paired:
        small = small.reshape(1, -1, 2 * channels).astype(BF16)
        filled = small.shape[1]
        small = jnp.pad(small, ((0, 0), (0, 16 - filled), (0, 0)))
        first, second = hold(first, input_slope), hold(second, input_slope)
        dense_terms = dense_terms[:-3] + after(dense_terms[-3:], input_slope)
        small = after(small, first[-1], second[-1], dense_terms[-3:])
        small = total([small, links.swap(small, Links.CORE)])

        def halve_both(first, second, first_bits, second_bits, extra):
            first = links.halve(first, first_bits)
            second = links.halve(second, second_bits, extra)
            second_send = second[0][0][0]
            first, second = links.exchange(*first), links.exchange(*second)
            rows_sent = second_send.shape[1] - extra.shape[1]
            extra = total([extra, second[-1][:, rows_sent:]])
            return first, second[:-1] + [second[-1][:, :rows_sent]], extra

        first, second, small = halve_both(first, second, Links.Z_NEAR, Links.TENSOR, small)
        first, second, small = halve_both(first, second, Links.NEAR, Links.Z_NEAR, small)
        first, second, small = halve_both(first, second, Links.Z_FAR, Links.Z_FAR, small)
        first, second = total(first), total(second)
        first, second = links.grow(first, Links.Z_FAR), links.grow(second, Links.Z_FAR)
        count = first.shape[1]
        got = links.swap(jnp.concatenate([first, small], 1), Links.NEAR)
        first, small = jnp.concatenate([first, got[:, :count]], 1), total([small, got[:, count:]])
        second = links.grow(second, Links.Z_NEAR)
        first, second = [first, links.swap(first, Links.Z_NEAR)], [second, links.swap(second, Links.NEAR)]
        first += [links.swap(f, Links.CORE) for f in first]
        second += [links.swap(f, Links.CORE) for f in second]
        first, second = [f[0] for f in first], [f[0] for f in second]
        small = small[0, :filled].reshape(-1).astype(F32)
        upper_sum, lower_sum = total(dense_terms)
    else:
        small = lax.psum(small, ("dp", "tensor"))
        upper_sum, lower_sum = links.dense_sums([own_keep, own_send, other_keep, other_send])
        first, second = links.mixer_sums(first), links.mixer_sums(second)
    upper_slope, lower_slope = upper_sum.astype(F32).T, lower_sum.astype(F32)
    forget_slope, admit_slope, value_slope, output_slope = finish_slopes(first, second, scalars)
    shard = width // (n_dp * n_tensor)
    at = (lax.axis_index("dp") * n_tensor + place) * shard
    premix_slope = lax.dynamic_slice(small, (at,), (shard,))
    dense_slope = lax.dynamic_slice(small, (width + at,), (shard,))
    bias_slope = lax.dynamic_slice(small, (2 * width + place * own,), (own,))
    return (
        block_out.reshape(rows, width),
        input_slope.reshape(rows, width),
        premix_slope,
        forget_slope,
        admit_slope,
        value_slope,
        bias_slope,
        output_slope,
        dense_slope,
        upper_slope,
        lower_slope,
    )


def solution(mesh):
    placed = (
        P(("dp", "tensor"), None),
        P(("dp", "tensor"), None),
        P("dp", None),
        P(),
        P(None, "tensor"),
        P(None, "tensor"),
        P(None, "tensor"),
        P("tensor"),
        P("tensor", None),
        P(),
        P(None, ("dp", "tensor")),
        P(("dp", "tensor"), None),
    )
    return jax.shard_map(
        on_device,
        mesh=mesh,
        in_specs=placed,
        out_specs=(
            P(("dp", "tensor"), None),
            P(("dp", "tensor"), None),
            P(("dp", "tensor")),
            P(None, "tensor"),
            P(None, "tensor"),
            P(None, "tensor"),
            P("tensor"),
            P("tensor", None),
            P(("dp", "tensor")),
            P(None, ("dp", "tensor")),
            P(("dp", "tensor"), None),
        ),
        check_vma=False,
    )
```

```python
import functools

import jax
import jax.numpy as jnp
from jax import lax
from jax.experimental import pallas as pl
from jax.experimental.pallas import tpu as pltpu
from jax.sharding import PartitionSpec as P

EPSILON = 1e-06
LONGEST = 2048
SEGMENTS = 8
PLACES = 16
STEPS = 64
BLOCK = SEGMENTS * STEPS
GROUP = 32
GELU_SLOPE = 0.7978845608028654
GELU_CUBE = 0.044715
VMEM_BYTES = 56 * 1024 * 1024
F32 = jnp.float32
BF16 = jnp.bfloat16


def in_hbm(values):
    return pltpu.with_memory_space_constraint(values, pltpu.HBM)


def hbm(shape, dtype):
    return pltpu.HBM(shape, dtype)


def dot_nn(left, right):
    return lax.dot_general(left, right, (((1,), (0,)), ((), ())), preferred_element_type=F32)


def dot_nt(left, right):
    return lax.dot_general(left, right, (((1,), (1,)), ((), ())), preferred_element_type=F32)


def row_scale(rows):
    return lax.rsqrt(jnp.mean(rows * rows, -1, keepdims=True) + EPSILON)


def fold_rows(values):
    return jnp.sum(values.reshape(-1, 8, values.shape[-1]), 0)


def put_blocks(values, halves, me, first):
    tall = values.shape[0] // PLACES
    for place in range(PLACES):
        block = pl.multiple_of((place ^ me) * tall, tall)
        there = (place % (PLACES // 2)) * tall
        out = halves[place // (PLACES // 2)]
        out[there : there + tall, first : first + values.shape[1]] = values[pl.ds(block, tall), :].astype(out.dtype)


def interleave(block, scratch):
    lanes = scratch.shape[0]
    for lane in range(lanes):
        for run in range(SEGMENTS):
            part = block[run, :, lane * 128 : (lane + 1) * 128]
            scratch[lane, pl.ds(run, block.shape[1], stride=SEGMENTS), :] = part.astype(F32)
    return jnp.concatenate([scratch[lane] for lane in range(lanes)], -1)


def separate(values, scratch, out):
    lanes = scratch.shape[0]
    for lane in range(lanes):
        scratch[lane] = values[:, lane * 128 : (lane + 1) * 128]
    for run in range(SEGMENTS):
        parts = [scratch[lane, pl.ds(run, out.shape[1], stride=SEGMENTS), :] for lane in range(lanes)]
        out[run] = jnp.concatenate(parts, -1).astype(out.dtype)


def gates(forget_logit, admit_logit):
    top = jnp.maximum(jnp.maximum(-admit_logit, -forget_logit), 0.0)
    one = jnp.exp(-top)
    admit_exp = jnp.exp(-admit_logit - top)
    forget_exp = jnp.exp(-forget_logit - top)
    keep_part = one + admit_exp
    admit_part = one + forget_exp
    total = keep_part + admit_part
    inverse = pl.reciprocal(total, approx=True)
    inverse = inverse * (2.0 - total * inverse)
    keep = keep_part * inverse
    admit = admit_part * inverse
    return keep, admit, keep * (forget_exp * inverse), -admit * (admit_exp * inverse)


def goes_on(lengths_ref, scalars_ref, run, tall):
    place = scalars_ref[0] + run * tall
    begin = jnp.int32(0)
    fresh = False
    for entry in range(lengths_ref.shape[1]):
        length = lengths_ref[0, entry]
        fresh = fresh | ((begin == place) & (length > 0))
        begin = begin + length
    return jnp.where(fresh, 0.0, 1.0).astype(F32)


def product_of_runs(values, masks):
    result = masks[0] * values[0:1]
    for run in range(1, SEGMENTS):
        result = result * (masks[run] * values[run : run + 1])
    return result


def mixer_kernel(first, *refs):
    if first:
        x_ref, gain_ref, *refs = refs
    else:
        normed_in, *refs = refs
    wf, wa, wv, bias, lengths, scalars, carry, *refs = refs
    if first:
        x_out, normed_out, *refs = refs
    admit_out, state_out, forget_fac, admit_fac, ends_out, *refs = refs
    logits, hs, ps, vs, fs, as_, enter, *refs = refs
    phase, block = pl.program_id(0), pl.program_id(1)
    channels = wf.shape[1]
    start = pl.multiple_of(block * BLOCK, BLOCK)

    @pl.when((phase == 0) & (block == 0))
    def _():
        hs[0:8, :] = jnp.zeros((8, channels), F32)
        ps[0:8, :] = jnp.ones((8, channels), F32)

    @pl.when(phase == 0)
    def _():
        if first:
            rows = interleave(x_ref[...], refs[0])
            x_out[...] = rows.astype(BF16)
            normed = (rows * row_scale(rows) * gain_ref[...]).astype(BF16)
            normed_out[...] = normed
        else:
            normed = normed_in[...]
        wide = min(channels, 256)
        chunks = channels // wide
        weights = (wf, wa, wv)

        def project(chunk, kind):
            logits[chunk, kind] = dot_nn(normed, weights[kind][:, chunk * wide : (chunk + 1) * wide])

        def gate(chunk, lane, here, chain):
            inner, cols = slice(lane, lane + 128), slice(chunk * wide + lane, chunk * wide + lane + 128)
            rows = slice(here, here + GROUP)
            there = pl.ds(start + here, GROUP)
            value = logits[chunk, 2, rows, inner]
            keep, admit, forget_side, admit_side = gates(
                logits[chunk, 0, rows, inner], logits[chunk, 1, rows, inner] + bias[:, cols]
            )
            admit_out[rows, cols] = admit.astype(BF16)
            vs[there, cols] = value
            fs[there, cols] = forget_side
            as_[there, cols] = admit_side
            inflow = admit * value
            state, gain = chain
            for step in range(0, GROUP, 8):
                state = keep[step : step + 8] * state + inflow[step : step + 8]
                gain = gain * keep[step : step + 8]
                hs[pl.ds(start + here + step + 8, 8), cols] = state
                ps[pl.ds(start + here + step + 8, 8), cols] = gain
            return state, gain

        for kind in range(3):
            project(0, kind)
        for chunk in range(chunks):
            firsts = range(chunk * wide, (chunk + 1) * wide, 128)
            chains = [(hs[pl.ds(start, 8), c : c + 128], ps[pl.ds(start, 8), c : c + 128]) for c in firsts]
            units = [(here, lane) for here in range(0, BLOCK, GROUP) for lane in range(len(chains))]
            ahead = [(chunk + 1, kind) for kind in range(3)] if chunk + 1 < chunks else []
            for index, (here, lane) in enumerate(units):
                if ahead and index % max(1, len(units) // 3) == 0:
                    project(*ahead.pop(0))
                chains[lane] = gate(chunk, lane * 128, here, chains[lane])
            for item in ahead:
                project(*item)

    @pl.when((phase == 1) & (block == 0))
    def _():
        total = hs.shape[0]
        ends, gains = hs[total - 8 : total, :], ps[total - 8 : total, :]
        masks = [goes_on(lengths, scalars, run, (total - 8) // SEGMENTS) for run in range(SEGMENTS)]
        entering = masks[0] * carry[...]
        enter[0:1] = entering
        for run in range(1, SEGMENTS):
            entering = masks[run] * (ends[run - 1 : run] + gains[run - 1 : run] * entering)
            enter[run : run + 1] = entering
        ends_out[0:1, :] = ends[7:8] + gains[7:8] * enter[7:8, :]
        ends_out[1:2, :] = product_of_runs(gains, masks)
        ends_out[2:8, :] = jnp.zeros((6, channels), F32)

    @pl.when(phase == 1)
    def _():
        def some_rows(group, _):
            here = pl.multiple_of(group * 64, 64)
            there = pl.multiple_of(start + here, 64)
            for lane in range(0, channels, 128):
                cols = pl.ds(lane, 128)
                entering = enter[:, lane : lane + 128]
                states = hs[pl.ds(there, 72), cols].reshape(9, 8, 128) + ps[pl.ds(there, 72), cols].reshape(9, 8, 128) * entering
                states = states.reshape(72, 128)
                state_out[pl.ds(here, 64), cols] = states[8:].astype(BF16)
                change = states[:64] - vs[pl.ds(there, 64), cols]
                forget_fac[pl.ds(here, 64), cols] = (change * fs[pl.ds(there, 64), cols]).astype(BF16)
                admit_fac[pl.ds(here, 64), cols] = (change * as_[pl.ds(there, 64), cols]).astype(BF16)
            return 0

        lax.fori_loop(0, BLOCK // 64, some_rows, 0)


def mixer_forward(first, rows_in, gain, weights, bias, lengths, scalars, carry):
    width = rows_in.shape[-1]
    rows = rows_in.size // width
    channels = weights[0].shape[1]
    blocks = rows // BLOCK
    early = lambda phase, block: (jnp.where(phase == 0, block, blocks - 1), 0)
    late = lambda phase, block: (jnp.where(phase == 0, 0, block), 0)
    whole = lambda phase, block: (0, 0)
    if first:
        in_specs = [
            pl.BlockSpec((SEGMENTS, STEPS, width), lambda phase, block: (0, jnp.where(phase == 0, block, blocks - 1), 0)),
            pl.BlockSpec((1, width), whole),
        ]
        operands = [rows_in.reshape(SEGMENTS, rows // SEGMENTS, width), gain]
        out_specs = [pl.BlockSpec((BLOCK, width), early)] * 2
        out_shape = [hbm((rows, width), BF16)] * 2
    else:
        in_specs, operands = [pl.BlockSpec((BLOCK, width), early)], [rows_in]
        out_specs, out_shape = [], []
    in_specs += [pl.BlockSpec((width, channels), whole)] * 3
    in_specs += [pl.BlockSpec((1, channels), whole)] + [pl.BlockSpec(memory_space=pltpu.SMEM)] * 2 + [pl.BlockSpec((1, channels), whole)]
    out_specs += [pl.BlockSpec((BLOCK, channels), early)] + [pl.BlockSpec((BLOCK, channels), late)] * 3
    out_specs += [pl.BlockSpec((8, channels), whole)]
    out_shape += [hbm((rows, channels), BF16)] * 4
    out_shape += [hbm((8, channels), F32)]
    wide = min(channels, 256)
    scratch = [pltpu.VMEM((channels // wide, 3, BLOCK, wide), F32)]
    scratch += [pltpu.VMEM((rows + 8, channels), F32)] * 2
    scratch += [pltpu.VMEM((rows, channels), F32)] * 3
    scratch += [pltpu.VMEM((8, channels), F32)]
    if first:
        scratch += [pltpu.VMEM((width // 128, BLOCK, 128), F32)]
    return pl.pallas_call(
        functools.partial(mixer_kernel, first),
        grid=(2, blocks),
        in_specs=in_specs,
        out_specs=out_specs,
        out_shape=out_shape,
        scratch_shapes=scratch,
        compiler_params=pltpu.CompilerParams(vmem_limit_bytes=36 * 1024 * 1024, dimension_semantics=("arbitrary", "arbitrary")),
        cost_estimate=pl.CostEstimate(flops=2 * rows * width * 3 * channels, bytes_accessed=rows * channels * 16, transcendentals=4 * rows * channels),
        name="mixer_forward",
    )(in_hbm(operands[0]), *operands[1:], *weights, bias, lengths, scalars, carry)


def dense_kernel(stage, sets, pieces, *refs):
    states, refs = refs[:sets], refs[sets:]
    if stage == 0:
        x_ref, c_ref, *refs = refs
        outs_w, refs = refs[:sets], refs[sets:]
    else:
        middle_ref, sum_ref, delta_ref, dense_ref, cotangent_ref, *refs = refs
    gain_ref, scalars, *refs = refs
    pieces_w, refs = refs[:pieces], refs[pieces:]
    keep_out, send_out, *refs = refs
    if stage == 0:
        middle_out, sum_out, delta_out, dense_out, cotangent_out, upper_acc, lower_acc, cotangent_s = refs
    else:
        out_ref, mixed_ref, slope_ref, *refs = refs
        outputs_ref, refs = refs[:sets], refs[sets:]
        upper_acc, lower_acc, output_acc, out_s = refs
    step = pl.program_id(0)
    gain = gain_ref[...]
    shards, both, width = pieces_w[0].shape
    half = both // 2

    @pl.when(step == 0)
    def _():
        upper_acc[...] = jnp.zeros_like(upper_acc)
        lower_acc[...] = jnp.zeros_like(lower_acc)
        if stage == 1:
            output_acc[...] = jnp.zeros_like(output_acc)
            slope_ref[...] = jnp.zeros_like(slope_ref)

    if stage == 0:
        middle = x_ref[...].astype(F32)
        for state, weight in zip(states, outs_w):
            middle = middle + dot_nn(state[...], weight[...])
        middle_out[...] = middle.astype(BF16)
        dense_in = (middle * row_scale(middle) * gain).astype(BF16)
        dense_out[...] = dense_in
        cotangent = interleave(c_ref[...], cotangent_s).astype(BF16)
        cotangent_out[...] = cotangent
    else:
        dense_in, cotangent = dense_ref[...], cotangent_ref[...]
    dense_t, cotangent_t = dense_in.T, cotangent.T
    fed, delta = None, None
    joined = max(1, 512 // (shards * half))
    for chunk in range(0, pieces, joined):
        some = pieces_w[chunk : chunk + joined]
        upper_w = jnp.concatenate([w[:, :half, :].reshape(shards * half, width) for w in some], 0)
        lower_w = jnp.concatenate([w[:, half:, :].reshape(shards * half, width) for w in some], 0)
        cols = slice(chunk * shards * half, (chunk + joined) * shards * half)
        upper = dot_nt(dense_in, upper_w)
        square = upper * upper
        bell = 0.5 + 0.5 * jnp.tanh(upper * (GELU_SLOPE + GELU_SLOPE * GELU_CUBE * square))
        active = upper * bell
        slope = bell + active * (1.0 - bell) * (2.0 * GELU_SLOPE + 6.0 * GELU_SLOPE * GELU_CUBE * square)
        active = active.astype(BF16)
        part = dot_nn(active, lower_w)
        fed = part if fed is None else fed + part
        upper_delta = (slope * dot_nt(cotangent, lower_w)).astype(BF16)
        part = dot_nn(upper_delta, upper_w)
        delta = part if delta is None else delta + part
        lower_acc[:, cols] += dot_nn(cotangent_t, active)
        upper_acc[:, cols] += dot_nn(dense_t, upper_delta)
    if stage == 0:
        sum_out[...] = (middle + fed).astype(BF16)
        delta_out[...] = delta.astype(BF16)
    else:
        separate(sum_ref[...].astype(F32) + fed, out_s, out_ref)
        middle = middle_ref[...].astype(F32)
        scale = row_scale(middle)
        delta = delta_ref[...].astype(F32) + delta
        slope_ref[...] += fold_rows(delta * middle * scale)
        scaled = delta * gain
        inner = jnp.mean(scaled * middle, -1, keepdims=True)
        mixed = (cotangent.astype(F32) + scale * (scaled - middle * (scale * scale * inner))).astype(BF16)
        mixed_ref[...] = mixed
        mixed_t = mixed.T
        channels = states[0].shape[1]
        for index, state in enumerate(states):
            output_acc[:, index * channels : (index + 1) * channels] += dot_nn(mixed_t, state[...])

    @pl.when(step == pl.num_programs(0) - 1)
    def _():
        for shard in range(0, pieces * shards, 2):
            cols = slice(shard * half, (shard + 2) * half)
            out = keep_out if shard < pieces * shards // 2 else send_out
            there = shard % (pieces * shards // 2)
            out[there : there + 2, :half, :] = upper_acc[:, cols].T.astype(BF16).reshape(2, half, width)
            out[there : there + 2, half:, :] = lower_acc[:, cols].T.astype(BF16).reshape(2, half, width)
        if stage == 1:
            tall = output_acc.shape[0] // PLACES
            for index, output in enumerate(outputs_ref):
                for place in range(PLACES):
                    there = pl.multiple_of((place ^ scalars[2]) * tall, tall)
                    output[place * tall : (place + 1) * tall, :] = output_acc[
                        pl.ds(there, tall), index * channels : (index + 1) * channels
                    ].astype(BF16)


def dense_both(stage, states, entering, output_weights, gain, scalars, pieces):
    rows, channels = states[0].shape
    width = gain.shape[1]
    shards, both, _ = pieces[0].shape
    hidden = len(pieces) * shards * both // 2
    sets = len(states)
    tall = min(rows, 512)
    by_rows = lambda block: (block, 0)
    whole = lambda block: (0, 0)
    runs_spec = pl.BlockSpec((SEGMENTS, tall // SEGMENTS, width), lambda block: (0, block, 0))
    runs_shape = (SEGMENTS, rows // SEGMENTS, width)
    row_spec = pl.BlockSpec((tall, width), by_rows)
    grads = (len(pieces) * shards // 2, both, width)
    in_specs = [pl.BlockSpec((tall, channels), by_rows)] * sets
    out_specs = [pl.BlockSpec(grads, lambda block: (0, 0, 0))] * 2
    out_shape = [hbm(grads, BF16)] * 2
    scratch = [pltpu.VMEM((width, hidden), F32)] * 2
    if stage == 0:
        in_specs += [row_spec, runs_spec] + [pl.BlockSpec((channels, width), whole)] * sets
        entering = [entering[0], entering[1].reshape(runs_shape), *output_weights]
        out_specs += [row_spec] * 5
        out_shape += [hbm((rows, width), BF16)] * 5
    else:
        in_specs += [row_spec] * 5
        out_specs += [runs_spec, row_spec, pl.BlockSpec((8, width), whole)] + [pl.BlockSpec((width, channels), whole)] * sets
        out_shape += [hbm(runs_shape, BF16), hbm((rows, width), BF16)]
        out_shape += [hbm((8, width), F32)] + [hbm((width, channels), BF16)] * sets
        scratch += [pltpu.VMEM((width, sets * channels), F32)]
    scratch += [pltpu.VMEM((width // 128, tall, 128), F32)]
    in_specs += [pl.BlockSpec((1, width), whole), pl.BlockSpec(memory_space=pltpu.SMEM)]
    in_specs += [pl.BlockSpec((shards, both, width), lambda block: (0, 0, 0))] * len(pieces)
    return pl.pallas_call(
        functools.partial(dense_kernel, stage, sets, len(pieces)),
        grid=(rows // tall,),
        in_specs=in_specs,
        out_specs=out_specs,
        out_shape=out_shape,
        scratch_shapes=scratch,
        compiler_params=pltpu.CompilerParams(vmem_limit_bytes=44 * 1024 * 1024, dimension_semantics=("arbitrary",)),
        cost_estimate=pl.CostEstimate(flops=12 * rows * width * hidden, bytes_accessed=rows * width * 24, transcendentals=rows * hidden),
        name="dense_first" if stage == 0 else "dense_second",
    )(*[in_hbm(v) for v in states], *[in_hbm(v) if v.shape[0] != channels else v for v in entering], gain, scalars, *pieces)


def mixer_back_kernel(sets, mixed_ref, normed_ref, lengths, scalars, *refs):
    per_set = [refs[index * 6 : index * 6 + 6] for index in range(sets)]
    refs = refs[6 * sets :]
    carried_out, refs = refs[:sets], refs[sets:]
    first_out, second_out, refs = refs[:2], refs[2:4], refs[4:]
    bias_out, ends_out, *refs = refs
    cs, ps, state_delta, admits, deltas, slopes_acc, last, enter = refs
    phase, block = pl.program_id(0), pl.program_id(1)
    blocks = pl.num_programs(1)
    channels = per_set[0][1].shape[1]
    place = jnp.where(phase == 0, blocks - 1 - block, block)
    start = pl.multiple_of(place * BLOCK, BLOCK)

    @pl.when((phase == 0) & (block == 0))
    def _():
        last[:, 0:8, :] = jnp.zeros((sets, 8, channels), F32)
        last[:, 8:16, :] = jnp.ones((sets, 8, channels), F32)

    @pl.when(phase == 0)
    def _():
        def arrive(index):
            state_delta[index] = dot_nt(mixed_ref[...], per_set[index][0][...])

        arrive(0)
        for index in range(sets):
            admit_ref = per_set[index][1]
            for lane in range(0, channels, 128):
                if lane == 0 and index + 1 < sets:
                    arrive(index + 1)
                cols = slice(lane, lane + 128)
                kept, gain = last[index, 0:8, cols], last[index, 8:16, cols]
                for here in range(BLOCK - 16, -1, -16):
                    admit = admit_ref[here : here + 16, cols]
                    admits[index, pl.ds(start + here, 16), cols] = admit
                    keep = 1.0 - admit.astype(F32)
                    for step in (8, 0):
                        carried = state_delta[index, here + step : here + step + 8, cols] + kept
                        cs[index, pl.ds(start + here + step, 8), cols] = carried
                        ps[index, pl.ds(start + here + step, 8), cols] = gain
                        kept = keep[step : step + 8] * carried
                        gain = keep[step : step + 8] * gain
                last[index, 0:8, cols] = kept
                last[index, 8:16, cols] = gain

    @pl.when((phase == 1) & (block == 0))
    def _():
        masks = [goes_on(lengths, scalars, run, cs.shape[1] // SEGMENTS) for run in range(SEGMENTS)]
        for index in range(sets):
            kept, gain = last[index, 0:8, :], last[index, 8:16, :]
            entering = per_set[index][4][...]
            enter[index, 7:8, :] = entering
            for run in range(SEGMENTS - 1, 0, -1):
                entering = masks[run] * (kept[run : run + 1] + gain[run : run + 1] * entering)
                enter[index, run - 1 : run, :] = entering
            ends_out[index, 0:1, :] = masks[0] * (kept[0:1] + gain[0:1] * entering)
            ends_out[index, 1:2, :] = product_of_runs(gain, masks)
            ends_out[index, 2:8, :] = jnp.zeros((6, channels), F32)
        bias_out[...] = jnp.zeros_like(bias_out)
        slopes_acc[...] = jnp.zeros_like(slopes_acc)

    @pl.when(phase == 1)
    def _():
        normed_t = normed_ref[...].T
        wide = min(channels, 256)
        chunks = [(index, first) for index in range(sets) for first in range(0, channels, wide)]

        def move(index, lane, here):
            _, _, forget_fac, admit_fac, _, _ = per_set[index]
            cols = slice(lane, lane + 128)
            rows, there = slice(here, here + GROUP), pl.ds(start + here, GROUP)
            gains = ps[index, there, cols].reshape(GROUP // 8, 8, 128)
            carried = (cs[index, there, cols].reshape(GROUP // 8, 8, 128) + gains * enter[index, :, cols]).reshape(GROUP, 128)
            carried_out[index][rows, cols] = carried.astype(BF16)
            admit_delta = (carried * admit_fac[rows, cols].astype(F32)).astype(BF16)
            deltas[index, 0, rows, cols] = (carried * forget_fac[rows, cols].astype(F32)).astype(BF16)
            deltas[index, 1, rows, cols] = admit_delta
            deltas[index, 2, rows, cols] = (carried * admits[index, there, cols].astype(F32)).astype(BF16)
            return fold_rows(admit_delta.astype(F32))

        def reduce(index, first, kind):
            cols = slice(first, first + wide)
            slopes_acc[index, kind, :, cols] += dot_nn(normed_t, deltas[index, kind, :, cols])

        behind = []
        for index, first in chunks:
            lanes = range(first, first + wide, 128)
            biases = [jnp.zeros((8, 128), F32) for _ in lanes]
            units = [(here, which) for here in range(0, BLOCK, GROUP) for which in range(len(lanes))]
            for position, (here, which) in enumerate(units):
                if behind and position % max(1, len(units) // 3) == 0:
                    reduce(*behind.pop(0))
                biases[which] = biases[which] + move(index, lanes[which], here)
            for lane, bias in zip(lanes, biases):
                bias_out[index, :, lane : lane + 128] += bias
            for item in behind:
                reduce(*item)
            behind = [(index, first, kind) for kind in range(3)]
        for item in behind:
            reduce(*item)
        for index in range(sets):
            output_grads = per_set[index][5]
            tall = output_grads.shape[0]
            for half in range(2):

                @pl.when(block // (blocks // 2) == half)
                def _():
                    there = pl.multiple_of(block % (blocks // 2) * tall, tall)
                    second_out[half][index, pl.ds(there, tall), channels:] = output_grads[...]

    @pl.when((phase == 1) & (block == blocks - 1))
    def _():
        for index in range(sets):
            put_blocks(slopes_acc.at[index, 0], [out.at[index] for out in first_out], scalars[1], 0)
            put_blocks(slopes_acc.at[index, 1], [out.at[index] for out in first_out], scalars[1], channels)
            put_blocks(slopes_acc.at[index, 2], [out.at[index] for out in second_out], scalars[2], 0)


def mixer_backward(mixed, normed, lengths, scalars, per_set):
    rows, width = mixed.shape
    sets = len(per_set)
    channels = per_set[0][1].shape[1]
    blocks = rows // BLOCK
    back = lambda phase, block: (jnp.where(phase == 0, blocks - 1 - block, 0), 0)
    late = lambda phase, block: (jnp.where(phase == 0, 0, block), 0)
    whole = lambda phase, block: (0, 0)
    all3 = lambda phase, block: (0, 0, 0)
    set_specs = [
        pl.BlockSpec((channels, width), whole),
        pl.BlockSpec((BLOCK, channels), back),
        pl.BlockSpec((BLOCK, channels), late),
        pl.BlockSpec((BLOCK, channels), late),
        pl.BlockSpec((1, channels), whole),
        pl.BlockSpec((width // blocks, channels), late),
    ]
    results = pl.pallas_call(
        functools.partial(mixer_back_kernel, sets),
        grid=(2, blocks),
        in_specs=[
            pl.BlockSpec((BLOCK, width), back),
            pl.BlockSpec((BLOCK, width), late),
            pl.BlockSpec(memory_space=pltpu.SMEM),
            pl.BlockSpec(memory_space=pltpu.SMEM),
        ]
        + set_specs * sets,
        out_specs=[pl.BlockSpec((BLOCK, channels), late)] * sets
        + [pl.BlockSpec((sets, width // 2, 2 * channels), all3)] * 4
        + [pl.BlockSpec((sets, 8, channels), all3)] * 2,
        out_shape=[jax.ShapeDtypeStruct((rows, channels), BF16)] * sets
        + [jax.ShapeDtypeStruct((sets, width // 2, 2 * channels), BF16)] * 4
        + [jax.ShapeDtypeStruct((sets, 8, channels), F32)] * 2,
        scratch_shapes=[
            pltpu.VMEM((sets, rows, channels), F32),
            pltpu.VMEM((sets, rows, channels), F32),
            pltpu.VMEM((sets, BLOCK, channels), F32),
            pltpu.VMEM((sets, rows, channels), BF16),
            pltpu.VMEM((sets, 3, BLOCK, channels), BF16),
            pltpu.VMEM((sets, 3, width, channels), F32),
            pltpu.VMEM((sets, 16, channels), F32),
            pltpu.VMEM((sets, 8, channels), F32),
        ],
        compiler_params=pltpu.CompilerParams(vmem_limit_bytes=VMEM_BYTES, dimension_semantics=("arbitrary", "arbitrary")),
        cost_estimate=pl.CostEstimate(flops=2 * rows * width * 4 * channels * sets, bytes_accessed=rows * channels * 12 * sets, transcendentals=0),
        name="mixer_backward",
    )(in_hbm(mixed), in_hbm(normed), lengths, scalars, *[in_hbm(item) if item.shape[0] == rows else item for one in per_set for item in one])
    return results[:sets], results[sets : sets + 2], results[sets + 2 : sets + 4], *results[sets + 4 :]


def input_kernel(sets, *refs):
    x_ref, mixed_ref, gain_ref, *refs = refs
    factors, refs = refs[: 4 * sets], refs[4 * sets :]
    weights, refs = refs[: 3 * sets], refs[3 * sets :]
    out_ref, slope_ref, out_s = refs

    @pl.when(pl.program_id(0) == 0)
    def _():
        slope_ref[...] = jnp.zeros_like(slope_ref)

    normed_delta = None
    for index in range(sets):
        carried = factors[4 * index][...].astype(F32)
        for part in range(3):
            delta = (carried * factors[4 * index + 1 + part][...].astype(F32)).astype(BF16)
            term = dot_nt(delta, weights[3 * index + part][...])
            normed_delta = term if normed_delta is None else normed_delta + term
    rows = x_ref[...].astype(F32)
    scale = row_scale(rows)
    slope_ref[...] += fold_rows(normed_delta * rows * scale)
    scaled = normed_delta * gain_ref[...]
    inner = jnp.mean(scaled * rows, -1, keepdims=True)
    result = mixed_ref[...].astype(F32) + scale * (scaled - rows * (scale * scale * inner))
    separate(result, out_s, out_ref)

    @pl.when(pl.program_id(0) == pl.num_programs(0) - 1)
    def _():
        slope_ref[0:1, :] = jnp.sum(slope_ref[...], 0, keepdims=True)


def input_backward(x_rows, mixed, gain, factors, weights):
    rows, width = x_rows.shape
    sets = len(factors) // 4
    channels = weights[0].shape[1]
    by_rows = lambda block: (block, 0)
    whole = lambda block: (0, 0)
    return pl.pallas_call(
        functools.partial(input_kernel, sets),
        grid=(rows // BLOCK,),
        in_specs=[pl.BlockSpec((BLOCK, width), by_rows)] * 2
        + [pl.BlockSpec((1, width), whole)]
        + [pl.BlockSpec((BLOCK, channels), by_rows)] * (4 * sets)
        + [pl.BlockSpec((width, channels), whole)] * (3 * sets),
        out_specs=[pl.BlockSpec((SEGMENTS, STEPS, width), lambda block: (0, block, 0)), pl.BlockSpec((8, width), whole)],
        out_shape=[hbm((SEGMENTS, rows // SEGMENTS, width), F32), hbm((8, width), F32)],
        scratch_shapes=[pltpu.VMEM((width // 128, BLOCK, 128), F32)],
        compiler_params=pltpu.CompilerParams(vmem_limit_bytes=44 * 1024 * 1024, dimension_semantics=("arbitrary",)),
        cost_estimate=pl.CostEstimate(flops=2 * rows * width * 3 * channels * sets, bytes_accessed=rows * channels * 8 * sets, transcendentals=0),
        name="input_backward",
    )(in_hbm(x_rows), in_hbm(mixed), gain, *[in_hbm(f) for f in factors], *weights)


def finish_kernel(channels, count, *refs):
    first_refs, second_refs = refs[:count], refs[count : 2 * count]
    scalars, forget_out, admit_out, value_out, output_out, scratch = refs[2 * count :]
    tall = scratch.shape[0] // PLACES
    each = PLACES // count
    for place in range(PLACES):
        here = slice(place % each * tall, (place % each + 1) * tall)
        for index, (sums, outs) in enumerate(((first_refs, (forget_out, admit_out)), (second_refs, (value_out, scratch)))):
            there = pl.multiple_of((place ^ scalars[1 + index]) * tall, tall)
            piece = sums[place // each]
            outs[0][pl.ds(there, tall), :] = piece[here, :channels].astype(F32)
            outs[1][pl.ds(there, tall), :] = piece[here, channels:].astype(F32)
    output_out[...] = scratch[...].T


def finish_slopes(first, second, scalars):
    count = len(first)
    width, channels = count * first[0].shape[0], first[0].shape[1] // 2
    return pl.pallas_call(
        functools.partial(finish_kernel, channels, count),
        in_specs=[pl.BlockSpec(memory_space=pltpu.VMEM)] * (2 * count) + [pl.BlockSpec(memory_space=pltpu.SMEM)],
        out_shape=[jax.ShapeDtypeStruct((width, channels), F32)] * 3 + [jax.ShapeDtypeStruct((channels, width), F32)],
        scratch_shapes=[pltpu.VMEM((width, channels), F32)],
        compiler_params=pltpu.CompilerParams(vmem_limit_bytes=VMEM_BYTES),
        name="finish_slopes",
    )(*first, *second, scalars)


def regroup(stacked, half):
    count, both, width = stacked.shape
    if both == 2 * half:
        return stacked
    arrays = jnp.moveaxis(stacked.reshape(count, 2, both // 2, width), 1, 0).reshape(2, -1, half, width)
    return jnp.moveaxis(arrays, 0, 1).reshape(-1, 2 * half, width)


def after(values, *earlier):
    return lax.optimization_barrier((values, earlier))[0]


def total(terms):
    result = terms[0].astype(F32)
    for term in terms[1:]:
        result = result + term.astype(F32)
    return result.astype(terms[0].dtype)


def sum_kernel(*refs):
    for index in range(len(refs) // 3):
        left, right, out = refs[2 * index], refs[2 * index + 1], refs[2 * (len(refs) // 3) + index]
        out[...] = (left[...].astype(F32) + right[...].astype(F32)).astype(BF16)


def paired_sums(pairs, blocks, places):
    specs = [pl.BlockSpec(block, functools.partial(lambda place, step: place, place)) for block, place in zip(blocks, places)]
    return pl.pallas_call(
        sum_kernel,
        grid=(1,),
        in_specs=[spec for spec in specs for _ in range(2)],
        out_specs=[pl.BlockSpec(block, lambda step: (0, 0, 0)) for block in blocks],
        out_shape=[jax.ShapeDtypeStruct(block, BF16) for block in blocks],
        compiler_params=pltpu.CompilerParams(vmem_limit_bytes=VMEM_BYTES),
        name="paired_sums",
    )(*[item for pair in pairs for item in pair])


def hold(terms, *earlier):
    return terms[:-1] + [after(terms[-1], *earlier)]


def part(terms, index, axis):
    half = terms[0].shape[axis] // 2
    return [lax.slice_in_dim(t, index * half, (index + 1) * half, axis=axis) for t in terms]


def pack_kernel(*refs):
    mine_out, output_out = refs[5:]
    for index, ref in enumerate(refs[1:4]):
        mine_out[index] = ref[...]
    output_out[...] = refs[4][...]


def pack_halves(weights, half):
    tall, wide = weights[0].shape[0] // 2, weights[0].shape[1]
    return pl.pallas_call(
        pack_kernel,
        grid_spec=pltpu.PrefetchScalarGridSpec(
            num_scalar_prefetch=1,
            grid=(1,),
            in_specs=[pl.BlockSpec((tall, wide), lambda step, half: (half[0], 0))] * 4,
            out_specs=[pl.BlockSpec((3, tall, wide), lambda step, half: (0, 0, 0)), pl.BlockSpec((tall, wide), lambda step, half: (0, 0))],
        ),
        out_shape=[jax.ShapeDtypeStruct((3, tall, wide), BF16), jax.ShapeDtypeStruct((tall, wide), BF16)],
        name="pack_halves",
    )(jnp.reshape(half, (1,)).astype(jnp.int32), *weights)


class Links:
    TENSOR, CORE, NEAR, Z_NEAR, Z_FAR = 1, 2, 4, 8, 16

    def __init__(self):
        dp = lax.axis_index("dp")
        core, near, z_near, z_far = dp % 2, dp // 2 % 2, dp // 4 % 2, dp // 8
        self.core = core
        self.me = [core * 8 + z_near * 4 + near * 2 + z_far, core * 8 + near * 4 + z_near * 2 + z_far]

    def swap(self, values, bits):
        pairs = [(device, device ^ bits) for device in range(32)]
        return lax.ppermute(values, ("dp", "tensor"), pairs)

    def begin_weights(self, own_weights):
        mine, mine_output = pack_halves(own_weights, self.core)
        return mine, mine_output, self.swap(mine, self.TENSOR)

    def end_weights(self, got):
        rest = self.swap(got, self.CORE)
        lower = self.core == 0
        return jnp.concatenate([jnp.where(lower, got, rest), jnp.where(lower, rest, got)], -2)

    def begin_dense(self, shard):
        return [shard] + [self.swap(shard, bits) for bits in (self.Z_NEAR, self.Z_FAR, self.Z_NEAR | self.Z_FAR)]

    def dense_pieces(self, pieces):
        own = jnp.stack(pieces)
        return own, self.swap(own, self.NEAR), self.swap(own, self.CORE)

    def dense_across(self, own_terms, other_terms):
        pick = lambda terms, near: total([t[near * 4 : near * 4 + 4] for t in terms])
        sends = [(pick(other_terms, 0), self.TENSOR), (pick(own_terms, 1), self.NEAR), (pick(other_terms, 1), self.TENSOR | self.NEAR)]
        return sends, [t[:4] for t in own_terms]

    def dense_along(self, terms):
        sends = []
        for index, bits in ((1, self.Z_NEAR), (2, self.Z_FAR), (3, self.Z_NEAR | self.Z_FAR)):
            sends.append((total([t[index] for t in terms]), bits))
        return sends, [t[0] for t in terms]

    def exchange(self, sends, kept):
        return kept + [self.swap(values, bits) for values, bits in sends]

    def halve(self, terms, bits, extra=None):
        axis = 0 if bits == self.TENSOR else 1
        send = total(part(terms, 1, axis))
        if extra is not None:
            send = jnp.concatenate([send, extra], 1)
        return [(send, bits)], part(terms, 0, axis)

    def grow(self, values, bits):
        return jnp.concatenate([values, self.swap(values, bits)], 1)


class Plain:
    def __init__(self, n_tensor, own, hidden):
        self.n_tensor, self.own, self.hidden = n_tensor, own, hidden
        self.me = [0, 0]

    def weights(self, own_weights):
        whole = [lax.all_gather(w, "tensor", axis=1, tiled=True) for w in own_weights[:3]]
        pairs = [jnp.split(w, 2, 1) for w in whole]
        pairs.append(jnp.split(lax.all_gather(own_weights[3], "tensor", axis=0, tiled=True), 2, 0))
        return [p[0] for p in pairs], [p[1] for p in pairs]

    def bias(self, own_bias):
        return tuple(jnp.split(lax.all_gather(own_bias, "tensor", axis=0, tiled=True), 2))

    def dense(self, shard):
        whole = regroup(lax.all_gather(shard, ("dp", "tensor"), axis=0), 64)
        pieces = [whole[first : first + 4] for first in range(0, whole.shape[0], 4)]
        return pieces[: len(pieces) // 2], pieces[len(pieces) // 2 :]

    def dense_sums(self, grads):
        whole = regroup(jnp.concatenate(grads, 0), self.hidden)
        return lax.psum_scatter(whole, ("dp", "tensor"), scatter_dimension=0, tiled=True)[0]

    def mixer_sums(self, grads):
        grads = jnp.concatenate(grads, 1)
        _, width, columns = grads.shape
        whole = jnp.moveaxis(grads.reshape(2, width, 2, columns // 2), 0, 2).reshape(width, 2, columns)
        part = lax.psum_scatter(whole, "tensor", scatter_dimension=2, tiled=True)
        return jnp.split(lax.psum(part, "dp").reshape(width, 2 * self.own), 2, 0)

def on_device(
    block_in,
    out_cotangent,
    seq_lengths,
    premix_gain,
    forget_weight,
    admit_weight,
    value_weight,
    admit_bias,
    output_weight,
    dense_gain,
    upper_weight,
    lower_weight,
):
    n_dp, n_tensor = lax.axis_size("dp"), lax.axis_size("tensor")
    rows, width = block_in.shape
    place = lax.axis_index("tensor")
    own = forget_weight.shape[1]
    premix = premix_gain.astype(F32)[None]
    dense = dense_gain.astype(F32)[None]
    paired = (n_dp, n_tensor) == (16, 2)
    hidden = lower_weight.shape[0]
    links = Links() if paired else Plain(n_tensor, own, hidden)
    scalars = jnp.stack([place * rows] + links.me).astype(jnp.int32)
    own_weights = [forget_weight, admit_weight, value_weight, output_weight]
    dense_shard = jnp.concatenate([upper_weight.T, lower_weight], 0)
    if paired:
        weights, biases = [own_weights], [admit_bias]
        channels = own
        mine, mine_output, got = links.begin_weights(own_weights)
        pieces = links.begin_dense(after(dense_shard, mine))
        biases.append(links.swap(after(admit_bias, pieces[0]), Links.TENSOR))
    else:
        weights, biases = links.weights(own_weights), links.bias(admit_bias)
        channels = weights[0][0].shape[1]
    crossing = rows % LONGEST != 0
    nothing = jnp.zeros((1, channels), F32)

    def chained(ends, backwards):
        every = lax.all_gather(ends, "tensor", axis=0)
        entering = jnp.zeros_like(ends[0:1])
        mine = entering
        order = range(n_tensor - 1, -1, -1) if backwards else range(n_tensor)
        for index in order:
            mine = jnp.where(place == index, entering, mine)
            entering = every[index, 0:1] + every[index, 1:2] * entering
        return mine

    def forward(first, rows_in, index):
        carry = nothing
        args = (first, rows_in, premix, weights[index][:3], biases[index].astype(F32)[None], seq_lengths, scalars)
        if crossing:
            carry = chained(mixer_forward(*args, carry)[-1], False)
        return mixer_forward(*args, carry)

    x_rows, normed, *kept_0 = forward(True, block_in, 0)
    if paired:
        got, pieces, biases[1] = after((got, pieces, biases[1]), normed)
        got_output = links.swap(after(mine_output, got), Links.TENSOR)
        own_four, near_four, own_rest = links.dense_pieces(pieces)
        other_weights = links.end_weights(got)
        weights.append([other_weights[index] for index in range(3)])
    kept_1 = forward(False, normed, 1)
    kept = [kept_0, kept_1]
    if paired:
        near_four, held_four = after((near_four, own_four), kept_1[1])
        weights[1].append(links.end_weights(after(got_output, kept_1[1])))
        other_four = links.swap(held_four, Links.TENSOR)
        far_four = links.swap(held_four, Links.TENSOR | Links.NEAR)
        pieces_0 = [own_four, near_four, own_rest, links.swap(near_four, Links.CORE)]
    else:
        pieces_0, pieces_1 = links.dense(dense_shard)
    outputs = [w[3] for w in weights]
    states = [k[1] for k in kept]
    own_keep, own_send, *rows_0 = dense_both(0, states, (x_rows, out_cotangent), outputs, dense, scalars, pieces_0)
    if paired:
        far_four, other_four = after((far_four, other_four), rows_0[0])
        pieces_1 = [other_four, far_four, links.swap(other_four, Links.CORE), links.swap(far_four, Links.CORE)]
        own_terms = [own_keep, links.swap(own_send, Links.CORE)]
    other_keep, other_send, block_out, mixed, dense_part, *output_grads = dense_both(1, states, rows_0, None, dense, scalars, pieces_1)
    back_mixed = mixed
    if paired:
        other_terms = [other_keep, links.swap(other_send, Links.CORE)]
        dense_sends, dense_kept = links.dense_across(own_terms, other_terms)
        back_mixed = after(mixed, [values for values, _ in dense_sends])
        dense_terms = links.exchange(dense_sends, dense_kept)

    carries = [nothing, nothing]
    for _ in range(2 if crossing else 1):
        per_set = [
            (outputs[index], kept[index][0], kept[index][2], kept[index][3], carries[index], output_grads[index])
            for index in range(2)
        ]
        carried, first, second, bias_parts, ends = mixer_backward(back_mixed, normed, seq_lengths, scalars, per_set)
        if crossing:
            carries = [chained(ends[index], True) for index in range(2)]
    factors = [f for index in range(2) for f in (carried[index], kept[index][2], kept[index][3], kept[index][0])]
    if paired:
        dense_terms = hold(dense_terms, carried[0])
        along, along_kept = links.dense_along(dense_terms)
        core_sends = after([first[1], second[1]], dense_terms[-3:])
        first = [first[0], links.swap(core_sends[0], Links.CORE)]
        second = [second[0], links.swap(core_sends[1], Links.CORE)]
        sets, tall, wide = first[0].shape
        sends = paired_sums((first, second), ((1, tall, wide), (sets, tall // 2, wide)), ((1, 0, 0), (0, 1, 0)))
        first = [(sends[0], Links.TENSOR)], part(first, 0, 0)
        second = [(sends[1], Links.NEAR)], part(second, 0, 1)
        factors[0] = after(factors[0], first[0][0][0], second[0][0][0], [values for values, _ in along])
        first, second = links.exchange(*first), links.exchange(*second)
        dense_terms = links.exchange(along, along_kept)
    input_slope, premix_part = input_backward(x_rows, mixed, premix, factors, weights[0][:3] + weights[1][:3])

    bias_parts = jnp.sum(bias_parts, 1)
    if paired:
        bias_parts = jnp.where(place == 0, bias_parts, bias_parts[::-1])
    small = jnp.concatenate([premix_part[0], jnp.sum(dense_part, 0), bias_parts[0], bias_parts[1]], 0)
    if paired:
        small = small.reshape(1, -1, 2 * channels).astype(BF16)
        filled = small.shape[1]
        small = jnp.pad(small, ((0, 0), (0, 16 - filled), (0, 0)))
        first, second = hold(first, input_slope), hold(second, input_slope)
        dense_terms = dense_terms[:-3] + after(dense_terms[-3:], input_slope)
        small = after(small, first[-1], second[-1], dense_terms[-3:])
        small = total([small, links.swap(small, Links.CORE)])

        def halve_both(first, second, first_bits, second_bits, extra):
            first = links.halve(first, first_bits)
            second = links.halve(second, second_bits, extra)
            second_send = second[0][0][0]
            first, second = links.exchange(*first), links.exchange(*second)
            rows_sent = second_send.shape[1] - extra.shape[1]
            extra = total([extra, second[-1][:, rows_sent:]])
            return first, second[:-1] + [second[-1][:, :rows_sent]], extra

        first, second, small = halve_both(first, second, Links.Z_NEAR, Links.TENSOR, small)
        first, second, small = halve_both(first, second, Links.NEAR, Links.Z_NEAR, small)
        first, second, small = halve_both(first, second, Links.Z_FAR, Links.Z_FAR, small)
        first, second = total(first), total(second)
        first, second = links.grow(first, Links.Z_FAR), links.grow(second, Links.Z_FAR)
        count = first.shape[1]
        got = links.swap(jnp.concatenate([first, small], 1), Links.NEAR)
        first, small = jnp.concatenate([first, got[:, :count]], 1), total([small, got[:, count:]])
        second = links.grow(second, Links.Z_NEAR)
        first, second = [first, links.swap(first, Links.Z_NEAR)], [second, links.swap(second, Links.NEAR)]
        first += [links.swap(f, Links.CORE) for f in first]
        second += [links.swap(f, Links.CORE) for f in second]
        first, second = [f[0] for f in first], [f[0] for f in second]
        small = small[0, :filled].reshape(-1).astype(F32)
        dense_sum = total(dense_terms)
    else:
        small = lax.psum(small, ("dp", "tensor"))
        dense_sum = links.dense_sums([own_keep, own_send, other_keep, other_send])
        first, second = links.mixer_sums(first), links.mixer_sums(second)
    dense_sum = dense_sum.astype(F32)
    upper_slope, lower_slope = dense_sum[:hidden].T, dense_sum[hidden:]
    forget_slope, admit_slope, value_slope, output_slope = finish_slopes(first, second, scalars)
    shard = width // (n_dp * n_tensor)
    at = (lax.axis_index("dp") * n_tensor + place) * shard
    premix_slope = lax.dynamic_slice(small, (at,), (shard,))
    dense_slope = lax.dynamic_slice(small, (width + at,), (shard,))
    bias_slope = lax.dynamic_slice(small, (2 * width + place * own,), (own,))
    return (
        block_out.reshape(rows, width),
        input_slope.reshape(rows, width),
        premix_slope,
        forget_slope,
        admit_slope,
        value_slope,
        bias_slope,
        output_slope,
        dense_slope,
        upper_slope,
        lower_slope,
    )


def solution(mesh):
    placed = (
        P(("dp", "tensor"), None),
        P(("dp", "tensor"), None),
        P("dp", None),
        P(),
        P(None, "tensor"),
        P(None, "tensor"),
        P(None, "tensor"),
        P("tensor"),
        P("tensor", None),
        P(),
        P(None, ("dp", "tensor")),
        P(("dp", "tensor"), None),
    )
    return jax.shard_map(
        on_device,
        mesh=mesh,
        in_specs=placed,
        out_specs=(
            P(("dp", "tensor"), None),
            P(("dp", "tensor"), None),
            P(("dp", "tensor")),
            P(None, "tensor"),
            P(None, "tensor"),
            P(None, "tensor"),
            P("tensor"),
            P("tensor", None),
            P(("dp", "tensor")),
            P(None, ("dp", "tensor")),
            P(("dp", "tensor"), None),
        ),
        check_vma=False,
    )
```

```python
import functools

import jax
import jax.numpy as jnp
from jax import lax
from jax.experimental import pallas as pl
from jax.experimental.pallas import tpu as pltpu
from jax.sharding import PartitionSpec as P

EPSILON = 1e-06
LONGEST = 2048
SEGMENTS = 8
PLACES = 16
STEPS = 64
BLOCK = SEGMENTS * STEPS
GROUP = 32
GELU_SLOPE = 0.7978845608028654
GELU_CUBE = 0.044715
VMEM_BYTES = 56 * 1024 * 1024
F32 = jnp.float32
BF16 = jnp.bfloat16


def in_hbm(values):
    return pltpu.with_memory_space_constraint(values, pltpu.HBM)


def hbm(shape, dtype):
    return pltpu.HBM(shape, dtype)


def dot_nn(left, right):
    return lax.dot_general(left, right, (((1,), (0,)), ((), ())), preferred_element_type=F32)


def dot_nt(left, right):
    return lax.dot_general(left, right, (((1,), (1,)), ((), ())), preferred_element_type=F32)


def row_scale(rows):
    return lax.rsqrt(jnp.mean(rows * rows, -1, keepdims=True) + EPSILON)


def fold_rows(values):
    return jnp.sum(values.reshape(-1, 8, values.shape[-1]), 0)


def put_blocks(values, halves, me, first):
    tall = values.shape[0] // PLACES
    for place in range(PLACES):
        block = pl.multiple_of((place ^ me) * tall, tall)
        there = (place % (PLACES // 2)) * tall
        out = halves[place // (PLACES // 2)]
        out[there : there + tall, first : first + values.shape[1]] = values[pl.ds(block, tall), :].astype(out.dtype)


def interleave(block, scratch):
    lanes = scratch.shape[0]
    for lane in range(lanes):
        for run in range(SEGMENTS):
            part = block[run, :, lane * 128 : (lane + 1) * 128]
            scratch[lane, pl.ds(run, block.shape[1], stride=SEGMENTS), :] = part.astype(F32)
    return jnp.concatenate([scratch[lane] for lane in range(lanes)], -1)


def separate(values, scratch, out):
    lanes = scratch.shape[0]
    for lane in range(lanes):
        scratch[lane] = values[:, lane * 128 : (lane + 1) * 128]
    for run in range(SEGMENTS):
        parts = [scratch[lane, pl.ds(run, out.shape[1], stride=SEGMENTS), :] for lane in range(lanes)]
        out[run] = jnp.concatenate(parts, -1).astype(out.dtype)


def gates(forget_logit, admit_logit):
    top = jnp.maximum(jnp.maximum(-admit_logit, -forget_logit), 0.0)
    one = jnp.exp(-top)
    admit_exp = jnp.exp(-admit_logit - top)
    forget_exp = jnp.exp(-forget_logit - top)
    keep_part = one + admit_exp
    admit_part = one + forget_exp
    total = keep_part + admit_part
    inverse = pl.reciprocal(total, approx=True)
    inverse = inverse * (2.0 - total * inverse)
    keep = keep_part * inverse
    admit = admit_part * inverse
    return keep, admit, keep * (forget_exp * inverse), -admit * (admit_exp * inverse)


def goes_on(lengths_ref, scalars_ref, run, tall):
    place = scalars_ref[0] + run * tall
    begin = jnp.int32(0)
    fresh = False
    for entry in range(lengths_ref.shape[1]):
        length = lengths_ref[0, entry]
        fresh = fresh | ((begin == place) & (length > 0))
        begin = begin + length
    return jnp.where(fresh, 0.0, 1.0).astype(F32)


def product_of_runs(values, masks):
    result = masks[0] * values[0:1]
    for run in range(1, SEGMENTS):
        result = result * (masks[run] * values[run : run + 1])
    return result


def mixer_kernel(first, *refs):
    if first:
        x_ref, gain_ref, *refs = refs
    else:
        normed_in, *refs = refs
    wf, wa, wv, bias, lengths, scalars, carry, *refs = refs
    if first:
        x_out, normed_out, *refs = refs
    admit_out, state_out, forget_fac, admit_fac, ends_out, *refs = refs
    logits, hs, ps, vs, fs, as_, enter, *refs = refs
    phase, block = pl.program_id(0), pl.program_id(1)
    channels = wf.shape[1]
    start = pl.multiple_of(block * BLOCK, BLOCK)

    @pl.when((phase == 0) & (block == 0))
    def _():
        hs[0:8, :] = jnp.zeros((8, channels), F32)
        ps[0:8, :] = jnp.ones((8, channels), F32)

    @pl.when(phase == 0)
    def _():
        if first:
            rows = interleave(x_ref[...], refs[0])
            x_out[...] = rows.astype(BF16)
            normed = (rows * row_scale(rows) * gain_ref[...]).astype(BF16)
            normed_out[...] = normed
        else:
            normed = normed_in[...]
        wide = min(channels, 256)
        chunks = channels // wide
        weights = (wf, wa, wv)

        def project(chunk, kind):
            logits[chunk, kind] = dot_nn(normed, weights[kind][:, chunk * wide : (chunk + 1) * wide])

        def gate(chunk, lane, here, chain):
            inner, cols = slice(lane, lane + 128), slice(chunk * wide + lane, chunk * wide + lane + 128)
            rows = slice(here, here + GROUP)
            there = pl.ds(start + here, GROUP)
            value = logits[chunk, 2, rows, inner]
            keep, admit, forget_side, admit_side = gates(
                logits[chunk, 0, rows, inner], logits[chunk, 1, rows, inner] + bias[:, cols]
            )
            admit_out[rows, cols] = admit.astype(BF16)
            vs[there, cols] = value
            fs[there, cols] = forget_side
            as_[there, cols] = admit_side
            inflow = admit * value
            state, gain = chain
            for step in range(0, GROUP, 8):
                state = keep[step : step + 8] * state + inflow[step : step + 8]
                gain = gain * keep[step : step + 8]
                hs[pl.ds(start + here + step + 8, 8), cols] = state
                ps[pl.ds(start + here + step + 8, 8), cols] = gain
            return state, gain

        for kind in range(3):
            project(0, kind)
        for chunk in range(chunks):
            firsts = range(chunk * wide, (chunk + 1) * wide, 128)
            chains = [(hs[pl.ds(start, 8), c : c + 128], ps[pl.ds(start, 8), c : c + 128]) for c in firsts]
            units = [(here, lane) for here in range(0, BLOCK, GROUP) for lane in range(len(chains))]
            ahead = [(chunk + 1, kind) for kind in range(3)] if chunk + 1 < chunks else []
            for index, (here, lane) in enumerate(units):
                if ahead and index % max(1, len(units) // 3) == 0:
                    project(*ahead.pop(0))
                chains[lane] = gate(chunk, lane * 128, here, chains[lane])
            for item in ahead:
                project(*item)

    @pl.when((phase == 1) & (block == 0))
    def _():
        total = hs.shape[0]
        ends, gains = hs[total - 8 : total, :], ps[total - 8 : total, :]
        masks = [goes_on(lengths, scalars, run, (total - 8) // SEGMENTS) for run in range(SEGMENTS)]
        entering = masks[0] * carry[...]
        enter[0:1] = entering
        for run in range(1, SEGMENTS):
            entering = masks[run] * (ends[run - 1 : run] + gains[run - 1 : run] * entering)
            enter[run : run + 1] = entering
        ends_out[0:1, :] = ends[7:8] + gains[7:8] * enter[7:8, :]
        ends_out[1:2, :] = product_of_runs(gains, masks)
        ends_out[2:8, :] = jnp.zeros((6, channels), F32)

    @pl.when(phase == 1)
    def _():
        def some_rows(group, _):
            here = pl.multiple_of(group * 64, 64)
            there = pl.multiple_of(start + here, 64)
            for lane in range(0, channels, 128):
                cols = pl.ds(lane, 128)
                entering = enter[:, lane : lane + 128]
                states = hs[pl.ds(there, 72), cols].reshape(9, 8, 128) + ps[pl.ds(there, 72), cols].reshape(9, 8, 128) * entering
                states = states.reshape(72, 128)
                state_out[pl.ds(here, 64), cols] = states[8:].astype(BF16)
                change = states[:64] - vs[pl.ds(there, 64), cols]
                forget_fac[pl.ds(here, 64), cols] = (change * fs[pl.ds(there, 64), cols]).astype(BF16)
                admit_fac[pl.ds(here, 64), cols] = (change * as_[pl.ds(there, 64), cols]).astype(BF16)
            return 0

        lax.fori_loop(0, BLOCK // 64, some_rows, 0)


def mixer_forward(first, rows_in, gain, weights, bias, lengths, scalars, carry):
    width = rows_in.shape[-1]
    rows = rows_in.size // width
    channels = weights[0].shape[1]
    blocks = rows // BLOCK
    early = lambda phase, block: (jnp.where(phase == 0, block, blocks - 1), 0)
    late = lambda phase, block: (jnp.where(phase == 0, 0, block), 0)
    whole = lambda phase, block: (0, 0)
    if first:
        in_specs = [
            pl.BlockSpec((SEGMENTS, STEPS, width), lambda phase, block: (0, jnp.where(phase == 0, block, blocks - 1), 0)),
            pl.BlockSpec((1, width), whole),
        ]
        operands = [rows_in.reshape(SEGMENTS, rows // SEGMENTS, width), gain]
        out_specs = [pl.BlockSpec((BLOCK, width), early)] * 2
        out_shape = [hbm((rows, width), BF16)] * 2
    else:
        in_specs, operands = [pl.BlockSpec((BLOCK, width), early)], [rows_in]
        out_specs, out_shape = [], []
    in_specs += [pl.BlockSpec((width, channels), whole)] * 3
    in_specs += [pl.BlockSpec((1, channels), whole)] + [pl.BlockSpec(memory_space=pltpu.SMEM)] * 2 + [pl.BlockSpec((1, channels), whole)]
    out_specs += [pl.BlockSpec((BLOCK, channels), early)] + [pl.BlockSpec((BLOCK, channels), late)] * 3
    out_specs += [pl.BlockSpec((8, channels), whole)]
    out_shape += [hbm((rows, channels), BF16)] * 4
    out_shape += [hbm((8, channels), F32)]
    wide = min(channels, 256)
    scratch = [pltpu.VMEM((channels // wide, 3, BLOCK, wide), F32)]
    scratch += [pltpu.VMEM((rows + 8, channels), F32)] * 2
    scratch += [pltpu.VMEM((rows, channels), F32)] * 3
    scratch += [pltpu.VMEM((8, channels), F32)]
    if first:
        scratch += [pltpu.VMEM((width // 128, BLOCK, 128), F32)]
    return pl.pallas_call(
        functools.partial(mixer_kernel, first),
        grid=(2, blocks),
        in_specs=in_specs,
        out_specs=out_specs,
        out_shape=out_shape,
        scratch_shapes=scratch,
        compiler_params=pltpu.CompilerParams(vmem_limit_bytes=36 * 1024 * 1024, dimension_semantics=("arbitrary", "arbitrary")),
        cost_estimate=pl.CostEstimate(flops=2 * rows * width * 3 * channels, bytes_accessed=rows * channels * 16, transcendentals=4 * rows * channels),
        name="mixer_forward",
    )(in_hbm(operands[0]), *operands[1:], *weights, bias, lengths, scalars, carry)


def dense_kernel(stage, sets, pieces, *refs):
    states, refs = refs[:sets], refs[sets:]
    if stage == 0:
        x_ref, c_ref, *refs = refs
        outs_w, refs = refs[:sets], refs[sets:]
    else:
        middle_ref, sum_ref, delta_ref, dense_ref, cotangent_ref, *refs = refs
    gain_ref, scalars, *refs = refs
    pieces_w, refs = refs[:pieces], refs[pieces:]
    keep_out, send_out, *refs = refs
    if stage == 0:
        middle_out, sum_out, delta_out, dense_out, cotangent_out, upper_acc, lower_acc, cotangent_s = refs
    else:
        out_ref, mixed_ref, slope_ref, *refs = refs
        outputs_ref, refs = refs[:sets], refs[sets:]
        upper_acc, lower_acc, output_acc, out_s = refs
    step = pl.program_id(0)
    gain = gain_ref[...]
    shards, both, width = pieces_w[0].shape
    half = both // 2

    @pl.when(step == 0)
    def _():
        upper_acc[...] = jnp.zeros_like(upper_acc)
        lower_acc[...] = jnp.zeros_like(lower_acc)
        if stage == 1:
            output_acc[...] = jnp.zeros_like(output_acc)
            slope_ref[...] = jnp.zeros_like(slope_ref)

    if stage == 0:
        middle = x_ref[...].astype(F32)
        for state, weight in zip(states, outs_w):
            middle = middle + dot_nn(state[...], weight[...])
        middle_out[...] = middle.astype(BF16)
        dense_in = (middle * row_scale(middle) * gain).astype(BF16)
        dense_out[...] = dense_in
        cotangent = interleave(c_ref[...], cotangent_s).astype(BF16)
        cotangent_out[...] = cotangent
    else:
        dense_in, cotangent = dense_ref[...], cotangent_ref[...]
    dense_t, cotangent_t = dense_in.T, cotangent.T
    fed, delta = None, None
    joined = max(1, 512 // (shards * half))
    for chunk in range(0, pieces, joined):
        some = pieces_w[chunk : chunk + joined]
        upper_w = jnp.concatenate([w[:, :half, :].reshape(shards * half, width) for w in some], 0)
        lower_w = jnp.concatenate([w[:, half:, :].reshape(shards * half, width) for w in some], 0)
        cols = slice(chunk * shards * half, (chunk + joined) * shards * half)
        upper = dot_nt(dense_in, upper_w)
        square = upper * upper
        bell = 0.5 + 0.5 * jnp.tanh(upper * (GELU_SLOPE + GELU_SLOPE * GELU_CUBE * square))
        active = upper * bell
        slope = bell + active * (1.0 - bell) * (2.0 * GELU_SLOPE + 6.0 * GELU_SLOPE * GELU_CUBE * square)
        active = active.astype(BF16)
        part = dot_nn(active, lower_w)
        fed = part if fed is None else fed + part
        upper_delta = (slope * dot_nt(cotangent, lower_w)).astype(BF16)
        part = dot_nn(upper_delta, upper_w)
        delta = part if delta is None else delta + part
        lower_acc[:, cols] += dot_nn(cotangent_t, active)
        upper_acc[:, cols] += dot_nn(dense_t, upper_delta)
    if stage == 0:
        sum_out[...] = (middle + fed).astype(BF16)
        delta_out[...] = delta.astype(BF16)
    else:
        separate(sum_ref[...].astype(F32) + fed, out_s, out_ref)
        middle = middle_ref[...].astype(F32)
        scale = row_scale(middle)
        delta = delta_ref[...].astype(F32) + delta
        slope_ref[...] += fold_rows(delta * middle * scale)
        scaled = delta * gain
        inner = jnp.mean(scaled * middle, -1, keepdims=True)
        mixed = (cotangent.astype(F32) + scale * (scaled - middle * (scale * scale * inner))).astype(BF16)
        mixed_ref[...] = mixed
        mixed_t = mixed.T
        channels = states[0].shape[1]
        for index, state in enumerate(states):
            output_acc[:, index * channels : (index + 1) * channels] += dot_nn(mixed_t, state[...])

    @pl.when(step == pl.num_programs(0) - 1)
    def _():
        for shard in range(0, pieces * shards, 2):
            cols = slice(shard * half, (shard + 2) * half)
            out = keep_out if shard < pieces * shards // 2 else send_out
            there = shard % (pieces * shards // 2)
            out[there : there + 2, :half, :] = upper_acc[:, cols].T.astype(BF16).reshape(2, half, width)
            out[there : there + 2, half:, :] = lower_acc[:, cols].T.astype(BF16).reshape(2, half, width)
        if stage == 1:
            slope_ref[0:1, :] = jnp.sum(slope_ref[...], 0, keepdims=True)
            tall = output_acc.shape[0] // PLACES
            for index, output in enumerate(outputs_ref):
                for place in range(PLACES):
                    there = pl.multiple_of((place ^ scalars[2]) * tall, tall)
                    output[place * tall : (place + 1) * tall, :] = output_acc[
                        pl.ds(there, tall), index * channels : (index + 1) * channels
                    ].astype(BF16)


def dense_both(stage, states, entering, output_weights, gain, scalars, pieces):
    rows, channels = states[0].shape
    width = gain.shape[1]
    shards, both, _ = pieces[0].shape
    hidden = len(pieces) * shards * both // 2
    sets = len(states)
    tall = min(rows, 512)
    by_rows = lambda block: (block, 0)
    whole = lambda block: (0, 0)
    runs_spec = pl.BlockSpec((SEGMENTS, tall // SEGMENTS, width), lambda block: (0, block, 0))
    runs_shape = (SEGMENTS, rows // SEGMENTS, width)
    row_spec = pl.BlockSpec((tall, width), by_rows)
    grads = (len(pieces) * shards // 2, both, width)
    in_specs = [pl.BlockSpec((tall, channels), by_rows)] * sets
    out_specs = [pl.BlockSpec(grads, lambda block: (0, 0, 0))] * 2
    out_shape = [hbm(grads, BF16)] * 2
    scratch = [pltpu.VMEM((width, hidden), F32)] * 2
    if stage == 0:
        in_specs += [row_spec, runs_spec] + [pl.BlockSpec((channels, width), whole)] * sets
        entering = [entering[0], entering[1].reshape(runs_shape), *output_weights]
        out_specs += [row_spec] * 5
        out_shape += [hbm((rows, width), BF16)] * 5
    else:
        in_specs += [row_spec] * 5
        out_specs += [runs_spec, row_spec, pl.BlockSpec((8, width), whole)] + [pl.BlockSpec((width, channels), whole)] * sets
        out_shape += [hbm(runs_shape, BF16), hbm((rows, width), BF16)]
        out_shape += [hbm((8, width), F32)] + [hbm((width, channels), BF16)] * sets
        scratch += [pltpu.VMEM((width, sets * channels), F32)]
    scratch += [pltpu.VMEM((width // 128, tall, 128), F32)]
    in_specs += [pl.BlockSpec((1, width), whole), pl.BlockSpec(memory_space=pltpu.SMEM)]
    in_specs += [pl.BlockSpec((shards, both, width), lambda block: (0, 0, 0))] * len(pieces)
    return pl.pallas_call(
        functools.partial(dense_kernel, stage, sets, len(pieces)),
        grid=(rows // tall,),
        in_specs=in_specs,
        out_specs=out_specs,
        out_shape=out_shape,
        scratch_shapes=scratch,
        compiler_params=pltpu.CompilerParams(vmem_limit_bytes=44 * 1024 * 1024, dimension_semantics=("arbitrary",)),
        cost_estimate=pl.CostEstimate(flops=12 * rows * width * hidden, bytes_accessed=rows * width * 24, transcendentals=rows * hidden),
        name="dense_first" if stage == 0 else "dense_second",
    )(*[in_hbm(v) for v in states], *[in_hbm(v) if v.shape[0] != channels else v for v in entering], gain, scalars, *pieces)


def mixer_back_kernel(sets, mixed_ref, normed_ref, lengths, scalars, *refs):
    per_set = [refs[index * 6 : index * 6 + 6] for index in range(sets)]
    refs = refs[6 * sets :]
    carried_out, refs = refs[:sets], refs[sets:]
    first_out, second_out, refs = refs[:2], refs[2:4], refs[4:]
    bias_out, ends_out, *refs = refs
    cs, ps, state_delta, admits, deltas, slopes_acc, last, enter = refs
    phase, block = pl.program_id(0), pl.program_id(1)
    blocks = pl.num_programs(1)
    channels = per_set[0][1].shape[1]
    place = jnp.where(phase == 0, blocks - 1 - block, block)
    start = pl.multiple_of(place * BLOCK, BLOCK)

    @pl.when((phase == 0) & (block == 0))
    def _():
        last[:, 0:8, :] = jnp.zeros((sets, 8, channels), F32)
        last[:, 8:16, :] = jnp.ones((sets, 8, channels), F32)

    @pl.when(phase == 0)
    def _():
        def arrive(index):
            state_delta[index] = dot_nt(mixed_ref[...], per_set[index][0][...])

        arrive(0)
        for index in range(sets):
            admit_ref = per_set[index][1]
            for lane in range(0, channels, 128):
                if lane == 0 and index + 1 < sets:
                    arrive(index + 1)
                cols = slice(lane, lane + 128)
                kept, gain = last[index, 0:8, cols], last[index, 8:16, cols]
                for here in range(BLOCK - 16, -1, -16):
                    admit = admit_ref[here : here + 16, cols]
                    admits[index, pl.ds(start + here, 16), cols] = admit
                    keep = 1.0 - admit.astype(F32)
                    for step in (8, 0):
                        carried = state_delta[index, here + step : here + step + 8, cols] + kept
                        cs[index, pl.ds(start + here + step, 8), cols] = carried
                        ps[index, pl.ds(start + here + step, 8), cols] = gain
                        kept = keep[step : step + 8] * carried
                        gain = keep[step : step + 8] * gain
                last[index, 0:8, cols] = kept
                last[index, 8:16, cols] = gain

    @pl.when((phase == 1) & (block == 0))
    def _():
        masks = [goes_on(lengths, scalars, run, cs.shape[1] // SEGMENTS) for run in range(SEGMENTS)]
        for index in range(sets):
            kept, gain = last[index, 0:8, :], last[index, 8:16, :]
            entering = per_set[index][4][...]
            enter[index, 7:8, :] = entering
            for run in range(SEGMENTS - 1, 0, -1):
                entering = masks[run] * (kept[run : run + 1] + gain[run : run + 1] * entering)
                enter[index, run - 1 : run, :] = entering
            ends_out[index, 0:1, :] = masks[0] * (kept[0:1] + gain[0:1] * entering)
            ends_out[index, 1:2, :] = product_of_runs(gain, masks)
            ends_out[index, 2:8, :] = jnp.zeros((6, channels), F32)
        bias_out[...] = jnp.zeros_like(bias_out)
        slopes_acc[...] = jnp.zeros_like(slopes_acc)

    @pl.when(phase == 1)
    def _():
        normed_t = normed_ref[...].T
        wide = min(channels, 256)
        chunks = [(index, first) for index in range(sets) for first in range(0, channels, wide)]

        def move(index, lane, here):
            _, _, forget_fac, admit_fac, _, _ = per_set[index]
            cols = slice(lane, lane + 128)
            rows, there = slice(here, here + GROUP), pl.ds(start + here, GROUP)
            gains = ps[index, there, cols].reshape(GROUP // 8, 8, 128)
            carried = (cs[index, there, cols].reshape(GROUP // 8, 8, 128) + gains * enter[index, :, cols]).reshape(GROUP, 128)
            carried_out[index][rows, cols] = carried.astype(BF16)
            admit_delta = (carried * admit_fac[rows, cols].astype(F32)).astype(BF16)
            deltas[index, 0, rows, cols] = (carried * forget_fac[rows, cols].astype(F32)).astype(BF16)
            deltas[index, 1, rows, cols] = admit_delta
            deltas[index, 2, rows, cols] = (carried * admits[index, there, cols].astype(F32)).astype(BF16)
            return fold_rows(admit_delta.astype(F32))

        def reduce(index, first, kind):
            cols = slice(first, first + wide)
            slopes_acc[index, kind, :, cols] += dot_nn(normed_t, deltas[index, kind, :, cols])

        behind = []
        for index, first in chunks:
            lanes = range(first, first + wide, 128)
            biases = [jnp.zeros((8, 128), F32) for _ in lanes]
            units = [(here, which) for here in range(0, BLOCK, GROUP) for which in range(len(lanes))]
            for position, (here, which) in enumerate(units):
                if behind and position % max(1, len(units) // 3) == 0:
                    reduce(*behind.pop(0))
                biases[which] = biases[which] + move(index, lanes[which], here)
            for lane, bias in zip(lanes, biases):
                bias_out[index, :, lane : lane + 128] += bias
            for item in behind:
                reduce(*item)
            behind = [(index, first, kind) for kind in range(3)]
        for item in behind:
            reduce(*item)
        for index in range(sets):
            output_grads = per_set[index][5]
            tall = output_grads.shape[0]
            for half in range(2):

                @pl.when(block // (blocks // 2) == half)
                def _():
                    there = pl.multiple_of(block % (blocks // 2) * tall, tall)
                    second_out[half][index, pl.ds(there, tall), channels:] = output_grads[...]

    @pl.when((phase == 1) & (block == blocks - 1))
    def _():
        for index in range(sets):
            bias_out[index, 0:1, :] = jnp.sum(bias_out[index], 0, keepdims=True)
            put_blocks(slopes_acc.at[index, 0], [out.at[index] for out in first_out], scalars[1], 0)
            put_blocks(slopes_acc.at[index, 1], [out.at[index] for out in first_out], scalars[1], channels)
            put_blocks(slopes_acc.at[index, 2], [out.at[index] for out in second_out], scalars[2], 0)


def mixer_backward(mixed, normed, lengths, scalars, per_set):
    rows, width = mixed.shape
    sets = len(per_set)
    channels = per_set[0][1].shape[1]
    blocks = rows // BLOCK
    back = lambda phase, block: (jnp.where(phase == 0, blocks - 1 - block, 0), 0)
    late = lambda phase, block: (jnp.where(phase == 0, 0, block), 0)
    whole = lambda phase, block: (0, 0)
    all3 = lambda phase, block: (0, 0, 0)
    set_specs = [
        pl.BlockSpec((channels, width), whole),
        pl.BlockSpec((BLOCK, channels), back),
        pl.BlockSpec((BLOCK, channels), late),
        pl.BlockSpec((BLOCK, channels), late),
        pl.BlockSpec((1, channels), whole),
        pl.BlockSpec((width // blocks, channels), late),
    ]
    results = pl.pallas_call(
        functools.partial(mixer_back_kernel, sets),
        grid=(2, blocks),
        in_specs=[
            pl.BlockSpec((BLOCK, width), back),
            pl.BlockSpec((BLOCK, width), late),
            pl.BlockSpec(memory_space=pltpu.SMEM),
            pl.BlockSpec(memory_space=pltpu.SMEM),
        ]
        + set_specs * sets,
        out_specs=[pl.BlockSpec((BLOCK, channels), late)] * sets
        + [pl.BlockSpec((sets, width // 2, 2 * channels), all3)] * 4
        + [pl.BlockSpec((sets, 8, channels), all3)] * 2,
        out_shape=[jax.ShapeDtypeStruct((rows, channels), BF16)] * sets
        + [jax.ShapeDtypeStruct((sets, width // 2, 2 * channels), BF16)] * 4
        + [jax.ShapeDtypeStruct((sets, 8, channels), F32)] * 2,
        scratch_shapes=[
            pltpu.VMEM((sets, rows, channels), F32),
            pltpu.VMEM((sets, rows, channels), F32),
            pltpu.VMEM((sets, BLOCK, channels), F32),
            pltpu.VMEM((sets, rows, channels), BF16),
            pltpu.VMEM((sets, 3, BLOCK, channels), BF16),
            pltpu.VMEM((sets, 3, width, channels), F32),
            pltpu.VMEM((sets, 16, channels), F32),
            pltpu.VMEM((sets, 8, channels), F32),
        ],
        compiler_params=pltpu.CompilerParams(vmem_limit_bytes=50 * 1024 * 1024, dimension_semantics=("arbitrary", "arbitrary")),
        cost_estimate=pl.CostEstimate(flops=2 * rows * width * 4 * channels * sets, bytes_accessed=rows * channels * 12 * sets, transcendentals=0),
        name="mixer_backward",
    )(in_hbm(mixed), in_hbm(normed), lengths, scalars, *[in_hbm(item) if item.shape[0] == rows else item for one in per_set for item in one])
    return results[:sets], results[sets : sets + 2], results[sets + 2 : sets + 4], *results[sets + 4 :]


def input_kernel(sets, *refs):
    x_ref, mixed_ref, gain_ref, *refs = refs
    factors, refs = refs[: 4 * sets], refs[4 * sets :]
    weights, refs = refs[: 3 * sets], refs[3 * sets :]
    dense_ref, bias_ref, scalars, out_ref, small_ref, slope_ref, out_s = refs

    @pl.when(pl.program_id(0) == 0)
    def _():
        slope_ref[...] = jnp.zeros_like(slope_ref)

    normed_delta = None
    for index in range(sets):
        carried = factors[4 * index][...].astype(F32)
        for part in range(3):
            delta = (carried * factors[4 * index + 1 + part][...].astype(F32)).astype(BF16)
            term = dot_nt(delta, weights[3 * index + part][...])
            normed_delta = term if normed_delta is None else normed_delta + term
    rows = x_ref[...].astype(F32)
    scale = row_scale(rows)
    slope_ref[...] += fold_rows(normed_delta * rows * scale)
    scaled = normed_delta * gain_ref[...]
    inner = jnp.mean(scaled * rows, -1, keepdims=True)
    result = mixed_ref[...].astype(F32) + scale * (scaled - rows * (scale * scale * inner))
    separate(result, out_s, out_ref)

    @pl.when(pl.program_id(0) == pl.num_programs(0) - 1)
    def _():
        gains = jnp.concatenate([jnp.sum(slope_ref[...], 0, keepdims=True), dense_ref[0:1, :]], 1)
        low = jnp.where(scalars[3] == 0, bias_ref[0, 0:1, :], bias_ref[1, 0:1, :])
        high = jnp.where(scalars[3] == 0, bias_ref[1, 0:1, :], bias_ref[0, 0:1, :])
        biases = jnp.concatenate([low, high], 1)
        rest = jnp.zeros((small_ref.shape[0] - 2, biases.shape[1]), F32)
        small_ref[...] = jnp.concatenate([gains, biases, rest], 0).astype(BF16)


def input_backward(x_rows, mixed, gain, factors, weights, dense_part, bias_parts, scalars):
    rows, width = x_rows.shape
    sets = len(factors) // 4
    channels = weights[0].shape[1]
    by_rows = lambda block: (block, 0)
    whole = lambda block: (0, 0)
    return pl.pallas_call(
        functools.partial(input_kernel, sets),
        grid=(rows // BLOCK,),
        in_specs=[pl.BlockSpec((BLOCK, width), by_rows)] * 2
        + [pl.BlockSpec((1, width), whole)]
        + [pl.BlockSpec((BLOCK, channels), by_rows)] * (4 * sets)
        + [pl.BlockSpec((width, channels), whole)] * (3 * sets)
        + [pl.BlockSpec((8, width), whole), pl.BlockSpec((sets, 8, channels), lambda block: (0, 0, 0)), pl.BlockSpec(memory_space=pltpu.SMEM)],
        out_specs=[pl.BlockSpec((SEGMENTS, STEPS, width), lambda block: (0, block, 0)), pl.BlockSpec((16, sets * channels), whole)],
        out_shape=[hbm((SEGMENTS, rows // SEGMENTS, width), F32), jax.ShapeDtypeStruct((16, sets * channels), BF16)],
        scratch_shapes=[pltpu.VMEM((8, width), F32), pltpu.VMEM((width // 128, BLOCK, 128), F32)],
        compiler_params=pltpu.CompilerParams(vmem_limit_bytes=44 * 1024 * 1024, dimension_semantics=("arbitrary",)),
        cost_estimate=pl.CostEstimate(flops=2 * rows * width * 3 * channels * sets, bytes_accessed=rows * channels * 8 * sets, transcendentals=0),
        name="input_backward",
    )(in_hbm(x_rows), in_hbm(mixed), gain, *[in_hbm(f) for f in factors], *weights, dense_part, bias_parts, scalars)


def finish_kernel(channels, count, *refs):
    first_refs, second_refs = refs[:count], refs[count : 2 * count]
    scalars, forget_out, admit_out, value_out, output_out, scratch = refs[2 * count :]
    tall = scratch.shape[0] // PLACES
    each = PLACES // count
    for place in range(PLACES):
        here = slice(place % each * tall, (place % each + 1) * tall)
        for index, (sums, outs) in enumerate(((first_refs, (forget_out, admit_out)), (second_refs, (value_out, scratch)))):
            there = pl.multiple_of((place ^ scalars[1 + index]) * tall, tall)
            piece = sums[place // each]
            outs[0][pl.ds(there, tall), :] = piece[here, :channels].astype(F32)
            outs[1][pl.ds(there, tall), :] = piece[here, channels:].astype(F32)
    output_out[...] = scratch[...].T


def finish_slopes(first, second, scalars):
    count = len(first)
    width, channels = count * first[0].shape[0], first[0].shape[1] // 2
    return pl.pallas_call(
        functools.partial(finish_kernel, channels, count),
        in_specs=[pl.BlockSpec(memory_space=pltpu.VMEM)] * (2 * count) + [pl.BlockSpec(memory_space=pltpu.SMEM)],
        out_shape=[jax.ShapeDtypeStruct((width, channels), F32)] * 3 + [jax.ShapeDtypeStruct((channels, width), F32)],
        scratch_shapes=[pltpu.VMEM((width, channels), F32)],
        compiler_params=pltpu.CompilerParams(vmem_limit_bytes=VMEM_BYTES),
        name="finish_slopes",
    )(*first, *second, scalars)


def regroup(stacked, half):
    count, both, width = stacked.shape
    if both == 2 * half:
        return stacked
    arrays = jnp.moveaxis(stacked.reshape(count, 2, both // 2, width), 1, 0).reshape(2, -1, half, width)
    return jnp.moveaxis(arrays, 0, 1).reshape(-1, 2 * half, width)


def after(values, *earlier):
    return lax.optimization_barrier((values, earlier))[0]


def total(terms):
    result = terms[0].astype(F32)
    for term in terms[1:]:
        result = result + term.astype(F32)
    return result.astype(terms[0].dtype)


def sum_kernel(*refs):
    count = len(refs) // 3
    for index in range(count):
        left, right, out = refs[2 * index], refs[2 * index + 1], refs[2 * count + index]
        out[...] = (left[...].astype(F32) + right[...].astype(F32)).astype(BF16)


def paired_sums(pairs, blocks, places):
    specs = [pl.BlockSpec(block, functools.partial(lambda place, step: place, place)) for block, place in zip(blocks, places)]
    return pl.pallas_call(
        sum_kernel,
        grid=(1,),
        in_specs=[spec for spec in specs for _ in range(2)],
        out_specs=[pl.BlockSpec(block, lambda step: (0, 0, 0)) for block in blocks],
        out_shape=[jax.ShapeDtypeStruct(block, BF16) for block in blocks],
        compiler_params=pltpu.CompilerParams(vmem_limit_bytes=VMEM_BYTES),
        name="paired_sums",
    )(*[item for pair in pairs for item in pair])


def hold(terms, *earlier):
    return terms[:-1] + [after(terms[-1], *earlier)]


def part(terms, index, axis):
    half = terms[0].shape[axis] // 2
    return [lax.slice_in_dim(t, index * half, (index + 1) * half, axis=axis) for t in terms]


def pack_kernel(*refs):
    mine_out, output_out = refs[5:]
    for index, ref in enumerate(refs[1:4]):
        mine_out[index] = ref[...]
    output_out[...] = refs[4][...]


def pack_halves(weights, half):
    tall, wide = weights[0].shape[0] // 2, weights[0].shape[1]
    return pl.pallas_call(
        pack_kernel,
        grid_spec=pltpu.PrefetchScalarGridSpec(
            num_scalar_prefetch=1,
            grid=(1,),
            in_specs=[pl.BlockSpec((tall, wide), lambda step, half: (half[0], 0))] * 4,
            out_specs=[pl.BlockSpec((3, tall, wide), lambda step, half: (0, 0, 0)), pl.BlockSpec((tall, wide), lambda step, half: (0, 0))],
        ),
        out_shape=[jax.ShapeDtypeStruct((3, tall, wide), BF16), jax.ShapeDtypeStruct((tall, wide), BF16)],
        name="pack_halves",
    )(jnp.reshape(half, (1,)).astype(jnp.int32), *weights)


class Links:
    TENSOR, CORE, NEAR, Z_NEAR, Z_FAR = 1, 2, 4, 8, 16

    def __init__(self):
        dp = lax.axis_index("dp")
        core, near, z_near = dp % 2, dp // 2 % 2, dp // 4 % 2
        self.core = core
        self.me = [core * 8 + z_near * 4 + near * 2, core * 8 + near * 4 + z_near * 2]

    def swap(self, values, bits):
        pairs = [(device, device ^ bits) for device in range(32)]
        return lax.ppermute(values, ("dp", "tensor"), pairs)

    def begin_weights(self, own_weights):
        mine, mine_output = pack_halves(own_weights, self.core)
        return mine, mine_output, self.swap(mine, self.TENSOR)

    def end_weights(self, got):
        rest = self.swap(got, self.CORE)
        lower = self.core == 0
        return jnp.concatenate([jnp.where(lower, got, rest), jnp.where(lower, rest, got)], -2)

    def begin_dense(self, shard):
        return [shard] + [self.swap(shard, bits) for bits in (self.Z_NEAR, self.Z_FAR, self.Z_NEAR | self.Z_FAR)]

    def dense_pieces(self, pieces):
        own = jnp.stack(pieces)
        return own, self.swap(own, self.NEAR), self.swap(own, self.CORE)

    def dense_across(self, own_terms, other_terms):
        pick = lambda terms, near: total([t[near * 4 : near * 4 + 4] for t in terms])
        sends = [(pick(other_terms, 0), self.TENSOR), (pick(own_terms, 1), self.NEAR), (pick(other_terms, 1), self.TENSOR | self.NEAR)]
        return sends, [t[:4] for t in own_terms]

    def dense_along(self, terms):
        sends = []
        for index, bits in ((1, self.Z_NEAR), (2, self.Z_FAR), (3, self.Z_NEAR | self.Z_FAR)):
            sends.append((total([t[index] for t in terms]), bits))
        return sends, [t[0] for t in terms]

    def exchange(self, sends, kept):
        return kept + [self.swap(values, bits) for values, bits in sends]

    def halve(self, terms, bits, extra=None):
        axis = 0 if bits == self.TENSOR else 1
        send = total(part(terms, 1, axis))
        if extra is not None:
            send = jnp.concatenate([send, extra], 1)
        return [(send, bits)], part(terms, 0, axis)

    def grow(self, values, bits):
        return jnp.concatenate([values, self.swap(values, bits)], 1)


class Plain:
    def __init__(self, n_tensor, own, hidden):
        self.n_tensor, self.own, self.hidden = n_tensor, own, hidden
        self.me = [0, 0]

    def weights(self, own_weights):
        whole = [lax.all_gather(w, "tensor", axis=1, tiled=True) for w in own_weights[:3]]
        pairs = [jnp.split(w, 2, 1) for w in whole]
        pairs.append(jnp.split(lax.all_gather(own_weights[3], "tensor", axis=0, tiled=True), 2, 0))
        return [p[0] for p in pairs], [p[1] for p in pairs]

    def bias(self, own_bias):
        return tuple(jnp.split(lax.all_gather(own_bias, "tensor", axis=0, tiled=True), 2))

    def dense(self, shard):
        whole = regroup(lax.all_gather(shard, ("dp", "tensor"), axis=0), 64)
        pieces = [whole[first : first + 4] for first in range(0, whole.shape[0], 4)]
        return pieces[: len(pieces) // 2], pieces[len(pieces) // 2 :]

    def dense_sums(self, grads):
        whole = regroup(jnp.concatenate(grads, 0), self.hidden)
        return lax.psum_scatter(whole, ("dp", "tensor"), scatter_dimension=0, tiled=True)[0]

    def mixer_sums(self, grads):
        grads = jnp.concatenate(grads, 1)
        _, width, columns = grads.shape
        whole = jnp.moveaxis(grads.reshape(2, width, 2, columns // 2), 0, 2).reshape(width, 2, columns)
        part = lax.psum_scatter(whole, "tensor", scatter_dimension=2, tiled=True)
        return jnp.split(lax.psum(part, "dp").reshape(width, 2 * self.own), 2, 0)

def on_device(
    block_in,
    out_cotangent,
    seq_lengths,
    premix_gain,
    forget_weight,
    admit_weight,
    value_weight,
    admit_bias,
    output_weight,
    dense_gain,
    upper_weight,
    lower_weight,
):
    n_dp, n_tensor = lax.axis_size("dp"), lax.axis_size("tensor")
    rows, width = block_in.shape
    place = lax.axis_index("tensor")
    own = forget_weight.shape[1]
    premix = premix_gain.astype(F32)[None]
    dense = dense_gain.astype(F32)[None]
    paired = (n_dp, n_tensor) == (16, 2)
    hidden = lower_weight.shape[0]
    links = Links() if paired else Plain(n_tensor, own, hidden)
    scalars = jnp.stack([place * rows] + links.me + [place if paired else 0]).astype(jnp.int32)
    own_weights = [forget_weight, admit_weight, value_weight, output_weight]
    dense_shard = jnp.concatenate([upper_weight.T, lower_weight], 0)
    if paired:
        weights, biases = [own_weights], [admit_bias]
        channels = own
        mine, mine_output, got = links.begin_weights(own_weights)
        pieces = links.begin_dense(after(dense_shard, mine))
        biases.append(links.swap(after(admit_bias, pieces[0]), Links.TENSOR))
    else:
        weights, biases = links.weights(own_weights), links.bias(admit_bias)
        channels = weights[0][0].shape[1]
    crossing = rows % LONGEST != 0
    nothing = jnp.zeros((1, channels), F32)

    def chained(ends, backwards):
        every = lax.all_gather(ends, "tensor", axis=0)
        entering = jnp.zeros_like(ends[0:1])
        mine = entering
        order = range(n_tensor - 1, -1, -1) if backwards else range(n_tensor)
        for index in order:
            mine = jnp.where(place == index, entering, mine)
            entering = every[index, 0:1] + every[index, 1:2] * entering
        return mine

    def forward(first, rows_in, index):
        carry = nothing
        args = (first, rows_in, premix, weights[index][:3], biases[index].astype(F32)[None], seq_lengths, scalars)
        if crossing:
            carry = chained(mixer_forward(*args, carry)[-1], False)
        return mixer_forward(*args, carry)

    x_rows, normed, *kept_0 = forward(True, block_in, 0)
    if paired:
        got, pieces, biases[1] = after((got, pieces, biases[1]), normed)
        got_output = links.swap(after(mine_output, got), Links.TENSOR)
        own_four, near_four, own_rest = links.dense_pieces(pieces)
        other_weights = links.end_weights(got)
        weights.append([other_weights[index] for index in range(3)])
    kept_1 = forward(False, normed, 1)
    kept = [kept_0, kept_1]
    if paired:
        near_four, held_four = after((near_four, own_four), kept_1[1])
        weights[1].append(links.end_weights(after(got_output, kept_1[1])))
        other_four = links.swap(held_four, Links.TENSOR)
        far_four = links.swap(held_four, Links.TENSOR | Links.NEAR)
        pieces_0 = [own_four, near_four, own_rest, links.swap(near_four, Links.CORE)]
    else:
        pieces_0, pieces_1 = links.dense(dense_shard)
    outputs = [w[3] for w in weights]
    states = [k[1] for k in kept]
    own_keep, own_send, *rows_0 = dense_both(0, states, (x_rows, out_cotangent), outputs, dense, scalars, pieces_0)
    if paired:
        far_four, other_four = after((far_four, other_four), rows_0[0])
        pieces_1 = [other_four, far_four, links.swap(other_four, Links.CORE), links.swap(far_four, Links.CORE)]
        own_terms = [own_keep, links.swap(own_send, Links.CORE)]
    other_keep, other_send, block_out, mixed, dense_part, *output_grads = dense_both(1, states, rows_0, None, dense, scalars, pieces_1)
    back_mixed = mixed
    if paired:
        other_terms = [other_keep, links.swap(other_send, Links.CORE)]
        dense_sends, dense_kept = links.dense_across(own_terms, other_terms)
        back_mixed = after(mixed, [values for values, _ in dense_sends])
        dense_terms = links.exchange(dense_sends, dense_kept)

    carries = [nothing, nothing]
    for _ in range(2 if crossing else 1):
        per_set = [
            (outputs[index], kept[index][0], kept[index][2], kept[index][3], carries[index], output_grads[index])
            for index in range(2)
        ]
        carried, first, second, bias_parts, ends = mixer_backward(back_mixed, normed, seq_lengths, scalars, per_set)
        if crossing:
            carries = [chained(ends[index], True) for index in range(2)]
    factors = [f for index in range(2) for f in (carried[index], kept[index][2], kept[index][3], kept[index][0])]
    if paired:
        dense_terms = hold(dense_terms, carried[0])
        along, along_kept = links.dense_along(dense_terms)
        core_sends = after([first[1], second[1]], dense_terms[-3:])
        first = [first[0], links.swap(core_sends[0], Links.CORE)]
        second = [second[0], links.swap(core_sends[1], Links.CORE)]
        sets, tall, wide = first[0].shape
        blocks = ((1, tall, wide), (sets, tall // 2, wide))
        sums = paired_sums((first, second) * 2, blocks * 2, ((1, 0, 0), (0, 1, 0), (0, 0, 0), (0, 0, 0)))
        first, second = ([(sums[0], Links.TENSOR)], [sums[2]]), ([(sums[1], Links.NEAR)], [sums[3]])
        factors[0] = after(factors[0], first[0][0][0], second[0][0][0], [values for values, _ in along])
        first, second = links.exchange(*first), links.exchange(*second)
        dense_terms = links.exchange(along, along_kept)
    input_slope, small = input_backward(
        x_rows, mixed, premix, factors, weights[0][:3] + weights[1][:3], dense_part, bias_parts, scalars
    )

    if paired:
        small = small[None]
        first, second = hold(first, input_slope), hold(second, input_slope)
        dense_terms = dense_terms[:-3] + after(dense_terms[-3:], input_slope)
        small = after(small, first[-1], second[-1], dense_terms[-3:])
        small = total([small, links.swap(small, Links.CORE)])

        def halve_both(first, second, first_bits, second_bits, extra):
            first, first_kept = links.halve(first, first_bits)
            second, second_kept = links.halve(second, second_bits, extra)
            second_send = second[0][0]
            if first_bits == Links.Z_NEAR:
                first_kept, second_kept = ([lax.optimization_barrier(total(kept))] for kept in (first_kept, second_kept))
            first, second = links.exchange(first, first_kept), links.exchange(second, second_kept)
            rows_sent = second_send.shape[1] - extra.shape[1]
            extra = total([extra, second[-1][:, rows_sent:]])
            return first, second[:-1] + [second[-1][:, :rows_sent]], extra

        first, second, small = halve_both(first, second, Links.Z_NEAR, Links.TENSOR, small)
        first, second, small = halve_both(first, second, Links.NEAR, Links.Z_NEAR, small)
        first, second = total(first), total(second)
        count = first.shape[1]
        first_got = links.swap(first, Links.Z_FAR)
        second_got = links.swap(jnp.concatenate([second, small], 1), Links.Z_FAR)
        first, second = total([first, first_got]), total([second, second_got[:, :count]])
        small = total([small, second_got[:, count:]])
        got = links.swap(jnp.concatenate([first, small], 1), Links.NEAR)
        first, small = jnp.concatenate([first, got[:, :count]], 1), total([small, got[:, count:]])
        second = links.grow(second, Links.Z_NEAR)
        first, second = [first, links.swap(first, Links.Z_NEAR)], [second, links.swap(second, Links.NEAR)]
        first += [links.swap(f, Links.CORE) for f in first]
        second += [links.swap(f, Links.CORE) for f in second]
        first, second = [f[0] for f in first], [f[0] for f in second]
        small = small[0].astype(F32)
        dense_sum = total(dense_terms)
    else:
        small = lax.psum(small.astype(F32), ("dp", "tensor"))
        dense_sum = links.dense_sums([own_keep, own_send, other_keep, other_send])
        first, second = links.mixer_sums(first), links.mixer_sums(second)
    dense_sum = dense_sum.astype(F32)
    upper_slope, lower_slope = dense_sum[:hidden].T, dense_sum[hidden:]
    forget_slope, admit_slope, value_slope, output_slope = finish_slopes(first, second, scalars)
    shard = width // (n_dp * n_tensor)
    at = (lax.axis_index("dp") * n_tensor + place) * shard
    premix_slope = lax.dynamic_slice(small, (0, at), (1, shard))[0]
    dense_slope = lax.dynamic_slice(small, (0, width + at), (1, shard))[0]
    bias_slope = lax.dynamic_slice(small, (1, place * own), (1, own))[0]
    return (
        block_out.reshape(rows, width),
        input_slope.reshape(rows, width),
        premix_slope,
        forget_slope,
        admit_slope,
        value_slope,
        bias_slope,
        output_slope,
        dense_slope,
        upper_slope,
        lower_slope,
    )


def solution(mesh):
    placed = (
        P(("dp", "tensor"), None),
        P(("dp", "tensor"), None),
        P("dp", None),
        P(),
        P(None, "tensor"),
        P(None, "tensor"),
        P(None, "tensor"),
        P("tensor"),
        P("tensor", None),
        P(),
        P(None, ("dp", "tensor")),
        P(("dp", "tensor"), None),
    )
    return jax.shard_map(
        on_device,
        mesh=mesh,
        in_specs=placed,
        out_specs=(
            P(("dp", "tensor"), None),
            P(("dp", "tensor"), None),
            P(("dp", "tensor")),
            P(None, "tensor"),
            P(None, "tensor"),
            P(None, "tensor"),
            P("tensor"),
            P("tensor", None),
            P(("dp", "tensor")),
            P(None, ("dp", "tensor")),
            P(("dp", "tensor"), None),
        ),
        check_vma=False,
    )
```

```python
import functools

import jax
import jax.numpy as jnp
from jax import lax
from jax.experimental import pallas as pl
from jax.experimental.pallas import tpu as pltpu
from jax.sharding import PartitionSpec as P

EPSILON = 1e-06
LONGEST = 2048
SEGMENTS = 8
PLACES = 16
STEPS = 64
BLOCK = SEGMENTS * STEPS
GROUP = 32
GELU_SLOPE = 0.7978845608028654
GELU_CUBE = 0.044715
VMEM_BYTES = 56 * 1024 * 1024
F32 = jnp.float32
BF16 = jnp.bfloat16


def in_hbm(values):
    return pltpu.with_memory_space_constraint(values, pltpu.HBM)


def hbm(shape, dtype):
    return pltpu.HBM(shape, dtype)


def dot_nn(left, right):
    return lax.dot_general(left, right, (((1,), (0,)), ((), ())), preferred_element_type=F32)


def dot_nt(left, right):
    return lax.dot_general(left, right, (((1,), (1,)), ((), ())), preferred_element_type=F32)


def row_scale(rows):
    return lax.rsqrt(jnp.mean(rows * rows, -1, keepdims=True) + EPSILON)


def fold_rows(values):
    return jnp.sum(values.reshape(-1, 8, values.shape[-1]), 0)


def put_blocks(values, halves, me, first):
    tall = values.shape[0] // PLACES
    for place in range(PLACES):
        block = pl.multiple_of((place ^ me) * tall, tall)
        there = (place % (PLACES // 2)) * tall
        out = halves[place // (PLACES // 2)]
        out[there : there + tall, first : first + values.shape[1]] = values[pl.ds(block, tall), :].astype(out.dtype)


def interleave(block, scratch):
    lanes = scratch.shape[0]
    for lane in range(lanes):
        for run in range(SEGMENTS):
            part = block[run, :, lane * 128 : (lane + 1) * 128]
            scratch[lane, pl.ds(run, block.shape[1], stride=SEGMENTS), :] = part.astype(F32)
    return jnp.concatenate([scratch[lane] for lane in range(lanes)], -1)


def separate(values, scratch, out):
    lanes = scratch.shape[0]
    for lane in range(lanes):
        scratch[lane] = values[:, lane * 128 : (lane + 1) * 128]
    for run in range(SEGMENTS):
        parts = [scratch[lane, pl.ds(run, out.shape[1], stride=SEGMENTS), :] for lane in range(lanes)]
        out[run] = jnp.concatenate(parts, -1).astype(out.dtype)


def gates(forget_logit, admit_logit):
    top = jnp.maximum(jnp.maximum(-admit_logit, -forget_logit), 0.0)
    one = jnp.exp(-top)
    admit_exp = jnp.exp(-admit_logit - top)
    forget_exp = jnp.exp(-forget_logit - top)
    keep_part = one + admit_exp
    admit_part = one + forget_exp
    total = keep_part + admit_part
    inverse = pl.reciprocal(total, approx=True)
    inverse = inverse * (2.0 - total * inverse)
    keep = keep_part * inverse
    admit = admit_part * inverse
    return keep, admit, keep * (forget_exp * inverse), -admit * (admit_exp * inverse)


def goes_on(lengths_ref, scalars_ref, run, tall):
    place = scalars_ref[0] + run * tall
    begin = jnp.int32(0)
    fresh = False
    for entry in range(lengths_ref.shape[1]):
        length = lengths_ref[0, entry]
        fresh = fresh | ((begin == place) & (length > 0))
        begin = begin + length
    return jnp.where(fresh, 0.0, 1.0).astype(F32)


def product_of_runs(values, masks):
    result = masks[0] * values[0:1]
    for run in range(1, SEGMENTS):
        result = result * (masks[run] * values[run : run + 1])
    return result


def mixer_kernel(first, *refs):
    if first:
        x_ref, gain_ref, *refs = refs
    else:
        normed_in, *refs = refs
    wf, wa, wv, bias, lengths, scalars, carry, *refs = refs
    if first:
        x_out, normed_out, *refs = refs
    admit_out, state_out, forget_fac, admit_fac, ends_out, *refs = refs
    logits, hs, ps, vs, fs, as_, enter, *refs = refs
    phase, block = pl.program_id(0), pl.program_id(1)
    channels = wf.shape[1]
    start = pl.multiple_of(block * BLOCK, BLOCK)

    @pl.when((phase == 0) & (block == 0))
    def _():
        hs[0:8, :] = jnp.zeros((8, channels), F32)
        ps[0:8, :] = jnp.ones((8, channels), F32)

    @pl.when(phase == 0)
    def _():
        if first:
            rows = interleave(x_ref[...], refs[0])
            x_out[...] = rows.astype(BF16)
            normed = (rows * row_scale(rows) * gain_ref[...]).astype(BF16)
            normed_out[...] = normed
        else:
            normed = normed_in[...]
        wide = min(channels, 256)
        chunks = channels // wide
        weights = (wf, wa, wv)

        def project(chunk, kind):
            logits[chunk, kind] = dot_nn(normed, weights[kind][:, chunk * wide : (chunk + 1) * wide])

        def gate(chunk, lane, here, chain):
            inner, cols = slice(lane, lane + 128), slice(chunk * wide + lane, chunk * wide + lane + 128)
            rows = slice(here, here + GROUP)
            there = pl.ds(start + here, GROUP)
            value = logits[chunk, 2, rows, inner]
            keep, admit, forget_side, admit_side = gates(
                logits[chunk, 0, rows, inner], logits[chunk, 1, rows, inner] + bias[:, cols]
            )
            admit_out[rows, cols] = admit.astype(BF16)
            vs[there, cols] = value
            fs[there, cols] = forget_side
            as_[there, cols] = admit_side
            inflow = admit * value
            state, gain = chain
            for step in range(0, GROUP, 8):
                state = keep[step : step + 8] * state + inflow[step : step + 8]
                gain = gain * keep[step : step + 8]
                hs[pl.ds(start + here + step + 8, 8), cols] = state
                ps[pl.ds(start + here + step + 8, 8), cols] = gain
            return state, gain

        for kind in range(3):
            project(0, kind)
        for chunk in range(chunks):
            firsts = range(chunk * wide, (chunk + 1) * wide, 128)
            chains = [(hs[pl.ds(start, 8), c : c + 128], ps[pl.ds(start, 8), c : c + 128]) for c in firsts]
            units = [(here, lane) for here in range(0, BLOCK, GROUP) for lane in range(len(chains))]
            ahead = [(chunk + 1, kind) for kind in range(3)] if chunk + 1 < chunks else []
            for index, (here, lane) in enumerate(units):
                if ahead and index % max(1, len(units) // 3) == 0:
                    project(*ahead.pop(0))
                chains[lane] = gate(chunk, lane * 128, here, chains[lane])
            for item in ahead:
                project(*item)

    @pl.when((phase == 1) & (block == 0))
    def _():
        total = hs.shape[0]
        ends, gains = hs[total - 8 : total, :], ps[total - 8 : total, :]
        masks = [goes_on(lengths, scalars, run, (total - 8) // SEGMENTS) for run in range(SEGMENTS)]
        entering = masks[0] * carry[...]
        enter[0:1] = entering
        for run in range(1, SEGMENTS):
            entering = masks[run] * (ends[run - 1 : run] + gains[run - 1 : run] * entering)
            enter[run : run + 1] = entering
        ends_out[0:1, :] = ends[7:8] + gains[7:8] * enter[7:8, :]
        ends_out[1:2, :] = product_of_runs(gains, masks)
        ends_out[2:8, :] = jnp.zeros((6, channels), F32)

    @pl.when(phase == 1)
    def _():
        def some_rows(group, _):
            here = pl.multiple_of(group * 64, 64)
            there = pl.multiple_of(start + here, 64)
            for lane in range(0, channels, 128):
                cols = pl.ds(lane, 128)
                entering = enter[:, lane : lane + 128]
                states = hs[pl.ds(there, 72), cols].reshape(9, 8, 128) + ps[pl.ds(there, 72), cols].reshape(9, 8, 128) * entering
                states = states.reshape(72, 128)
                state_out[pl.ds(here, 64), cols] = states[8:].astype(BF16)
                change = states[:64] - vs[pl.ds(there, 64), cols]
                forget_fac[pl.ds(here, 64), cols] = (change * fs[pl.ds(there, 64), cols]).astype(BF16)
                admit_fac[pl.ds(here, 64), cols] = (change * as_[pl.ds(there, 64), cols]).astype(BF16)
            return 0

        lax.fori_loop(0, BLOCK // 64, some_rows, 0)


def mixer_forward(first, rows_in, gain, weights, bias, lengths, scalars, carry):
    width = rows_in.shape[-1]
    rows = rows_in.size // width
    channels = weights[0].shape[1]
    blocks = rows // BLOCK
    early = lambda phase, block: (jnp.where(phase == 0, block, blocks - 1), 0)
    late = lambda phase, block: (jnp.where(phase == 0, 0, block), 0)
    whole = lambda phase, block: (0, 0)
    if first:
        in_specs = [
            pl.BlockSpec((SEGMENTS, STEPS, width), lambda phase, block: (0, jnp.where(phase == 0, block, blocks - 1), 0)),
            pl.BlockSpec((1, width), whole),
        ]
        operands = [rows_in.reshape(SEGMENTS, rows // SEGMENTS, width), gain]
        out_specs = [pl.BlockSpec((BLOCK, width), early)] * 2
        out_shape = [hbm((rows, width), BF16)] * 2
    else:
        in_specs, operands = [pl.BlockSpec((BLOCK, width), early)], [rows_in]
        out_specs, out_shape = [], []
    in_specs += [pl.BlockSpec((width, channels), whole)] * 3
    in_specs += [pl.BlockSpec((1, channels), whole)] + [pl.BlockSpec(memory_space=pltpu.SMEM)] * 2 + [pl.BlockSpec((1, channels), whole)]
    out_specs += [pl.BlockSpec((BLOCK, channels), early)] + [pl.BlockSpec((BLOCK, channels), late)] * 3
    out_specs += [pl.BlockSpec((8, channels), whole)]
    out_shape += [hbm((rows, channels), BF16)] * 4
    out_shape += [hbm((8, channels), F32)]
    wide = min(channels, 256)
    scratch = [pltpu.VMEM((channels // wide, 3, BLOCK, wide), F32)]
    scratch += [pltpu.VMEM((rows + 8, channels), F32)] * 2
    scratch += [pltpu.VMEM((rows, channels), F32)] * 3
    scratch += [pltpu.VMEM((8, channels), F32)]
    if first:
        scratch += [pltpu.VMEM((width // 128, BLOCK, 128), F32)]
    return pl.pallas_call(
        functools.partial(mixer_kernel, first),
        grid=(2, blocks),
        in_specs=in_specs,
        out_specs=out_specs,
        out_shape=out_shape,
        scratch_shapes=scratch,
        compiler_params=pltpu.CompilerParams(vmem_limit_bytes=36 * 1024 * 1024, dimension_semantics=("arbitrary", "arbitrary")),
        cost_estimate=pl.CostEstimate(flops=2 * rows * width * 3 * channels, bytes_accessed=rows * channels * 16, transcendentals=4 * rows * channels),
        name="mixer_forward",
    )(in_hbm(operands[0]), *operands[1:], *weights, bias, lengths, scalars, carry)


def dense_kernel(stage, sets, pieces, *refs):
    states, refs = refs[:sets], refs[sets:]
    if stage == 0:
        x_ref, c_ref, *refs = refs
        outs_w, refs = refs[:sets], refs[sets:]
    else:
        middle_ref, sum_ref, delta_ref, dense_ref, cotangent_ref, *refs = refs
    gain_ref, scalars, *refs = refs
    pieces_w, refs = refs[:pieces], refs[pieces:]
    keep_out, send_out, *refs = refs
    if stage == 0:
        middle_out, sum_out, delta_out, dense_out, cotangent_out, upper_acc, lower_acc, cotangent_s = refs
    else:
        out_ref, mixed_ref, slope_ref, *refs = refs
        outputs_ref, refs = refs[:sets], refs[sets:]
        upper_acc, lower_acc, output_acc, out_s = refs
    step = pl.program_id(0)
    gain = gain_ref[...]
    shards, both, width = pieces_w[0].shape
    half = both // 2

    @pl.when(step == 0)
    def _():
        upper_acc[...] = jnp.zeros_like(upper_acc)
        lower_acc[...] = jnp.zeros_like(lower_acc)
        if stage == 1:
            output_acc[...] = jnp.zeros_like(output_acc)
            slope_ref[...] = jnp.zeros_like(slope_ref)

    if stage == 0:
        middle = x_ref[...].astype(F32)
        for state, weight in zip(states, outs_w):
            middle = middle + dot_nn(state[...], weight[...])
        middle_out[...] = middle.astype(BF16)
        dense_in = (middle * row_scale(middle) * gain).astype(BF16)
        dense_out[...] = dense_in
        cotangent = interleave(c_ref[...], cotangent_s).astype(BF16)
        cotangent_out[...] = cotangent
    else:
        dense_in, cotangent = dense_ref[...], cotangent_ref[...]
    dense_t, cotangent_t = dense_in.T, cotangent.T
    joined = max(1, 512 // (shards * half))
    chunks = range(0, pieces, joined)

    def weights(chunk):
        some = pieces_w[chunk : chunk + joined]
        upper_w = jnp.concatenate([w[:, :half, :].reshape(shards * half, width) for w in some], 0)
        return upper_w, jnp.concatenate([w[:, half:, :].reshape(shards * half, width) for w in some], 0)

    def bend(upper):
        square = upper * upper
        bell = 0.5 + 0.5 * jnp.tanh(upper * (GELU_SLOPE + GELU_SLOPE * GELU_CUBE * square))
        active = upper * bell
        slope = bell + active * (1.0 - bell) * (2.0 * GELU_SLOPE + 6.0 * GELU_SLOPE * GELU_CUBE * square)
        return active.astype(BF16), slope

    def gather(chunk, active, upper_delta):
        cols = slice(chunk * shards * half, (chunk + joined) * shards * half)
        lower_acc[:, cols] += dot_nn(cotangent_t, active)
        upper_acc[:, cols] += dot_nn(dense_t, upper_delta)

    fed, delta, behind = None, None, None
    upper_w, lower_w = weights(0)
    upper, back = dot_nt(dense_in, upper_w), dot_nt(cotangent, lower_w)
    for chunk in chunks:
        following = chunk + joined
        if following < pieces:
            next_upper_w, next_lower_w = weights(following)
            next_upper = dot_nt(dense_in, next_upper_w)
        active, slope = bend(upper)
        upper_delta = (slope * back).astype(BF16)
        if following < pieces:
            next_back = dot_nt(cotangent, next_lower_w)
        if behind is not None:
            gather(*behind)
        fed_part, delta_part = dot_nn(active, lower_w), dot_nn(upper_delta, upper_w)
        fed = fed_part if fed is None else fed + fed_part
        delta = delta_part if delta is None else delta + delta_part
        behind = chunk, active, upper_delta
        if following < pieces:
            upper_w, lower_w, upper, back = next_upper_w, next_lower_w, next_upper, next_back
    gather(*behind)
    if stage == 0:
        sum_out[...] = (middle + fed).astype(BF16)
        delta_out[...] = delta.astype(BF16)
    else:
        separate(sum_ref[...].astype(F32) + fed, out_s, out_ref)
        middle = middle_ref[...].astype(F32)
        scale = row_scale(middle)
        delta = delta_ref[...].astype(F32) + delta
        slope_ref[...] += fold_rows(delta * middle * scale)
        scaled = delta * gain
        inner = jnp.mean(scaled * middle, -1, keepdims=True)
        mixed = (cotangent.astype(F32) + scale * (scaled - middle * (scale * scale * inner))).astype(BF16)
        mixed_ref[...] = mixed
        mixed_t = mixed.T
        channels = states[0].shape[1]
        for index, state in enumerate(states):
            output_acc[:, index * channels : (index + 1) * channels] += dot_nn(mixed_t, state[...])

    @pl.when(step == pl.num_programs(0) - 1)
    def _():
        for shard in range(0, pieces * shards, 2):
            cols = slice(shard * half, (shard + 2) * half)
            out = keep_out if shard < pieces * shards // 2 else send_out
            there = shard % (pieces * shards // 2)
            out[there : there + 2, :half, :] = upper_acc[:, cols].T.astype(BF16).reshape(2, half, width)
            out[there : there + 2, half:, :] = lower_acc[:, cols].T.astype(BF16).reshape(2, half, width)
        if stage == 1:
            slope_ref[0:1, :] = jnp.sum(slope_ref[...], 0, keepdims=True)
            tall = output_acc.shape[0] // PLACES
            for index, output in enumerate(outputs_ref):
                for place in range(PLACES):
                    there = pl.multiple_of((place ^ scalars[2]) * tall, tall)
                    output[place * tall : (place + 1) * tall, :] = output_acc[
                        pl.ds(there, tall), index * channels : (index + 1) * channels
                    ].astype(BF16)


def dense_both(stage, states, entering, output_weights, gain, scalars, pieces):
    rows, channels = states[0].shape
    width = gain.shape[1]
    shards, both, _ = pieces[0].shape
    hidden = len(pieces) * shards * both // 2
    sets = len(states)
    tall = min(rows, 512)
    by_rows = lambda block: (block, 0)
    whole = lambda block: (0, 0)
    runs_spec = pl.BlockSpec((SEGMENTS, tall // SEGMENTS, width), lambda block: (0, block, 0))
    runs_shape = (SEGMENTS, rows // SEGMENTS, width)
    row_spec = pl.BlockSpec((tall, width), by_rows)
    grads = (len(pieces) * shards // 2, both, width)
    in_specs = [pl.BlockSpec((tall, channels), by_rows)] * sets
    out_specs = [pl.BlockSpec(grads, lambda block: (0, 0, 0))] * 2
    out_shape = [hbm(grads, BF16)] * 2
    scratch = [pltpu.VMEM((width, hidden), F32)] * 2
    if stage == 0:
        in_specs += [row_spec, runs_spec] + [pl.BlockSpec((channels, width), whole)] * sets
        entering = [entering[0], entering[1].reshape(runs_shape), *output_weights]
        out_specs += [row_spec] * 5
        out_shape += [hbm((rows, width), BF16)] * 5
    else:
        in_specs += [row_spec] * 5
        out_specs += [runs_spec, row_spec, pl.BlockSpec((8, width), whole)] + [pl.BlockSpec((width, channels), whole)] * sets
        out_shape += [hbm(runs_shape, BF16), hbm((rows, width), BF16)]
        out_shape += [hbm((8, width), F32)] + [hbm((width, channels), BF16)] * sets
        scratch += [pltpu.VMEM((width, sets * channels), F32)]
    scratch += [pltpu.VMEM((width // 128, tall, 128), F32)]
    in_specs += [pl.BlockSpec((1, width), whole), pl.BlockSpec(memory_space=pltpu.SMEM)]
    in_specs += [pl.BlockSpec((shards, both, width), lambda block: (0, 0, 0))] * len(pieces)
    return pl.pallas_call(
        functools.partial(dense_kernel, stage, sets, len(pieces)),
        grid=(rows // tall,),
        in_specs=in_specs,
        out_specs=out_specs,
        out_shape=out_shape,
        scratch_shapes=scratch,
        compiler_params=pltpu.CompilerParams(vmem_limit_bytes=44 * 1024 * 1024, dimension_semantics=("arbitrary",)),
        cost_estimate=pl.CostEstimate(flops=12 * rows * width * hidden, bytes_accessed=rows * width * 24, transcendentals=rows * hidden),
        name="dense_first" if stage == 0 else "dense_second",
    )(*[in_hbm(v) for v in states], *[in_hbm(v) if v.shape[0] != channels else v for v in entering], gain, scalars, *pieces)


def mixer_back_kernel(sets, mixed_ref, normed_ref, lengths, scalars, *refs):
    per_set = [refs[index * 6 : index * 6 + 6] for index in range(sets)]
    refs = refs[6 * sets :]
    carried_out, refs = refs[:sets], refs[sets:]
    first_out, second_out, refs = refs[:2], refs[2:4], refs[4:]
    bias_out, ends_out, *refs = refs
    cs, ps, state_delta, admits, deltas, slopes_acc, last, enter = refs
    phase, block = pl.program_id(0), pl.program_id(1)
    blocks = pl.num_programs(1)
    channels = per_set[0][1].shape[1]
    place = jnp.where(phase == 0, blocks - 1 - block, block)
    start = pl.multiple_of(place * BLOCK, BLOCK)

    @pl.when((phase == 0) & (block == 0))
    def _():
        last[:, 0:8, :] = jnp.zeros((sets, 8, channels), F32)
        last[:, 8:16, :] = jnp.ones((sets, 8, channels), F32)

    @pl.when(phase == 0)
    def _():
        def arrive(index):
            state_delta[index] = dot_nt(mixed_ref[...], per_set[index][0][...])

        arrive(0)
        for index in range(sets):
            admit_ref = per_set[index][1]
            for lane in range(0, channels, 128):
                if lane == 0 and index + 1 < sets:
                    arrive(index + 1)
                cols = slice(lane, lane + 128)
                kept, gain = last[index, 0:8, cols], last[index, 8:16, cols]
                for here in range(BLOCK - 16, -1, -16):
                    admit = admit_ref[here : here + 16, cols]
                    admits[index, pl.ds(start + here, 16), cols] = admit
                    keep = 1.0 - admit.astype(F32)
                    for step in (8, 0):
                        carried = state_delta[index, here + step : here + step + 8, cols] + kept
                        cs[index, pl.ds(start + here + step, 8), cols] = carried
                        ps[index, pl.ds(start + here + step, 8), cols] = gain
                        kept = keep[step : step + 8] * carried
                        gain = keep[step : step + 8] * gain
                last[index, 0:8, cols] = kept
                last[index, 8:16, cols] = gain

    @pl.when((phase == 1) & (block == 0))
    def _():
        masks = [goes_on(lengths, scalars, run, cs.shape[1] // SEGMENTS) for run in range(SEGMENTS)]
        for index in range(sets):
            kept, gain = last[index, 0:8, :], last[index, 8:16, :]
            entering = per_set[index][4][...]
            enter[index, 7:8, :] = entering
            for run in range(SEGMENTS - 1, 0, -1):
                entering = masks[run] * (kept[run : run + 1] + gain[run : run + 1] * entering)
                enter[index, run - 1 : run, :] = entering
            ends_out[index, 0:1, :] = masks[0] * (kept[0:1] + gain[0:1] * entering)
            ends_out[index, 1:2, :] = product_of_runs(gain, masks)
            ends_out[index, 2:8, :] = jnp.zeros((6, channels), F32)
        bias_out[...] = jnp.zeros_like(bias_out)
        slopes_acc[...] = jnp.zeros_like(slopes_acc)

    @pl.when(phase == 1)
    def _():
        normed_t = normed_ref[...].T
        wide = min(channels, 256)
        chunks = [(index, first) for index in range(sets) for first in range(0, channels, wide)]

        def move(index, lane, here):
            _, _, forget_fac, admit_fac, _, _ = per_set[index]
            cols = slice(lane, lane + 128)
            rows, there = slice(here, here + GROUP), pl.ds(start + here, GROUP)
            gains = ps[index, there, cols].reshape(GROUP // 8, 8, 128)
            carried = (cs[index, there, cols].reshape(GROUP // 8, 8, 128) + gains * enter[index, :, cols]).reshape(GROUP, 128)
            carried_out[index][rows, cols] = carried.astype(BF16)
            admit_delta = (carried * admit_fac[rows, cols].astype(F32)).astype(BF16)
            deltas[index, 0, rows, cols] = (carried * forget_fac[rows, cols].astype(F32)).astype(BF16)
            deltas[index, 1, rows, cols] = admit_delta
            deltas[index, 2, rows, cols] = (carried * admits[index, there, cols].astype(F32)).astype(BF16)
            return fold_rows(admit_delta.astype(F32))

        def reduce(index, first, kind):
            cols = slice(first, first + wide)
            slopes_acc[index, kind, :, cols] += dot_nn(normed_t, deltas[index, kind, :, cols])

        behind = []
        for index, first in chunks:
            lanes = range(first, first + wide, 128)
            biases = [jnp.zeros((8, 128), F32) for _ in lanes]
            units = [(here, which) for here in range(0, BLOCK, GROUP) for which in range(len(lanes))]
            for position, (here, which) in enumerate(units):
                if behind and position % max(1, len(units) // 3) == 0:
                    reduce(*behind.pop(0))
                biases[which] = biases[which] + move(index, lanes[which], here)
            for lane, bias in zip(lanes, biases):
                bias_out[index, :, lane : lane + 128] += bias
            for item in behind:
                reduce(*item)
            behind = [(index, first, kind) for kind in range(3)]
        for item in behind:
            reduce(*item)
        for index in range(sets):
            output_grads = per_set[index][5]
            tall = output_grads.shape[0]
            turns = cs.shape[1] // BLOCK
            for half in range(2):
                if turns == 1:
                    second_out[half][index, :, channels:] = output_grads[half * (tall // 2) : (half + 1) * (tall // 2), :]
                    continue

                @pl.when(block // (turns // 2) == half)
                def _():
                    there = pl.multiple_of(block % (turns // 2) * tall, tall)
                    second_out[half][index, pl.ds(there, tall), channels:] = output_grads[...]

    @pl.when((phase == 1) & (block == blocks - 1))
    def _():
        for index in range(sets):
            bias_out[index, 0:1, :] = jnp.sum(bias_out[index], 0, keepdims=True)
            put_blocks(slopes_acc.at[index, 0], [out.at[index] for out in first_out], scalars[1], 0)
            put_blocks(slopes_acc.at[index, 1], [out.at[index] for out in first_out], scalars[1], channels)
            put_blocks(slopes_acc.at[index, 2], [out.at[index] for out in second_out], scalars[2], 0)


def mixer_backward(mixed, normed, lengths, scalars, per_set):
    rows, width = mixed.shape
    sets = len(per_set)
    channels = per_set[0][1].shape[1]
    blocks = rows // BLOCK
    back = lambda phase, block: (jnp.where(phase == 0, blocks - 1 - block, 0), 0)
    late = lambda phase, block: (jnp.where(phase == 0, 0, block), 0)
    whole = lambda phase, block: (0, 0)
    all3 = lambda phase, block: (0, 0, 0)
    set_specs = [
        pl.BlockSpec((channels, width), whole),
        pl.BlockSpec((BLOCK, channels), back),
        pl.BlockSpec((BLOCK, channels), late),
        pl.BlockSpec((BLOCK, channels), late),
        pl.BlockSpec((1, channels), whole),
        pl.BlockSpec((width // blocks, channels), late),
    ]
    results = pl.pallas_call(
        functools.partial(mixer_back_kernel, sets),
        grid=(2, blocks),
        in_specs=[
            pl.BlockSpec((BLOCK, width), back),
            pl.BlockSpec((BLOCK, width), late),
            pl.BlockSpec(memory_space=pltpu.SMEM),
            pl.BlockSpec(memory_space=pltpu.SMEM),
        ]
        + set_specs * sets,
        out_specs=[pl.BlockSpec((BLOCK, channels), late)] * sets
        + [pl.BlockSpec((sets, width // 2, 2 * channels), all3)] * 4
        + [pl.BlockSpec((sets, 8, channels), all3)] * 2,
        out_shape=[jax.ShapeDtypeStruct((rows, channels), BF16)] * sets
        + [jax.ShapeDtypeStruct((sets, width // 2, 2 * channels), BF16)] * 4
        + [jax.ShapeDtypeStruct((sets, 8, channels), F32)] * 2,
        scratch_shapes=[
            pltpu.VMEM((sets, rows, channels), F32),
            pltpu.VMEM((sets, rows, channels), F32),
            pltpu.VMEM((sets, BLOCK, channels), F32),
            pltpu.VMEM((sets, rows, channels), BF16),
            pltpu.VMEM((sets, 3, BLOCK, channels), BF16),
            pltpu.VMEM((sets, 3, width, channels), F32),
            pltpu.VMEM((sets, 16, channels), F32),
            pltpu.VMEM((sets, 8, channels), F32),
        ],
        compiler_params=pltpu.CompilerParams(vmem_limit_bytes=50 * 1024 * 1024, dimension_semantics=("arbitrary", "arbitrary")),
        cost_estimate=pl.CostEstimate(flops=2 * rows * width * 4 * channels * sets, bytes_accessed=rows * channels * 12 * sets, transcendentals=0),
        name="mixer_backward",
    )(in_hbm(mixed), in_hbm(normed), lengths, scalars, *[in_hbm(item) if item.shape[0] == rows else item for one in per_set for item in one])
    return results[:sets], results[sets : sets + 2], results[sets + 2 : sets + 4], *results[sets + 4 :]


def input_kernel(sets, *refs):
    x_ref, mixed_ref, gain_ref, *refs = refs
    factors, refs = refs[: 4 * sets], refs[4 * sets :]
    weights, refs = refs[: 3 * sets], refs[3 * sets :]
    dense_ref, bias_ref, scalars, out_ref, small_ref, slope_ref, out_s = refs

    @pl.when(pl.program_id(0) == 0)
    def _():
        slope_ref[...] = jnp.zeros_like(slope_ref)

    normed_delta = None
    for index in range(sets):
        carried = factors[4 * index][...].astype(F32)
        for part in range(3):
            delta = (carried * factors[4 * index + 1 + part][...].astype(F32)).astype(BF16)
            term = dot_nt(delta, weights[3 * index + part][...])
            normed_delta = term if normed_delta is None else normed_delta + term
    rows = x_ref[...].astype(F32)
    scale = row_scale(rows)
    slope_ref[...] += fold_rows(normed_delta * rows * scale)
    scaled = normed_delta * gain_ref[...]
    inner = jnp.mean(scaled * rows, -1, keepdims=True)
    result = mixed_ref[...].astype(F32) + scale * (scaled - rows * (scale * scale * inner))
    separate(result, out_s, out_ref)

    @pl.when(pl.program_id(0) == pl.num_programs(0) - 1)
    def _():
        gains = jnp.concatenate([jnp.sum(slope_ref[...], 0, keepdims=True), dense_ref[0:1, :]], 1)
        low = jnp.where(scalars[3] == 0, bias_ref[0, 0:1, :], bias_ref[1, 0:1, :])
        high = jnp.where(scalars[3] == 0, bias_ref[1, 0:1, :], bias_ref[0, 0:1, :])
        biases = jnp.concatenate([low, high], 1)
        rest = jnp.zeros((small_ref.shape[0] - 2, biases.shape[1]), F32)
        small_ref[...] = jnp.concatenate([gains, biases, rest], 0).astype(BF16)


def input_backward(x_rows, mixed, gain, factors, weights, dense_part, bias_parts, scalars):
    rows, width = x_rows.shape
    sets = len(factors) // 4
    channels = weights[0].shape[1]
    by_rows = lambda block: (block, 0)
    whole = lambda block: (0, 0)
    return pl.pallas_call(
        functools.partial(input_kernel, sets),
        grid=(rows // BLOCK,),
        in_specs=[pl.BlockSpec((BLOCK, width), by_rows)] * 2
        + [pl.BlockSpec((1, width), whole)]
        + [pl.BlockSpec((BLOCK, channels), by_rows)] * (4 * sets)
        + [pl.BlockSpec((width, channels), whole)] * (3 * sets)
        + [pl.BlockSpec((8, width), whole), pl.BlockSpec((sets, 8, channels), lambda block: (0, 0, 0)), pl.BlockSpec(memory_space=pltpu.SMEM)],
        out_specs=[pl.BlockSpec((SEGMENTS, STEPS, width), lambda block: (0, block, 0)), pl.BlockSpec((16, sets * channels), whole)],
        out_shape=[hbm((SEGMENTS, rows // SEGMENTS, width), F32), jax.ShapeDtypeStruct((16, sets * channels), BF16)],
        scratch_shapes=[pltpu.VMEM((8, width), F32), pltpu.VMEM((width // 128, BLOCK, 128), F32)],
        compiler_params=pltpu.CompilerParams(vmem_limit_bytes=34 * 1024 * 1024, dimension_semantics=("arbitrary",)),
        cost_estimate=pl.CostEstimate(flops=2 * rows * width * 3 * channels * sets, bytes_accessed=rows * channels * 8 * sets, transcendentals=0),
        name="input_backward",
    )(in_hbm(x_rows), in_hbm(mixed), gain, *[in_hbm(f) for f in factors], *weights, dense_part, bias_parts, scalars)


def finish_kernel(channels, count, *refs):
    first_refs, second_refs = refs[:count], refs[count : 2 * count]
    scalars, forget_out, admit_out, value_out, output_out, scratch = refs[2 * count :]
    tall = scratch.shape[0] // PLACES
    each = PLACES // count
    for place in range(PLACES):
        here = slice(place % each * tall, (place % each + 1) * tall)
        for index, (sums, outs) in enumerate(((first_refs, (forget_out, admit_out)), (second_refs, (value_out, scratch)))):
            there = pl.multiple_of((place ^ scalars[1 + index]) * tall, tall)
            piece = sums[place // each]
            outs[0][pl.ds(there, tall), :] = piece[here, :channels].astype(F32)
            outs[1][pl.ds(there, tall), :] = piece[here, channels:].astype(F32)
    output_out[...] = scratch[...].T


def finish_slopes(first, second, scalars):
    count = len(first)
    width, channels = count * first[0].shape[0], first[0].shape[1] // 2
    return pl.pallas_call(
        functools.partial(finish_kernel, channels, count),
        in_specs=[pl.BlockSpec(memory_space=pltpu.VMEM)] * (2 * count) + [pl.BlockSpec(memory_space=pltpu.SMEM)],
        out_shape=[jax.ShapeDtypeStruct((width, channels), F32)] * 3 + [jax.ShapeDtypeStruct((channels, width), F32)],
        scratch_shapes=[pltpu.VMEM((width, channels), F32)],
        compiler_params=pltpu.CompilerParams(vmem_limit_bytes=VMEM_BYTES),
        name="finish_slopes",
    )(*first, *second, scalars)


def regroup(stacked, half):
    count, both, width = stacked.shape
    if both == 2 * half:
        return stacked
    arrays = jnp.moveaxis(stacked.reshape(count, 2, both // 2, width), 1, 0).reshape(2, -1, half, width)
    return jnp.moveaxis(arrays, 0, 1).reshape(-1, 2 * half, width)


def after(values, *earlier):
    return lax.optimization_barrier((values, earlier))[0]


def total(terms):
    result = terms[0].astype(F32)
    for term in terms[1:]:
        result = result + term.astype(F32)
    return result.astype(terms[0].dtype)


def sum_kernel(*refs):
    count = len(refs) // 3
    for index in range(count):
        left, right, out = refs[2 * index], refs[2 * index + 1], refs[2 * count + index]
        out[...] = (left[...].astype(F32) + right[...].astype(F32)).astype(BF16)


def paired_sums(pairs, blocks, places):
    specs = [pl.BlockSpec(block, functools.partial(lambda place, step: place, place)) for block, place in zip(blocks, places)]
    return pl.pallas_call(
        sum_kernel,
        grid=(1,),
        in_specs=[spec for spec in specs for _ in range(2)],
        out_specs=[pl.BlockSpec(block, lambda step: (0, 0, 0)) for block in blocks],
        out_shape=[jax.ShapeDtypeStruct(block, BF16) for block in blocks],
        compiler_params=pltpu.CompilerParams(vmem_limit_bytes=VMEM_BYTES),
        name="paired_sums",
    )(*[item for pair in pairs for item in pair])


def hold(terms, *earlier):
    return terms[:-1] + [after(terms[-1], *earlier)]


def part(terms, index, axis):
    half = terms[0].shape[axis] // 2
    return [lax.slice_in_dim(t, index * half, (index + 1) * half, axis=axis) for t in terms]


def pack_kernel(*refs):
    mine_out, output_out = refs[5:]
    for index, ref in enumerate(refs[1:4]):
        mine_out[index] = ref[...]
    output_out[...] = refs[4][...]


def pack_halves(weights, half):
    tall, wide = weights[0].shape[0] // 2, weights[0].shape[1]
    return pl.pallas_call(
        pack_kernel,
        grid_spec=pltpu.PrefetchScalarGridSpec(
            num_scalar_prefetch=1,
            grid=(1,),
            in_specs=[pl.BlockSpec((tall, wide), lambda step, half: (half[0], 0))] * 4,
            out_specs=[pl.BlockSpec((3, tall, wide), lambda step, half: (0, 0, 0)), pl.BlockSpec((tall, wide), lambda step, half: (0, 0))],
        ),
        out_shape=[jax.ShapeDtypeStruct((3, tall, wide), BF16), jax.ShapeDtypeStruct((tall, wide), BF16)],
        name="pack_halves",
    )(jnp.reshape(half, (1,)).astype(jnp.int32), *weights)


class Links:
    TENSOR, CORE, NEAR, Z_NEAR, Z_FAR = 1, 2, 4, 8, 16

    def __init__(self):
        dp = lax.axis_index("dp")
        core, near, z_near = dp % 2, dp // 2 % 2, dp // 4 % 2
        self.core = core
        self.me = [core * 8 + z_near * 4 + near * 2, core * 8 + near * 4 + z_near * 2]

    def swap(self, values, bits):
        pairs = [(device, device ^ bits) for device in range(32)]
        return lax.ppermute(values, ("dp", "tensor"), pairs)

    def begin_weights(self, own_weights):
        mine, mine_output = pack_halves(own_weights, self.core)
        return mine, mine_output, self.swap(mine, self.TENSOR)

    def end_weights(self, got):
        rest = self.swap(got, self.CORE)
        lower = self.core == 0
        return jnp.concatenate([jnp.where(lower, got, rest), jnp.where(lower, rest, got)], -2)

    def begin_dense(self, shard):
        return [shard] + [self.swap(shard, bits) for bits in (self.Z_NEAR, self.Z_FAR, self.Z_NEAR | self.Z_FAR)]

    def dense_pieces(self, pieces):
        own = jnp.stack(pieces)
        return own, self.swap(own, self.NEAR), self.swap(own, self.CORE)

    def dense_across(self, own_terms, other_terms):
        pick = lambda terms, near: total([t[near * 4 : near * 4 + 4] for t in terms])
        sends = [(pick(other_terms, 0), self.TENSOR), (pick(own_terms, 1), self.NEAR), (pick(other_terms, 1), self.TENSOR | self.NEAR)]
        return sends, [t[:4] for t in own_terms]

    def dense_along(self, terms):
        sends = []
        for index, bits in ((1, self.Z_NEAR), (2, self.Z_FAR), (3, self.Z_NEAR | self.Z_FAR)):
            sends.append((total([t[index] for t in terms]), bits))
        return sends, [t[0] for t in terms]

    def exchange(self, sends, kept):
        return kept + [self.swap(values, bits) for values, bits in sends]

    def halve(self, terms, bits, extra=None):
        axis = 0 if bits == self.TENSOR else 1
        send = total(part(terms, 1, axis))
        if extra is not None:
            send = jnp.concatenate([send, extra], 1)
        return [(send, bits)], part(terms, 0, axis)

    def grow(self, values, bits):
        return jnp.concatenate([values, self.swap(values, bits)], 1)


class Plain:
    def __init__(self, n_tensor, own, hidden):
        self.n_tensor, self.own, self.hidden = n_tensor, own, hidden
        self.me = [0, 0]

    def weights(self, own_weights):
        whole = [lax.all_gather(w, "tensor", axis=1, tiled=True) for w in own_weights[:3]]
        pairs = [jnp.split(w, 2, 1) for w in whole]
        pairs.append(jnp.split(lax.all_gather(own_weights[3], "tensor", axis=0, tiled=True), 2, 0))
        return [p[0] for p in pairs], [p[1] for p in pairs]

    def bias(self, own_bias):
        return tuple(jnp.split(lax.all_gather(own_bias, "tensor", axis=0, tiled=True), 2))

    def dense(self, shard):
        whole = regroup(lax.all_gather(shard, ("dp", "tensor"), axis=0), 64)
        pieces = [whole[first : first + 4] for first in range(0, whole.shape[0], 4)]
        return pieces[: len(pieces) // 2], pieces[len(pieces) // 2 :]

    def dense_sums(self, grads):
        whole = regroup(jnp.concatenate(grads, 0), self.hidden)
        return lax.psum_scatter(whole, ("dp", "tensor"), scatter_dimension=0, tiled=True)[0]

    def mixer_sums(self, grads):
        grads = jnp.concatenate(grads, 1)
        _, width, columns = grads.shape
        whole = jnp.moveaxis(grads.reshape(2, width, 2, columns // 2), 0, 2).reshape(width, 2, columns)
        part = lax.psum_scatter(whole, "tensor", scatter_dimension=2, tiled=True)
        return jnp.split(lax.psum(part, "dp").reshape(width, 2 * self.own), 2, 0)

def on_device(
    block_in,
    out_cotangent,
    seq_lengths,
    premix_gain,
    forget_weight,
    admit_weight,
    value_weight,
    admit_bias,
    output_weight,
    dense_gain,
    upper_weight,
    lower_weight,
):
    n_dp, n_tensor = lax.axis_size("dp"), lax.axis_size("tensor")
    rows, width = block_in.shape
    place = lax.axis_index("tensor")
    own = forget_weight.shape[1]
    premix = premix_gain.astype(F32)[None]
    dense = dense_gain.astype(F32)[None]
    paired = (n_dp, n_tensor) == (16, 2)
    hidden = lower_weight.shape[0]
    links = Links() if paired else Plain(n_tensor, own, hidden)
    scalars = jnp.stack([place * rows] + links.me + [place if paired else 0]).astype(jnp.int32)
    own_weights = [forget_weight, admit_weight, value_weight, output_weight]
    dense_shard = jnp.concatenate([upper_weight.T, lower_weight], 0)
    if paired:
        weights, biases = [own_weights], [admit_bias]
        channels = own
        mine, mine_output, got = links.begin_weights(own_weights)
        pieces = links.begin_dense(after(dense_shard, mine))
        biases.append(links.swap(after(admit_bias, pieces[0]), Links.TENSOR))
    else:
        weights, biases = links.weights(own_weights), links.bias(admit_bias)
        channels = weights[0][0].shape[1]
    crossing = rows % LONGEST != 0
    nothing = jnp.zeros((1, channels), F32)

    def chained(ends, backwards):
        every = lax.all_gather(ends, "tensor", axis=0)
        entering = jnp.zeros_like(ends[0:1])
        mine = entering
        order = range(n_tensor - 1, -1, -1) if backwards else range(n_tensor)
        for index in order:
            mine = jnp.where(place == index, entering, mine)
            entering = every[index, 0:1] + every[index, 1:2] * entering
        return mine

    def forward(first, rows_in, index):
        carry = nothing
        args = (first, rows_in, premix, weights[index][:3], biases[index].astype(F32)[None], seq_lengths, scalars)
        if crossing:
            carry = chained(mixer_forward(*args, carry)[-1], False)
        return mixer_forward(*args, carry)

    x_rows, normed, *kept_0 = forward(True, block_in, 0)
    if paired:
        got, pieces, biases[1] = after((got, pieces, biases[1]), normed)
        got_output = links.swap(after(mine_output, got), Links.TENSOR)
        own_four, near_four, own_rest = links.dense_pieces(pieces)
        other_weights = links.end_weights(got)
        weights.append([other_weights[index] for index in range(3)])
    kept_1 = forward(False, normed, 1)
    kept = [kept_0, kept_1]
    if paired:
        near_four, held_four = after((near_four, own_four), kept_1[1])
        weights[1].append(links.end_weights(after(got_output, kept_1[1])))
        other_four = links.swap(held_four, Links.TENSOR)
        far_four = links.swap(held_four, Links.TENSOR | Links.NEAR)
        pieces_0 = [own_four, near_four, own_rest, links.swap(near_four, Links.CORE)]
    else:
        pieces_0, pieces_1 = links.dense(dense_shard)
    outputs = [w[3] for w in weights]
    states = [k[1] for k in kept]
    own_keep, own_send, *rows_0 = dense_both(0, states, (x_rows, out_cotangent), outputs, dense, scalars, pieces_0)
    if paired:
        far_four, other_four = after((far_four, other_four), rows_0[0])
        pieces_1 = [other_four, far_four, links.swap(other_four, Links.CORE), links.swap(far_four, Links.CORE)]
        own_terms = [own_keep, links.swap(after(own_send, pieces_1), Links.CORE)]
    other_keep, other_send, block_out, mixed, dense_part, *output_grads = dense_both(1, states, rows_0, None, dense, scalars, pieces_1)
    back_mixed = mixed
    if paired:
        own_terms[1] = after(own_terms[1], mixed)
        other_terms = [other_keep, links.swap(after(other_send, own_terms[1]), Links.CORE)]
        dense_sends, dense_kept = links.dense_across(own_terms, other_terms)
        back_mixed = after(mixed, [values for values, _ in dense_sends])
        dense_terms = links.exchange(dense_sends, dense_kept)

    carries = [nothing, nothing]
    for _ in range(2 if crossing else 1):
        per_set = [
            (outputs[index], kept[index][0], kept[index][2], kept[index][3], carries[index], output_grads[index])
            for index in range(2)
        ]
        carried, first, second, bias_parts, ends = mixer_backward(back_mixed, normed, seq_lengths, scalars, per_set)
        if crossing:
            carries = [chained(ends[index], True) for index in range(2)]
    factors = [f for index in range(2) for f in (carried[index], kept[index][2], kept[index][3], kept[index][0])]
    if paired:
        dense_terms = hold(dense_terms, carried[0])
        along, along_kept = links.dense_along(dense_terms)
        core_sends = after([first[1], second[1]], dense_terms[-3:])
        first = [first[0], links.swap(core_sends[0], Links.CORE)]
        second = [second[0], links.swap(core_sends[1], Links.CORE)]
        sets, tall, wide = first[0].shape
        blocks = ((1, tall, wide), (sets, tall // 2, wide))
        sums = paired_sums((first, second) * 2, blocks * 2, ((1, 0, 0), (0, 1, 0), (0, 0, 0), (0, 0, 0)))
        first, second = ([(sums[0], Links.TENSOR)], [sums[2]]), ([(sums[1], Links.NEAR)], [sums[3]])
        factors[0] = after(factors[0], first[0][0][0], second[0][0][0], [values for values, _ in along])
        first, second = links.exchange(*first), links.exchange(*second)
        dense_terms = links.exchange(along, along_kept)
    input_slope, small = input_backward(
        x_rows, mixed, premix, factors, weights[0][:3] + weights[1][:3], dense_part, bias_parts, scalars
    )

    if paired:
        small = small[None]
        first, second = hold(first, input_slope), hold(second, input_slope)
        dense_terms = dense_terms[:-3] + after(dense_terms[-3:], input_slope)
        small = after(small, first[-1], second[-1], dense_terms[-3:])
        small = total([small, links.swap(small, Links.CORE)])

        def halve_both(first, second, first_bits, second_bits, extra):
            first, first_kept = links.halve(first, first_bits)
            second, second_kept = links.halve(second, second_bits, extra)
            second_send = second[0][0]
            if first_bits == Links.Z_NEAR:
                first_kept, second_kept = ([lax.optimization_barrier(total(kept))] for kept in (first_kept, second_kept))
            first, second = links.exchange(first, first_kept), links.exchange(second, second_kept)
            rows_sent = second_send.shape[1] - extra.shape[1]
            extra = total([extra, second[-1][:, rows_sent:]])
            return first, second[:-1] + [second[-1][:, :rows_sent]], extra

        first, second, small = halve_both(first, second, Links.Z_NEAR, Links.TENSOR, small)
        first, second, small = halve_both(first, second, Links.NEAR, Links.Z_NEAR, small)
        first, second = total(first), total(second)
        count = first.shape[1]
        first_got = links.swap(first, Links.Z_FAR)
        second_got = links.swap(jnp.concatenate([second, small], 1), Links.Z_FAR)
        first, second = total([first, first_got]), total([second, second_got[:, :count]])
        small = total([small, second_got[:, count:]])
        got = links.swap(jnp.concatenate([first, small], 1), Links.NEAR)
        first, small = jnp.concatenate([first, got[:, :count]], 1), total([small, got[:, count:]])
        second = links.grow(second, Links.Z_NEAR)
        first, second = [first, links.swap(first, Links.Z_NEAR)], [second, links.swap(second, Links.NEAR)]
        first += [links.swap(f, Links.CORE) for f in first]
        second += [links.swap(f, Links.CORE) for f in second]
        first, second = [f[0] for f in first], [f[0] for f in second]
        small = small[0].astype(F32)
        dense_sum = total(dense_terms)
    else:
        small = lax.psum(small.astype(F32), ("dp", "tensor"))
        dense_sum = links.dense_sums([own_keep, own_send, other_keep, other_send])
        first, second = links.mixer_sums(first), links.mixer_sums(second)
    dense_sum = dense_sum.astype(F32)
    upper_slope, lower_slope = dense_sum[:hidden].T, dense_sum[hidden:]
    forget_slope, admit_slope, value_slope, output_slope = finish_slopes(first, second, scalars)
    shard = width // (n_dp * n_tensor)
    at = (lax.axis_index("dp") * n_tensor + place) * shard
    premix_slope = lax.dynamic_slice(small, (0, at), (1, shard))[0]
    dense_slope = lax.dynamic_slice(small, (0, width + at), (1, shard))[0]
    bias_slope = lax.dynamic_slice(small, (1, place * own), (1, own))[0]
    return (
        block_out.reshape(rows, width),
        input_slope.reshape(rows, width),
        premix_slope,
        forget_slope,
        admit_slope,
        value_slope,
        bias_slope,
        output_slope,
        dense_slope,
        upper_slope,
        lower_slope,
    )


def solution(mesh):
    placed = (
        P(("dp", "tensor"), None),
        P(("dp", "tensor"), None),
        P("dp", None),
        P(),
        P(None, "tensor"),
        P(None, "tensor"),
        P(None, "tensor"),
        P("tensor"),
        P("tensor", None),
        P(),
        P(None, ("dp", "tensor")),
        P(("dp", "tensor"), None),
    )
    return jax.shard_map(
        on_device,
        mesh=mesh,
        in_specs=placed,
        out_specs=(
            P(("dp", "tensor"), None),
            P(("dp", "tensor"), None),
            P(("dp", "tensor")),
            P(None, "tensor"),
            P(None, "tensor"),
            P(None, "tensor"),
            P("tensor"),
            P("tensor", None),
            P(("dp", "tensor")),
            P(None, ("dp", "tensor")),
            P(("dp", "tensor"), None),
        ),
        check_vma=False,
    )
```

```python
import functools

import jax
import jax.numpy as jnp
from jax import lax
from jax.experimental import pallas as pl
from jax.experimental.pallas import tpu as pltpu
from jax.sharding import PartitionSpec as P

EPSILON = 1e-06
LONGEST = 2048
SEGMENTS = 8
PLACES = 16
STEPS = 64
BLOCK = SEGMENTS * STEPS
GROUP = 32
GELU_SLOPE = 0.7978845608028654
GELU_CUBE = 0.044715
VMEM_BYTES = 56 * 1024 * 1024
F32 = jnp.float32
BF16 = jnp.bfloat16


def in_hbm(values):
    return pltpu.with_memory_space_constraint(values, pltpu.HBM)


def hbm(shape, dtype):
    return pltpu.HBM(shape, dtype)


def dot_nn(left, right):
    return lax.dot_general(left, right, (((1,), (0,)), ((), ())), preferred_element_type=F32)


def dot_nt(left, right):
    return lax.dot_general(left, right, (((1,), (1,)), ((), ())), preferred_element_type=F32)


def row_scale(rows):
    return lax.rsqrt(jnp.mean(rows * rows, -1, keepdims=True) + EPSILON)


def fold_rows(values):
    return jnp.sum(values.reshape(-1, 8, values.shape[-1]), 0)


def put_blocks(values, halves, me, first):
    tall = values.shape[0] // PLACES
    for place in range(PLACES):
        block = pl.multiple_of((place ^ me) * tall, tall)
        there = (place % (PLACES // 2)) * tall
        out = halves[place // (PLACES // 2)]
        out[there : there + tall, first : first + values.shape[1]] = values[pl.ds(block, tall), :].astype(out.dtype)


def interleave(block, scratch):
    lanes = scratch.shape[0]
    for lane in range(lanes):
        for run in range(SEGMENTS):
            part = block[run, :, lane * 128 : (lane + 1) * 128]
            scratch[lane, pl.ds(run, block.shape[1], stride=SEGMENTS), :] = part.astype(F32)
    return jnp.concatenate([scratch[lane] for lane in range(lanes)], -1)


def separate(values, scratch, out):
    lanes = scratch.shape[0]
    for lane in range(lanes):
        scratch[lane] = values[:, lane * 128 : (lane + 1) * 128]
    for run in range(SEGMENTS):
        parts = [scratch[lane, pl.ds(run, out.shape[1], stride=SEGMENTS), :] for lane in range(lanes)]
        out[run] = jnp.concatenate(parts, -1).astype(out.dtype)


def gates(forget_logit, admit_logit):
    top = jnp.maximum(jnp.maximum(-admit_logit, -forget_logit), 0.0)
    one = jnp.exp(-top)
    admit_exp = jnp.exp(-admit_logit - top)
    forget_exp = jnp.exp(-forget_logit - top)
    keep_part = one + admit_exp
    admit_part = one + forget_exp
    total = keep_part + admit_part
    inverse = pl.reciprocal(total, approx=True)
    inverse = inverse * (2.0 - total * inverse)
    keep = keep_part * inverse
    admit = admit_part * inverse
    return keep, admit, keep * (forget_exp * inverse), -admit * (admit_exp * inverse)


def goes_on(lengths_ref, scalars_ref, run, tall):
    place = scalars_ref[0] + run * tall
    begin = jnp.int32(0)
    fresh = False
    for entry in range(lengths_ref.shape[1]):
        length = lengths_ref[0, entry]
        fresh = fresh | ((begin == place) & (length > 0))
        begin = begin + length
    return jnp.where(fresh, 0.0, 1.0).astype(F32)


def product_of_runs(values, masks):
    result = masks[0] * values[0:1]
    for run in range(1, SEGMENTS):
        result = result * (masks[run] * values[run : run + 1])
    return result


def mixer_kernel(first, *refs):
    if first:
        x_ref, gain_ref, *refs = refs
    else:
        normed_in, *refs = refs
    wf, wa, wv, bias, lengths, scalars, carry, *refs = refs
    if first:
        x_out, normed_out, *refs = refs
    admit_out, state_out, forget_fac, admit_fac, ends_out, *refs = refs
    logits, hs, ps, vs, fs, as_, enter, *refs = refs
    phase, block = pl.program_id(0), pl.program_id(1)
    channels = wf.shape[1]
    start = pl.multiple_of(block * BLOCK, BLOCK)

    @pl.when((phase == 0) & (block == 0))
    def _():
        hs[0:8, :] = jnp.zeros((8, channels), F32)
        ps[0:8, :] = jnp.ones((8, channels), F32)

    @pl.when(phase == 0)
    def _():
        if first:
            rows = interleave(x_ref[...], refs[0])
            x_out[...] = rows.astype(BF16)
            normed = (rows * row_scale(rows) * gain_ref[...]).astype(BF16)
            normed_out[...] = normed
        else:
            normed = normed_in[...]
        wide = min(channels, 256)
        chunks = channels // wide
        weights = (wf, wa, wv)

        def project(chunk, kind):
            logits[chunk, kind] = dot_nn(normed, weights[kind][:, chunk * wide : (chunk + 1) * wide])

        def gate(chunk, lane, here, chain):
            inner, cols = slice(lane, lane + 128), slice(chunk * wide + lane, chunk * wide + lane + 128)
            rows = slice(here, here + GROUP)
            there = pl.ds(start + here, GROUP)
            value = logits[chunk, 2, rows, inner]
            keep, admit, forget_side, admit_side = gates(
                logits[chunk, 0, rows, inner], logits[chunk, 1, rows, inner] + bias[:, cols]
            )
            admit_out[rows, cols] = admit.astype(BF16)
            vs[there, cols] = value
            fs[there, cols] = forget_side
            as_[there, cols] = admit_side
            inflow = admit * value
            state, gain = chain
            for step in range(0, GROUP, 8):
                state = keep[step : step + 8] * state + inflow[step : step + 8]
                gain = gain * keep[step : step + 8]
                hs[pl.ds(start + here + step + 8, 8), cols] = state
                ps[pl.ds(start + here + step + 8, 8), cols] = gain
            return state, gain

        for kind in range(3):
            project(0, kind)
        for chunk in range(chunks):
            firsts = range(chunk * wide, (chunk + 1) * wide, 128)
            chains = [(hs[pl.ds(start, 8), c : c + 128], ps[pl.ds(start, 8), c : c + 128]) for c in firsts]
            units = [(here, lane) for here in range(0, BLOCK, GROUP) for lane in range(len(chains))]
            ahead = [(chunk + 1, kind) for kind in range(3)] if chunk + 1 < chunks else []
            for index, (here, lane) in enumerate(units):
                if ahead and index % max(1, len(units) // 3) == 0:
                    project(*ahead.pop(0))
                chains[lane] = gate(chunk, lane * 128, here, chains[lane])
            for item in ahead:
                project(*item)

    @pl.when((phase == 1) & (block == 0))
    def _():
        total = hs.shape[0]
        ends, gains = hs[total - 8 : total, :], ps[total - 8 : total, :]
        masks = [goes_on(lengths, scalars, run, (total - 8) // SEGMENTS) for run in range(SEGMENTS)]
        entering = masks[0] * carry[...]
        enter[0:1] = entering
        for run in range(1, SEGMENTS):
            entering = masks[run] * (ends[run - 1 : run] + gains[run - 1 : run] * entering)
            enter[run : run + 1] = entering
        ends_out[0:1, :] = ends[7:8] + gains[7:8] * enter[7:8, :]
        ends_out[1:2, :] = product_of_runs(gains, masks)
        ends_out[2:8, :] = jnp.zeros((6, channels), F32)

    @pl.when(phase == 1)
    def _():
        def some_rows(group, _):
            here = pl.multiple_of(group * 64, 64)
            there = pl.multiple_of(start + here, 64)
            for lane in range(0, channels, 128):
                cols = pl.ds(lane, 128)
                entering = enter[:, lane : lane + 128]
                states = hs[pl.ds(there, 72), cols].reshape(9, 8, 128) + ps[pl.ds(there, 72), cols].reshape(9, 8, 128) * entering
                states = states.reshape(72, 128)
                state_out[pl.ds(here, 64), cols] = states[8:].astype(BF16)
                change = states[:64] - vs[pl.ds(there, 64), cols]
                forget_fac[pl.ds(here, 64), cols] = (change * fs[pl.ds(there, 64), cols]).astype(BF16)
                admit_fac[pl.ds(here, 64), cols] = (change * as_[pl.ds(there, 64), cols]).astype(BF16)
            return 0

        lax.fori_loop(0, BLOCK // 64, some_rows, 0)


def mixer_forward(first, rows_in, gain, weights, bias, lengths, scalars, carry):
    width = rows_in.shape[-1]
    rows = rows_in.size // width
    channels = weights[0].shape[1]
    blocks = rows // BLOCK
    early = lambda phase, block: (jnp.where(phase == 0, block, blocks - 1), 0)
    late = lambda phase, block: (jnp.where(phase == 0, 0, block), 0)
    whole = lambda phase, block: (0, 0)
    if first:
        in_specs = [
            pl.BlockSpec((SEGMENTS, STEPS, width), lambda phase, block: (0, jnp.where(phase == 0, block, blocks - 1), 0)),
            pl.BlockSpec((1, width), whole),
        ]
        operands = [rows_in.reshape(SEGMENTS, rows // SEGMENTS, width), gain]
        out_specs = [pl.BlockSpec((BLOCK, width), early)] * 2
        out_shape = [hbm((rows, width), BF16)] * 2
    else:
        in_specs, operands = [pl.BlockSpec((BLOCK, width), early)], [rows_in]
        out_specs, out_shape = [], []
    in_specs += [pl.BlockSpec((width, channels), whole)] * 3
    in_specs += [pl.BlockSpec((1, channels), whole)] + [pl.BlockSpec(memory_space=pltpu.SMEM)] * 2 + [pl.BlockSpec((1, channels), whole)]
    out_specs += [pl.BlockSpec((BLOCK, channels), early)] + [pl.BlockSpec((BLOCK, channels), late)] * 3
    out_specs += [pl.BlockSpec((8, channels), whole)]
    out_shape += [hbm((rows, channels), BF16)] * 4
    out_shape += [hbm((8, channels), F32)]
    wide = min(channels, 256)
    scratch = [pltpu.VMEM((channels // wide, 3, BLOCK, wide), F32)]
    scratch += [pltpu.VMEM((rows + 8, channels), F32)] * 2
    scratch += [pltpu.VMEM((rows, channels), F32)] * 3
    scratch += [pltpu.VMEM((8, channels), F32)]
    if first:
        scratch += [pltpu.VMEM((width // 128, BLOCK, 128), F32)]
    return pl.pallas_call(
        functools.partial(mixer_kernel, first),
        grid=(2, blocks),
        in_specs=in_specs,
        out_specs=out_specs,
        out_shape=out_shape,
        scratch_shapes=scratch,
        compiler_params=pltpu.CompilerParams(vmem_limit_bytes=36 * 1024 * 1024, dimension_semantics=("arbitrary", "arbitrary")),
        cost_estimate=pl.CostEstimate(flops=2 * rows * width * 3 * channels, bytes_accessed=rows * channels * 16, transcendentals=4 * rows * channels),
        name="mixer_forward",
    )(in_hbm(operands[0]), *operands[1:], *weights, bias, lengths, scalars, carry)


def dense_kernel(stage, sets, pieces, *refs):
    states, refs = refs[:sets], refs[sets:]
    if stage == 0:
        x_ref, c_ref, *refs = refs
        outs_w, refs = refs[:sets], refs[sets:]
    else:
        middle_ref, sum_ref, delta_ref, dense_ref, cotangent_ref, *refs = refs
    gain_ref, scalars, *refs = refs
    pieces_w, refs = refs[:pieces], refs[pieces:]
    keep_out, send_out, *refs = refs
    if stage == 0:
        middle_out, sum_out, delta_out, dense_out, cotangent_out, upper_acc, lower_acc, cotangent_s = refs
    else:
        out_ref, mixed_ref, slope_ref, *refs = refs
        outputs_ref, refs = refs[:sets], refs[sets:]
        upper_acc, lower_acc, output_acc, out_s = refs
    step = pl.program_id(0)
    gain = gain_ref[...]
    shards, both, width = pieces_w[0].shape
    half = both // 2

    @pl.when(step == 0)
    def _():
        upper_acc[...] = jnp.zeros_like(upper_acc)
        lower_acc[...] = jnp.zeros_like(lower_acc)
        if stage == 1:
            output_acc[...] = jnp.zeros_like(output_acc)
            slope_ref[...] = jnp.zeros_like(slope_ref)

    if stage == 0:
        middle = x_ref[...].astype(F32)
        for state, weight in zip(states, outs_w):
            middle = middle + dot_nn(state[...], weight[...])
        middle_out[...] = middle.astype(BF16)
        dense_in = (middle * row_scale(middle) * gain).astype(BF16)
        dense_out[...] = dense_in
        cotangent = interleave(c_ref[...], cotangent_s).astype(BF16)
        cotangent_out[...] = cotangent
    else:
        dense_in, cotangent = dense_ref[...], cotangent_ref[...]
    dense_t, cotangent_t = dense_in.T, cotangent.T
    joined = max(1, 256 // (shards * half))
    chunks = range(0, pieces, joined)

    def weights(chunk):
        some = pieces_w[chunk : chunk + joined]
        upper_w = jnp.concatenate([w[:, :half, :].reshape(shards * half, width) for w in some], 0)
        return upper_w, jnp.concatenate([w[:, half:, :].reshape(shards * half, width) for w in some], 0)

    def bend(upper):
        square = upper * upper
        bell = 0.5 + 0.5 * jnp.tanh(upper * (GELU_SLOPE + GELU_SLOPE * GELU_CUBE * square))
        active = upper * bell
        slope = bell + active * (1.0 - bell) * (2.0 * GELU_SLOPE + 6.0 * GELU_SLOPE * GELU_CUBE * square)
        return active.astype(BF16), slope

    def gather(chunk, active, upper_delta):
        cols = slice(chunk * shards * half, (chunk + joined) * shards * half)
        lower_acc[:, cols] += dot_nn(cotangent_t, active)
        upper_acc[:, cols] += dot_nn(dense_t, upper_delta)

    fed, delta, behind = None, None, None
    upper_w, lower_w = weights(0)
    upper, back = dot_nt(dense_in, upper_w), dot_nt(cotangent, lower_w)
    for chunk in chunks:
        following = chunk + joined
        if following < pieces:
            next_upper_w, next_lower_w = weights(following)
            next_upper = dot_nt(dense_in, next_upper_w)
        active, slope = bend(upper)
        upper_delta = (slope * back).astype(BF16)
        if following < pieces:
            next_back = dot_nt(cotangent, next_lower_w)
        if behind is not None:
            gather(*behind)
        fed_part, delta_part = dot_nn(active, lower_w), dot_nn(upper_delta, upper_w)
        fed = fed_part if fed is None else fed + fed_part
        delta = delta_part if delta is None else delta + delta_part
        behind = chunk, active, upper_delta
        if following < pieces:
            upper_w, lower_w, upper, back = next_upper_w, next_lower_w, next_upper, next_back
    gather(*behind)
    if stage == 0:
        sum_out[...] = (middle + fed).astype(BF16)
        delta_out[...] = delta.astype(BF16)
    else:
        separate(sum_ref[...].astype(F32) + fed, out_s, out_ref)
        middle = middle_ref[...].astype(F32)
        scale = row_scale(middle)
        delta = delta_ref[...].astype(F32) + delta
        slope_ref[...] += fold_rows(delta * middle * scale)
        scaled = delta * gain
        inner = jnp.mean(scaled * middle, -1, keepdims=True)
        mixed = (cotangent.astype(F32) + scale * (scaled - middle * (scale * scale * inner))).astype(BF16)
        mixed_ref[...] = mixed
        mixed_t = mixed.T
        channels = states[0].shape[1]
        for index, state in enumerate(states):
            output_acc[:, index * channels : (index + 1) * channels] += dot_nn(mixed_t, state[...])

    @pl.when(step == pl.num_programs(0) - 1)
    def _():
        for shard in range(0, pieces * shards, 2):
            cols = slice(shard * half, (shard + 2) * half)
            out = keep_out if shard < pieces * shards // 2 else send_out
            there = shard % (pieces * shards // 2)
            out[there : there + 2, :half, :] = upper_acc[:, cols].T.astype(BF16).reshape(2, half, width)
            out[there : there + 2, half:, :] = lower_acc[:, cols].T.astype(BF16).reshape(2, half, width)
        if stage == 1:
            slope_ref[0:1, :] = jnp.sum(slope_ref[...], 0, keepdims=True)
            tall = output_acc.shape[0] // PLACES
            for index, output in enumerate(outputs_ref):
                for place in range(PLACES):
                    there = pl.multiple_of((place ^ scalars[2]) * tall, tall)
                    output[place * tall : (place + 1) * tall, :] = output_acc[
                        pl.ds(there, tall), index * channels : (index + 1) * channels
                    ].astype(BF16)


def dense_both(stage, states, entering, output_weights, gain, scalars, pieces):
    rows, channels = states[0].shape
    width = gain.shape[1]
    shards, both, _ = pieces[0].shape
    hidden = len(pieces) * shards * both // 2
    sets = len(states)
    tall = min(rows, 512)
    by_rows = lambda block: (block, 0)
    whole = lambda block: (0, 0)
    runs_spec = pl.BlockSpec((SEGMENTS, tall // SEGMENTS, width), lambda block: (0, block, 0))
    runs_shape = (SEGMENTS, rows // SEGMENTS, width)
    row_spec = pl.BlockSpec((tall, width), by_rows)
    grads = (len(pieces) * shards // 2, both, width)
    in_specs = [pl.BlockSpec((tall, channels), by_rows)] * sets
    out_specs = [pl.BlockSpec(grads, lambda block: (0, 0, 0))] * 2
    out_shape = [hbm(grads, BF16)] * 2
    scratch = [pltpu.VMEM((width, hidden), F32)] * 2
    if stage == 0:
        in_specs += [row_spec, runs_spec] + [pl.BlockSpec((channels, width), whole)] * sets
        entering = [entering[0], entering[1].reshape(runs_shape), *output_weights]
        out_specs += [row_spec] * 5
        out_shape += [hbm((rows, width), BF16)] * 5
    else:
        in_specs += [row_spec] * 5
        out_specs += [runs_spec, row_spec, pl.BlockSpec((8, width), whole)] + [pl.BlockSpec((width, channels), whole)] * sets
        out_shape += [hbm(runs_shape, BF16), hbm((rows, width), BF16)]
        out_shape += [hbm((8, width), F32)] + [hbm((width, channels), BF16)] * sets
        scratch += [pltpu.VMEM((width, sets * channels), F32)]
    scratch += [pltpu.VMEM((width // 128, tall, 128), F32)]
    in_specs += [pl.BlockSpec((1, width), whole), pl.BlockSpec(memory_space=pltpu.SMEM)]
    in_specs += [pl.BlockSpec((shards, both, width), lambda block: (0, 0, 0))] * len(pieces)
    return pl.pallas_call(
        functools.partial(dense_kernel, stage, sets, len(pieces)),
        grid=(rows // tall,),
        in_specs=in_specs,
        out_specs=out_specs,
        out_shape=out_shape,
        scratch_shapes=scratch,
        compiler_params=pltpu.CompilerParams(vmem_limit_bytes=44 * 1024 * 1024, dimension_semantics=("arbitrary",)),
        cost_estimate=pl.CostEstimate(flops=12 * rows * width * hidden, bytes_accessed=rows * width * 24, transcendentals=rows * hidden),
        name="dense_first" if stage == 0 else "dense_second",
    )(*[in_hbm(v) for v in states], *[in_hbm(v) if v.shape[0] != channels else v for v in entering], gain, scalars, *pieces)


def mixer_back_kernel(sets, mixed_ref, normed_ref, lengths, scalars, *refs):
    per_set = [refs[index * 6 : index * 6 + 6] for index in range(sets)]
    refs = refs[6 * sets :]
    carried_out, refs = refs[:sets], refs[sets:]
    first_out, second_out, refs = refs[:2], refs[2:4], refs[4:]
    bias_out, ends_out, *refs = refs
    cs, ps, state_delta, admits, deltas, slopes_acc, last, enter = refs
    phase, block = pl.program_id(0), pl.program_id(1)
    blocks = pl.num_programs(1)
    channels = per_set[0][1].shape[1]
    place = jnp.where(phase == 0, blocks - 1 - block, block)
    start = pl.multiple_of(place * BLOCK, BLOCK)

    @pl.when((phase == 0) & (block == 0))
    def _():
        last[:, 0:8, :] = jnp.zeros((sets, 8, channels), F32)
        last[:, 8:16, :] = jnp.ones((sets, 8, channels), F32)

    @pl.when(phase == 0)
    def _():
        def arrive(index):
            state_delta[index] = dot_nt(mixed_ref[...], per_set[index][0][...])

        arrive(0)
        for index in range(sets):
            admit_ref = per_set[index][1]
            for lane in range(0, channels, 128):
                if lane == 0 and index + 1 < sets:
                    arrive(index + 1)
                cols = slice(lane, lane + 128)
                kept, gain = last[index, 0:8, cols], last[index, 8:16, cols]
                for here in range(BLOCK - 16, -1, -16):
                    admit = admit_ref[here : here + 16, cols]
                    admits[index, pl.ds(start + here, 16), cols] = admit
                    keep = 1.0 - admit.astype(F32)
                    for step in (8, 0):
                        carried = state_delta[index, here + step : here + step + 8, cols] + kept
                        cs[index, pl.ds(start + here + step, 8), cols] = carried
                        ps[index, pl.ds(start + here + step, 8), cols] = gain
                        kept = keep[step : step + 8] * carried
                        gain = keep[step : step + 8] * gain
                last[index, 0:8, cols] = kept
                last[index, 8:16, cols] = gain

    @pl.when((phase == 1) & (block == 0))
    def _():
        masks = [goes_on(lengths, scalars, run, cs.shape[1] // SEGMENTS) for run in range(SEGMENTS)]
        for index in range(sets):
            kept, gain = last[index, 0:8, :], last[index, 8:16, :]
            entering = per_set[index][4][...]
            enter[index, 7:8, :] = entering
            for run in range(SEGMENTS - 1, 0, -1):
                entering = masks[run] * (kept[run : run + 1] + gain[run : run + 1] * entering)
                enter[index, run - 1 : run, :] = entering
            ends_out[index, 0:1, :] = masks[0] * (kept[0:1] + gain[0:1] * entering)
            ends_out[index, 1:2, :] = product_of_runs(gain, masks)
            ends_out[index, 2:8, :] = jnp.zeros((6, channels), F32)
        bias_out[...] = jnp.zeros_like(bias_out)
        slopes_acc[...] = jnp.zeros_like(slopes_acc)

    @pl.when(phase == 1)
    def _():
        normed_t = normed_ref[...].T
        wide = min(channels, 256)
        chunks = [(index, first) for index in range(sets) for first in range(0, channels, wide)]

        def move(index, lane, here):
            _, _, forget_fac, admit_fac, _, _ = per_set[index]
            cols = slice(lane, lane + 128)
            rows, there = slice(here, here + GROUP), pl.ds(start + here, GROUP)
            gains = ps[index, there, cols].reshape(GROUP // 8, 8, 128)
            carried = (cs[index, there, cols].reshape(GROUP // 8, 8, 128) + gains * enter[index, :, cols]).reshape(GROUP, 128)
            carried_out[index][rows, cols] = carried.astype(BF16)
            admit_delta = (carried * admit_fac[rows, cols].astype(F32)).astype(BF16)
            deltas[index, 0, rows, cols] = (carried * forget_fac[rows, cols].astype(F32)).astype(BF16)
            deltas[index, 1, rows, cols] = admit_delta
            deltas[index, 2, rows, cols] = (carried * admits[index, there, cols].astype(F32)).astype(BF16)
            return fold_rows(admit_delta.astype(F32))

        def reduce(index, first, kind):
            cols = slice(first, first + wide)
            slopes_acc[index, kind, :, cols] += dot_nn(normed_t, deltas[index, kind, :, cols])

        behind = []
        for index, first in chunks:
            lanes = range(first, first + wide, 128)
            biases = [jnp.zeros((8, 128), F32) for _ in lanes]
            units = [(here, which) for here in range(0, BLOCK, GROUP) for which in range(len(lanes))]
            for position, (here, which) in enumerate(units):
                if behind and position % max(1, len(units) // 3) == 0:
                    reduce(*behind.pop(0))
                biases[which] = biases[which] + move(index, lanes[which], here)
            for lane, bias in zip(lanes, biases):
                bias_out[index, :, lane : lane + 128] += bias
            for item in behind:
                reduce(*item)
            behind = [(index, first, kind) for kind in range(3)]
        for item in behind:
            reduce(*item)
        for index in range(sets):
            output_grads = per_set[index][5]
            tall = output_grads.shape[0]
            turns = cs.shape[1] // BLOCK
            for half in range(2):
                if turns == 1:
                    second_out[half][index, :, channels:] = output_grads[half * (tall // 2) : (half + 1) * (tall // 2), :]
                    continue

                @pl.when(block // (turns // 2) == half)
                def _():
                    there = pl.multiple_of(block % (turns // 2) * tall, tall)
                    second_out[half][index, pl.ds(there, tall), channels:] = output_grads[...]

    @pl.when((phase == 1) & (block == blocks - 1))
    def _():
        for index in range(sets):
            bias_out[index, 0:1, :] = jnp.sum(bias_out[index], 0, keepdims=True)
            put_blocks(slopes_acc.at[index, 0], [out.at[index] for out in first_out], scalars[1], 0)
            put_blocks(slopes_acc.at[index, 1], [out.at[index] for out in first_out], scalars[1], channels)
            put_blocks(slopes_acc.at[index, 2], [out.at[index] for out in second_out], scalars[2], 0)


def mixer_backward(mixed, normed, lengths, scalars, per_set):
    rows, width = mixed.shape
    sets = len(per_set)
    channels = per_set[0][1].shape[1]
    blocks = rows // BLOCK
    back = lambda phase, block: (jnp.where(phase == 0, blocks - 1 - block, 0), 0)
    late = lambda phase, block: (jnp.where(phase == 0, 0, block), 0)
    whole = lambda phase, block: (0, 0)
    all3 = lambda phase, block: (0, 0, 0)
    set_specs = [
        pl.BlockSpec((channels, width), whole),
        pl.BlockSpec((BLOCK, channels), back),
        pl.BlockSpec((BLOCK, channels), late),
        pl.BlockSpec((BLOCK, channels), late),
        pl.BlockSpec((1, channels), whole),
        pl.BlockSpec((width // blocks, channels), late),
    ]
    results = pl.pallas_call(
        functools.partial(mixer_back_kernel, sets),
        grid=(2, blocks),
        in_specs=[
            pl.BlockSpec((BLOCK, width), back),
            pl.BlockSpec((BLOCK, width), late),
            pl.BlockSpec(memory_space=pltpu.SMEM),
            pl.BlockSpec(memory_space=pltpu.SMEM),
        ]
        + set_specs * sets,
        out_specs=[pl.BlockSpec((BLOCK, channels), late)] * sets
        + [pl.BlockSpec((sets, width // 2, 2 * channels), all3)] * 4
        + [pl.BlockSpec((sets, 8, channels), all3)] * 2,
        out_shape=[jax.ShapeDtypeStruct((rows, channels), BF16)] * sets
        + [jax.ShapeDtypeStruct((sets, width // 2, 2 * channels), BF16)] * 4
        + [jax.ShapeDtypeStruct((sets, 8, channels), F32)] * 2,
        scratch_shapes=[
            pltpu.VMEM((sets, rows, channels), F32),
            pltpu.VMEM((sets, rows, channels), F32),
            pltpu.VMEM((sets, BLOCK, channels), F32),
            pltpu.VMEM((sets, rows, channels), BF16),
            pltpu.VMEM((sets, 3, BLOCK, channels), BF16),
            pltpu.VMEM((sets, 3, width, channels), F32),
            pltpu.VMEM((sets, 16, channels), F32),
            pltpu.VMEM((sets, 8, channels), F32),
        ],
        compiler_params=pltpu.CompilerParams(vmem_limit_bytes=50 * 1024 * 1024, dimension_semantics=("arbitrary", "arbitrary")),
        cost_estimate=pl.CostEstimate(flops=2 * rows * width * 4 * channels * sets, bytes_accessed=rows * channels * 12 * sets, transcendentals=0),
        name="mixer_backward",
    )(in_hbm(mixed), in_hbm(normed), lengths, scalars, *[in_hbm(item) if item.shape[0] == rows else item for one in per_set for item in one])
    return results[:sets], results[sets : sets + 2], results[sets + 2 : sets + 4], *results[sets + 4 :]


def input_kernel(sets, *refs):
    x_ref, mixed_ref, gain_ref, *refs = refs
    factors, refs = refs[: 4 * sets], refs[4 * sets :]
    weights, refs = refs[: 3 * sets], refs[3 * sets :]
    dense_ref, bias_ref, scalars, out_ref, small_ref, slope_ref, out_s = refs

    @pl.when(pl.program_id(0) == 0)
    def _():
        slope_ref[...] = jnp.zeros_like(slope_ref)

    normed_delta = None
    for index in range(sets):
        carried = factors[4 * index][...].astype(F32)
        for part in range(3):
            delta = (carried * factors[4 * index + 1 + part][...].astype(F32)).astype(BF16)
            term = dot_nt(delta, weights[3 * index + part][...])
            normed_delta = term if normed_delta is None else normed_delta + term
    rows = x_ref[...].astype(F32)
    scale = row_scale(rows)
    slope_ref[...] += fold_rows(normed_delta * rows * scale)
    scaled = normed_delta * gain_ref[...]
    inner = jnp.mean(scaled * rows, -1, keepdims=True)
    result = mixed_ref[...].astype(F32) + scale * (scaled - rows * (scale * scale * inner))
    separate(result, out_s, out_ref)

    @pl.when(pl.program_id(0) == pl.num_programs(0) - 1)
    def _():
        gains = jnp.concatenate([jnp.sum(slope_ref[...], 0, keepdims=True), dense_ref[0:1, :]], 1)
        low = jnp.where(scalars[3] == 0, bias_ref[0, 0:1, :], bias_ref[1, 0:1, :])
        high = jnp.where(scalars[3] == 0, bias_ref[1, 0:1, :], bias_ref[0, 0:1, :])
        biases = jnp.concatenate([low, high], 1)
        rest = jnp.zeros((small_ref.shape[0] - 2, biases.shape[1]), F32)
        small_ref[...] = jnp.concatenate([gains, biases, rest], 0).astype(BF16)


def input_backward(x_rows, mixed, gain, factors, weights, dense_part, bias_parts, scalars):
    rows, width = x_rows.shape
    sets = len(factors) // 4
    channels = weights[0].shape[1]
    by_rows = lambda block: (block, 0)
    whole = lambda block: (0, 0)
    return pl.pallas_call(
        functools.partial(input_kernel, sets),
        grid=(rows // BLOCK,),
        in_specs=[pl.BlockSpec((BLOCK, width), by_rows)] * 2
        + [pl.BlockSpec((1, width), whole)]
        + [pl.BlockSpec((BLOCK, channels), by_rows)] * (4 * sets)
        + [pl.BlockSpec((width, channels), whole)] * (3 * sets)
        + [pl.BlockSpec((8, width), whole), pl.BlockSpec((sets, 8, channels), lambda block: (0, 0, 0)), pl.BlockSpec(memory_space=pltpu.SMEM)],
        out_specs=[pl.BlockSpec((SEGMENTS, STEPS, width), lambda block: (0, block, 0)), pl.BlockSpec((16, sets * channels), whole)],
        out_shape=[hbm((SEGMENTS, rows // SEGMENTS, width), F32), jax.ShapeDtypeStruct((16, sets * channels), BF16)],
        scratch_shapes=[pltpu.VMEM((8, width), F32), pltpu.VMEM((width // 128, BLOCK, 128), F32)],
        compiler_params=pltpu.CompilerParams(vmem_limit_bytes=34 * 1024 * 1024, dimension_semantics=("arbitrary",)),
        cost_estimate=pl.CostEstimate(flops=2 * rows * width * 3 * channels * sets, bytes_accessed=rows * channels * 8 * sets, transcendentals=0),
        name="input_backward",
    )(in_hbm(x_rows), in_hbm(mixed), gain, *[in_hbm(f) for f in factors], *weights, dense_part, bias_parts, scalars)


def finish_kernel(channels, count, *refs):
    first_refs, second_refs = refs[:count], refs[count : 2 * count]
    scalars, forget_out, admit_out, value_out, output_out, scratch = refs[2 * count :]
    tall = scratch.shape[0] // PLACES
    each = PLACES // count
    for place in range(PLACES):
        here = slice(place % each * tall, (place % each + 1) * tall)
        for index, (sums, outs) in enumerate(((first_refs, (forget_out, admit_out)), (second_refs, (value_out, scratch)))):
            there = pl.multiple_of((place ^ scalars[1 + index]) * tall, tall)
            piece = sums[place // each]
            outs[0][pl.ds(there, tall), :] = piece[here, :channels].astype(F32)
            outs[1][pl.ds(there, tall), :] = piece[here, channels:].astype(F32)
    output_out[...] = scratch[...].T


def finish_slopes(first, second, scalars):
    count = len(first)
    width, channels = count * first[0].shape[0], first[0].shape[1] // 2
    return pl.pallas_call(
        functools.partial(finish_kernel, channels, count),
        in_specs=[pl.BlockSpec(memory_space=pltpu.VMEM)] * (2 * count) + [pl.BlockSpec(memory_space=pltpu.SMEM)],
        out_shape=[jax.ShapeDtypeStruct((width, channels), F32)] * 3 + [jax.ShapeDtypeStruct((channels, width), F32)],
        scratch_shapes=[pltpu.VMEM((width, channels), F32)],
        compiler_params=pltpu.CompilerParams(vmem_limit_bytes=VMEM_BYTES),
        name="finish_slopes",
    )(*first, *second, scalars)


def regroup(stacked, half):
    count, both, width = stacked.shape
    if both == 2 * half:
        return stacked
    arrays = jnp.moveaxis(stacked.reshape(count, 2, both // 2, width), 1, 0).reshape(2, -1, half, width)
    return jnp.moveaxis(arrays, 0, 1).reshape(-1, 2 * half, width)


def after(values, *earlier):
    return lax.optimization_barrier((values, earlier))[0]


def total(terms):
    result = terms[0].astype(F32)
    for term in terms[1:]:
        result = result + term.astype(F32)
    return result.astype(terms[0].dtype)


def sum_kernel(*refs):
    count = len(refs) // 3
    for index in range(count):
        left, right, out = refs[2 * index], refs[2 * index + 1], refs[2 * count + index]
        out[...] = (left[...].astype(F32) + right[...].astype(F32)).astype(BF16)


def paired_sums(pairs, blocks, places):
    specs = [pl.BlockSpec(block, functools.partial(lambda place, step: place, place)) for block, place in zip(blocks, places)]
    return pl.pallas_call(
        sum_kernel,
        grid=(1,),
        in_specs=[spec for spec in specs for _ in range(2)],
        out_specs=[pl.BlockSpec(block, lambda step: (0, 0, 0)) for block in blocks],
        out_shape=[jax.ShapeDtypeStruct(block, BF16) for block in blocks],
        compiler_params=pltpu.CompilerParams(vmem_limit_bytes=VMEM_BYTES),
        name="paired_sums",
    )(*[item for pair in pairs for item in pair])


def hold(terms, *earlier):
    return terms[:-1] + [after(terms[-1], *earlier)]


def part(terms, index, axis):
    half = terms[0].shape[axis] // 2
    return [lax.slice_in_dim(t, index * half, (index + 1) * half, axis=axis) for t in terms]


def pack_kernel(*refs):
    mine_out, output_out = refs[5:]
    for index, ref in enumerate(refs[1:4]):
        mine_out[index] = ref[...]
    output_out[...] = refs[4][...]


def pack_halves(weights, half):
    tall, wide = weights[0].shape[0] // 2, weights[0].shape[1]
    return pl.pallas_call(
        pack_kernel,
        grid_spec=pltpu.PrefetchScalarGridSpec(
            num_scalar_prefetch=1,
            grid=(1,),
            in_specs=[pl.BlockSpec((tall, wide), lambda step, half: (half[0], 0))] * 4,
            out_specs=[pl.BlockSpec((3, tall, wide), lambda step, half: (0, 0, 0)), pl.BlockSpec((tall, wide), lambda step, half: (0, 0))],
        ),
        out_shape=[jax.ShapeDtypeStruct((3, tall, wide), BF16), jax.ShapeDtypeStruct((tall, wide), BF16)],
        name="pack_halves",
    )(jnp.reshape(half, (1,)).astype(jnp.int32), *weights)


class Links:
    TENSOR, CORE, NEAR, Z_NEAR, Z_FAR = 1, 2, 4, 8, 16

    def __init__(self):
        dp = lax.axis_index("dp")
        core, near, z_near = dp % 2, dp // 2 % 2, dp // 4 % 2
        self.core = core
        self.me = [core * 8 + z_near * 4 + near * 2, core * 8 + near * 4 + z_near * 2]

    def swap(self, values, bits):
        pairs = [(device, device ^ bits) for device in range(32)]
        return lax.ppermute(values, ("dp", "tensor"), pairs)

    def begin_weights(self, own_weights):
        mine, mine_output = pack_halves(own_weights, self.core)
        return mine, mine_output, self.swap(mine, self.TENSOR)

    def end_weights(self, got):
        rest = self.swap(got, self.CORE)
        lower = self.core == 0
        return jnp.concatenate([jnp.where(lower, got, rest), jnp.where(lower, rest, got)], -2)

    def begin_dense(self, shard):
        return [shard] + [self.swap(shard, bits) for bits in (self.Z_NEAR, self.Z_FAR, self.Z_NEAR | self.Z_FAR)]

    def dense_pieces(self, pieces):
        own = jnp.stack(pieces)
        return own, self.swap(own, self.NEAR), self.swap(own, self.CORE)

    def dense_across(self, own_terms, other_terms):
        pick = lambda terms, near: total([t[near * 4 : near * 4 + 4] for t in terms])
        sends = [(pick(other_terms, 0), self.TENSOR), (pick(own_terms, 1), self.NEAR), (pick(other_terms, 1), self.TENSOR | self.NEAR)]
        return sends, [t[:4] for t in own_terms]

    def dense_along(self, terms):
        sends = []
        for index, bits in ((1, self.Z_NEAR), (2, self.Z_FAR), (3, self.Z_NEAR | self.Z_FAR)):
            sends.append((total([t[index] for t in terms]), bits))
        return sends, [t[0] for t in terms]

    def exchange(self, sends, kept):
        return kept + [self.swap(values, bits) for values, bits in sends]

    def halve(self, terms, bits, extra=None):
        axis = 0 if bits == self.TENSOR else 1
        send = total(part(terms, 1, axis))
        if extra is not None:
            send = jnp.concatenate([send, extra], 1)
        return [(send, bits)], part(terms, 0, axis)

    def grow(self, values, bits):
        return jnp.concatenate([values, self.swap(values, bits)], 1)


class Plain:
    def __init__(self, n_tensor, own, hidden):
        self.n_tensor, self.own, self.hidden = n_tensor, own, hidden
        self.me = [0, 0]

    def weights(self, own_weights):
        whole = [lax.all_gather(w, "tensor", axis=1, tiled=True) for w in own_weights[:3]]
        pairs = [jnp.split(w, 2, 1) for w in whole]
        pairs.append(jnp.split(lax.all_gather(own_weights[3], "tensor", axis=0, tiled=True), 2, 0))
        return [p[0] for p in pairs], [p[1] for p in pairs]

    def bias(self, own_bias):
        return tuple(jnp.split(lax.all_gather(own_bias, "tensor", axis=0, tiled=True), 2))

    def dense(self, shard):
        whole = regroup(lax.all_gather(shard, ("dp", "tensor"), axis=0), 64)
        pieces = [whole[first : first + 4] for first in range(0, whole.shape[0], 4)]
        return pieces[: len(pieces) // 2], pieces[len(pieces) // 2 :]

    def dense_sums(self, grads):
        whole = regroup(jnp.concatenate(grads, 0), self.hidden)
        return lax.psum_scatter(whole, ("dp", "tensor"), scatter_dimension=0, tiled=True)[0]

    def mixer_sums(self, grads):
        grads = jnp.concatenate(grads, 1)
        _, width, columns = grads.shape
        whole = jnp.moveaxis(grads.reshape(2, width, 2, columns // 2), 0, 2).reshape(width, 2, columns)
        part = lax.psum_scatter(whole, "tensor", scatter_dimension=2, tiled=True)
        return jnp.split(lax.psum(part, "dp").reshape(width, 2 * self.own), 2, 0)

def on_device(
    block_in,
    out_cotangent,
    seq_lengths,
    premix_gain,
    forget_weight,
    admit_weight,
    value_weight,
    admit_bias,
    output_weight,
    dense_gain,
    upper_weight,
    lower_weight,
):
    n_dp, n_tensor = lax.axis_size("dp"), lax.axis_size("tensor")
    rows, width = block_in.shape
    place = lax.axis_index("tensor")
    own = forget_weight.shape[1]
    premix = premix_gain.astype(F32)[None]
    dense = dense_gain.astype(F32)[None]
    paired = (n_dp, n_tensor) == (16, 2)
    hidden = lower_weight.shape[0]
    links = Links() if paired else Plain(n_tensor, own, hidden)
    scalars = jnp.stack([place * rows] + links.me + [place if paired else 0]).astype(jnp.int32)
    own_weights = [forget_weight, admit_weight, value_weight, output_weight]
    dense_shard = jnp.concatenate([upper_weight.T, lower_weight], 0)
    if paired:
        weights, biases = [own_weights], [admit_bias]
        channels = own
        mine, mine_output, got = links.begin_weights(own_weights)
        pieces = links.begin_dense(after(dense_shard, mine))
        biases.append(links.swap(after(admit_bias, pieces[0]), Links.TENSOR))
    else:
        weights, biases = links.weights(own_weights), links.bias(admit_bias)
        channels = weights[0][0].shape[1]
    crossing = rows % LONGEST != 0
    nothing = jnp.zeros((1, channels), F32)

    def chained(ends, backwards):
        every = lax.all_gather(ends, "tensor", axis=0)
        entering = jnp.zeros_like(ends[0:1])
        mine = entering
        order = range(n_tensor - 1, -1, -1) if backwards else range(n_tensor)
        for index in order:
            mine = jnp.where(place == index, entering, mine)
            entering = every[index, 0:1] + every[index, 1:2] * entering
        return mine

    def forward(first, rows_in, index):
        carry = nothing
        args = (first, rows_in, premix, weights[index][:3], biases[index].astype(F32)[None], seq_lengths, scalars)
        if crossing:
            carry = chained(mixer_forward(*args, carry)[-1], False)
        return mixer_forward(*args, carry)

    x_rows, normed, *kept_0 = forward(True, block_in, 0)
    if paired:
        got, pieces, biases[1] = after((got, pieces, biases[1]), normed)
        got_output = links.swap(after(mine_output, got), Links.TENSOR)
        own_four, near_four, own_rest = links.dense_pieces(pieces)
        other_weights = links.end_weights(got)
        weights.append([other_weights[index] for index in range(3)])
    kept_1 = forward(False, normed, 1)
    kept = [kept_0, kept_1]
    if paired:
        near_four, held_four = after((near_four, own_four), kept_1[1])
        weights[1].append(links.end_weights(after(got_output, kept_1[1])))
        other_four = links.swap(held_four, Links.TENSOR)
        far_four = links.swap(held_four, Links.TENSOR | Links.NEAR)
        pieces_0 = [own_four, near_four, own_rest, links.swap(near_four, Links.CORE)]
    else:
        pieces_0, pieces_1 = links.dense(dense_shard)
    outputs = [w[3] for w in weights]
    states = [k[1] for k in kept]
    own_keep, own_send, *rows_0 = dense_both(0, states, (x_rows, out_cotangent), outputs, dense, scalars, pieces_0)
    if paired:
        far_four, other_four = after((far_four, other_four), rows_0[0])
        pieces_1 = [other_four, far_four, links.swap(other_four, Links.CORE), links.swap(far_four, Links.CORE)]
        own_terms = [own_keep, links.swap(after(own_send, pieces_1), Links.CORE)]
    other_keep, other_send, block_out, mixed, dense_part, *output_grads = dense_both(1, states, rows_0, None, dense, scalars, pieces_1)
    back_mixed = mixed
    if paired:
        own_terms[1] = after(own_terms[1], mixed)
        other_terms = [other_keep, links.swap(after(other_send, own_terms[1]), Links.CORE)]
        dense_sends, dense_kept = links.dense_across(own_terms, other_terms)
        back_mixed = after(mixed, [values for values, _ in dense_sends])
        dense_terms = links.exchange(dense_sends, dense_kept)

    carries = [nothing, nothing]
    for _ in range(2 if crossing else 1):
        per_set = [
            (outputs[index], kept[index][0], kept[index][2], kept[index][3], carries[index], output_grads[index])
            for index in range(2)
        ]
        carried, first, second, bias_parts, ends = mixer_backward(back_mixed, normed, seq_lengths, scalars, per_set)
        if crossing:
            carries = [chained(ends[index], True) for index in range(2)]
    factors = [f for index in range(2) for f in (carried[index], kept[index][2], kept[index][3], kept[index][0])]
    if paired:
        dense_terms = hold(dense_terms, carried[0])
        along, along_kept = links.dense_along(dense_terms)
        core_sends = after([first[1], second[1]], dense_terms[-3:])
        first = [first[0], links.swap(core_sends[0], Links.CORE)]
        second = [second[0], links.swap(core_sends[1], Links.CORE)]
        sets, tall, wide = first[0].shape
        blocks = ((1, tall, wide), (sets, tall // 2, wide))
        sums = paired_sums((first, second) * 2, blocks * 2, ((1, 0, 0), (0, 1, 0), (0, 0, 0), (0, 0, 0)))
        first, second = ([(sums[0], Links.TENSOR)], [sums[2]]), ([(sums[1], Links.NEAR)], [sums[3]])
        factors[0] = after(factors[0], first[0][0][0], second[0][0][0], [values for values, _ in along])
        first, second = links.exchange(*first), links.exchange(*second)
        dense_terms = links.exchange(along, along_kept)
    input_slope, small = input_backward(
        x_rows, mixed, premix, factors, weights[0][:3] + weights[1][:3], dense_part, bias_parts, scalars
    )

    if paired:
        small = small[None]
        first, second = hold(first, input_slope), hold(second, input_slope)
        dense_terms = dense_terms[:-3] + after(dense_terms[-3:], input_slope)
        small = after(small, first[-1], second[-1], dense_terms[-3:])
        small = total([small, links.swap(small, Links.CORE)])

        def halve_both(first, second, first_bits, second_bits, extra):
            first, first_kept = links.halve(first, first_bits)
            second, second_kept = links.halve(second, second_bits, extra)
            second_send = second[0][0]
            if first_bits == Links.Z_NEAR:
                first_kept, second_kept = ([lax.optimization_barrier(total(kept))] for kept in (first_kept, second_kept))
            first, second = links.exchange(first, first_kept), links.exchange(second, second_kept)
            rows_sent = second_send.shape[1] - extra.shape[1]
            extra = total([extra, second[-1][:, rows_sent:]])
            return first, second[:-1] + [second[-1][:, :rows_sent]], extra

        first, second, small = halve_both(first, second, Links.Z_NEAR, Links.TENSOR, small)
        first, second, small = halve_both(first, second, Links.NEAR, Links.Z_NEAR, small)
        first, second = total(first), total(second)
        count = first.shape[1]
        first_got = links.swap(first, Links.Z_FAR)
        second_got = links.swap(jnp.concatenate([second, small], 1), Links.Z_FAR)
        first, second = total([first, first_got]), total([second, second_got[:, :count]])
        small = total([small, second_got[:, count:]])
        got = links.swap(jnp.concatenate([first, small], 1), Links.NEAR)
        first, small = jnp.concatenate([first, got[:, :count]], 1), total([small, got[:, count:]])
        second = links.grow(second, Links.Z_NEAR)
        first, second = [first, links.swap(first, Links.Z_NEAR)], [second, links.swap(second, Links.NEAR)]
        first += [links.swap(f, Links.CORE) for f in first]
        second += [links.swap(f, Links.CORE) for f in second]
        first, second = [f[0] for f in first], [f[0] for f in second]
        small = small[0].astype(F32)
        dense_sum = total(dense_terms)
    else:
        small = lax.psum(small.astype(F32), ("dp", "tensor"))
        dense_sum = links.dense_sums([own_keep, own_send, other_keep, other_send])
        first, second = links.mixer_sums(first), links.mixer_sums(second)
    dense_sum = dense_sum.astype(F32)
    upper_slope, lower_slope = dense_sum[:hidden].T, dense_sum[hidden:]
    forget_slope, admit_slope, value_slope, output_slope = finish_slopes(first, second, scalars)
    shard = width // (n_dp * n_tensor)
    at = (lax.axis_index("dp") * n_tensor + place) * shard
    premix_slope = lax.dynamic_slice(small, (0, at), (1, shard))[0]
    dense_slope = lax.dynamic_slice(small, (0, width + at), (1, shard))[0]
    bias_slope = lax.dynamic_slice(small, (1, place * own), (1, own))[0]
    return (
        block_out.reshape(rows, width),
        input_slope.reshape(rows, width),
        premix_slope,
        forget_slope,
        admit_slope,
        value_slope,
        bias_slope,
        output_slope,
        dense_slope,
        upper_slope,
        lower_slope,
    )


def solution(mesh):
    placed = (
        P(("dp", "tensor"), None),
        P(("dp", "tensor"), None),
        P("dp", None),
        P(),
        P(None, "tensor"),
        P(None, "tensor"),
        P(None, "tensor"),
        P("tensor"),
        P("tensor", None),
        P(),
        P(None, ("dp", "tensor")),
        P(("dp", "tensor"), None),
    )
    return jax.shard_map(
        on_device,
        mesh=mesh,
        in_specs=placed,
        out_specs=(
            P(("dp", "tensor"), None),
            P(("dp", "tensor"), None),
            P(("dp", "tensor")),
            P(None, "tensor"),
            P(None, "tensor"),
            P(None, "tensor"),
            P("tensor"),
            P("tensor", None),
            P(("dp", "tensor")),
            P(None, ("dp", "tensor")),
            P(("dp", "tensor"), None),
        ),
        check_vma=False,
    )
```
